32 devices in a mesh: section: 2 (over core), dp: 16 (over z, y, x).
Axes of the slice: x: 2, y: 2, z: 4, core: 2. Of those that a mesh axis runs over, the one named last changes fastest.
Arguments:
- boundary: bfloat16 [2, 16384, 768], P('section', 'dp'), may hold values from -6 to 6
- lengths: int32 [32, 4], P('dp'), may hold values from 32 to 384, as said below
- norm_one_gain: float32 [2, 768], P('section'), may hold values from 0.1 to 1.9
- norm_one_bias: float32 [2, 768], P('section'), may hold values from -3 to 3
- query_weight: bfloat16 [2, 768, 768], P('section'), may hold values from -0.21875 to 0.21875
- query_bias: float32 [2, 768], P('section'), may hold values from -3 to 3
- key_weight: bfloat16 [2, 768, 768], P('section'), may hold values from -0.21875 to 0.21875
- value_weight: bfloat16 [2, 768, 384], P('section'), may hold values from -0.21875 to 0.21875
- value_bias: float32 [2, 384], P('section'), may hold values from -3 to 3
- first_value_weight: bfloat16 [768, 384], replicated, may hold values from -0.21875 to 0.21875
- first_value_bias: float32 [384], replicated, may hold values from -3 to 3
- out_weight: bfloat16 [2, 768, 768], P('section'), may hold values from -0.875 to 0.875
- out_bias: float32 [2, 768], P('section'), may hold values from -3 to 3
- norm_two_gain: float32 [2, 768], P('section'), may hold values from 0.1 to 1.9
- norm_two_bias: float32 [2, 768], P('section'), may hold values from -3 to 3
- up_weight: bfloat16 [2, 768, 3072], P('section'), may hold values from -0.21875 to 0.21875
- up_bias: float32 [2, 3072], P('section'), may hold values from -3 to 3
- down_weight: bfloat16 [2, 3072, 768], P('section'), may hold values from -0.109375 to 0.109375
- down_bias: float32 [2, 768], P('section'), may hold values from -3 to 3
Outputs:
- block_ends: bfloat16 [2, 16384, 768], P('section', 'dp')
- norm_one_gain_grad: float32 [2, 768], P('section')
- norm_one_bias_grad: float32 [2, 768], P('section')
- query_weight_grad: float32 [2, 768, 768], P('section')
- query_bias_grad: float32 [2, 768], P('section')
- key_weight_grad: float32 [2, 768, 768], P('section')
- value_weight_grad: float32 [2, 768, 384], P('section')
- value_bias_grad: float32 [2, 384], P('section')
- first_value_weight_grad: float32 [768, 384], P('section')
- first_value_bias_grad: float32 [384], P('section')
- out_weight_grad: float32 [2, 768, 768], P('section')
- out_bias_grad: float32 [2, 768], P('section')
- norm_two_gain_grad: float32 [2, 768], P('section')
- norm_two_bias_grad: float32 [2, 768], P('section')
- up_weight_grad: float32 [2, 768, 3072], P('section')
- up_bias_grad: float32 [2, 3072], P('section')
- down_weight_grad: float32 [2, 3072, 768], P('section')
- down_bias_grad: float32 [2, 768], P('section')
The draws below stay inside these ranges and needn't reach their ends.
Inputs may be any that keep to these rules, and one draw needn't show every extreme that they name: Row s holds, in order, the lengths of the 4 sequences that fill slot s of 512 tokens; in every row the longest is exactly 384.
All inputs are finite; a program needn't handle non-finite values.
Results may differ from the reference program's by a relative error of at most 0.017.
Values may be sent and summed in bfloat16 or wider, within the bound.
No kernel may reach another device: no remote copies, remote signals or barrier semaphores. Data moves between devices by JAX's collectives and lax.ppermute only.
A program may use at most 256 MiB of HBM per device.

```python
import jax
import jax.numpy as jnp
from jax import lax

HEADS = 12
HEAD = 64
FF = 3072
D = 768
HALF = 384
SLOT = 512
SEQ_SLOT = 4
MOST = 384
LEAST = 32
SLOTS = 32
TOKENS = 16384


def draw_lengths(key, part):
    key = jax.random.fold_in(key, 11)
    spare = SLOT - MOST - (SEQ_SLOT - 1) * LEAST

    def one_row(row_key):
        cut_key, order_key = jax.random.split(row_key)
        cuts = jnp.sort(jax.random.randint(cut_key, (SEQ_SLOT - 2,), 0, spare + 1).astype(jnp.int32))
        edges = jnp.concatenate([jnp.zeros((1,), jnp.int32), cuts, jnp.full((1,), spare, jnp.int32)])
        others = edges[1:] - edges[:-1] + LEAST
        whole_row = jnp.concatenate([jnp.full((1,), MOST, jnp.int32), others.astype(jnp.int32)])
        return jax.random.permutation(order_key, whole_row)
    return jax.vmap(one_row)(jax.random.split(key, SLOTS)).astype(jnp.int32)


def block_levels(stream_key, dims, cuts, smallest, top_value):
    level, own = 1.0, jax.random.fold_in(stream_key, 6)
    for dim, blocks in cuts:
        draws = jnp.exp(jax.random.uniform(jax.random.fold_in(own, dim), (blocks,), jnp.float32, smallest / len(cuts), top_value / len(cuts)))
        level = level * jnp.repeat(draws, dims[dim] // blocks).reshape([-1 if axis == dim else 1 for axis in range(len(dims))])
    return level


def noise(key, shape, deviation, bound, cuts=(), kind=jnp.bfloat16):
    entries = deviation * jax.random.normal(key, shape, jnp.float32)
    if cuts:
        entries = entries * block_levels(key, shape, cuts, -0.22, 0.18)
    return jnp.clip(entries, -bound, bound).astype(kind)


def setup_inputs(seed: int = 0) -> dict:
    key_of = jax.random.split(jax.random.key(seed), 20)
    return {
        "boundary": noise(key_of[0], (2, TOKENS, D), 1.0, 6.0, ((0, 2), (1, 16))),
        "lengths": draw_lengths(jax.random.fold_in(key_of[19], 71), 0),
        "norm_one_gain": jnp.clip(1.0 + 0.18 * jax.random.normal(key_of[2], (2, D), jnp.float32), 0.1, 1.9),
        "norm_one_bias": noise(key_of[3], (2, D), 0.5, 3.0, ((0, 2),), jnp.float32),
        "query_weight": noise(key_of[4], (2, D, D), D ** -0.5, 0.21875, ((0, 2),)),
        "query_bias": noise(key_of[5], (2, D), 0.5, 3.0, ((0, 2),), jnp.float32),
        "key_weight": noise(key_of[6], (2, D, D), D ** -0.5, 0.21875, ((0, 2),)),
        "value_weight": noise(key_of[7], (2, D, HALF), D ** -0.5, 0.21875, ((0, 2),)),
        "value_bias": noise(key_of[8], (2, HALF), 0.5, 3.0, ((0, 2),), jnp.float32),
        "first_value_weight": noise(key_of[9], (D, HALF), D ** -0.5, 0.21875),
        "first_value_bias": noise(key_of[10], (HALF,), 0.5, 3.0, (), jnp.float32),
        "out_weight": noise(key_of[11], (2, D, D), (D // 16) ** -0.5, 0.875, ((0, 2),)),
        "out_bias": noise(key_of[12], (2, D), 0.5, 3.0, ((0, 2),), jnp.float32),
        "norm_two_gain": jnp.clip(1.0 + 0.18 * jax.random.normal(key_of[13], (2, D), jnp.float32), 0.1, 1.9),
        "norm_two_bias": noise(key_of[14], (2, D), 0.5, 3.0, ((0, 2),), jnp.float32),
        "up_weight": noise(key_of[15], (2, D, FF), D ** -0.5, 0.21875, ((0, 2),)),
        "up_bias": noise(key_of[16], (2, FF), 0.5, 3.0, ((0, 2),), jnp.float32),
        "down_weight": noise(key_of[17], (2, FF, D), FF ** -0.5, 0.109375, ((0, 2),)),
        "down_bias": noise(key_of[18], (2, D), 0.5, 3.0, ((0, 2),), jnp.float32),
    }


@jax.custom_vjp
def low(v):
    return lax.optimization_barrier(v.astype(jnp.bfloat16)).astype(jnp.float32)

@jax.custom_vjp
def low_back(v):
    return v

def low_keep(v):
    return (low(v), None)

def low_pass(kept, grad):
    return (grad,)

def back_keep(v):
    return (v, None)

def back_low(kept, grad):
    return (low(grad),)
low.defvjp(low_keep, low_pass)
low_back.defvjp(back_keep, back_low)
eps_norm = 1e-05
neg_fill = -1e+30

def matmul(left, right):
    return jnp.dot(left, right, precision=lax.Precision.HIGHEST, preferred_element_type=jnp.float32)

def normed(rows_in, gain, bias):
    centre = lax.optimization_barrier(jnp.mean(rows_in, axis=-1, keepdims=True))
    centred = rows_in - centre
    spread = lax.optimization_barrier(jnp.mean(centred * centred, axis=-1, keepdims=True))
    return centred * lax.rsqrt(spread + eps_norm) * gain + bias

def attend(packed):
    queries, key_rows, values, lengths_row = packed
    row_count = queries.shape[0]
    cut_points = jnp.cumsum(lengths_row)
    positions = jnp.arange(row_count, dtype=jnp.int32)
    segments = lax.optimization_barrier(jnp.sum((positions[:, None] >= cut_points[None, :]).astype(jnp.int32), axis=1))
    allowed = (segments[:, None] == segments[None, :]) & (positions[None, :] <= positions[:, None])
    scores = jnp.einsum('qhd,khd->hqk', queries, key_rows, precision=lax.Precision.HIGHEST) * HEAD ** (-0.5)
    scores = jnp.where(allowed[None], low_back(scores), neg_fill)
    row_peak = lax.optimization_barrier(jnp.max(scores, axis=-1, keepdims=True))
    exponent = jnp.exp(scores - row_peak)
    weights_low = low(exponent / lax.optimization_barrier(jnp.sum(exponent, axis=-1, keepdims=True)))
    return jnp.einsum('hqk,khd->qhd', weights_low, values, precision=lax.Precision.HIGHEST)

def attention_all(queries, key_rows, values, lengths):
    shaped = (SLOTS, SLOT, HEADS, HEAD)
    mixed = lax.map(jax.checkpoint(attend), (queries.reshape(shaped), key_rows.reshape(shaped), values.reshape(shaped), lengths))
    return mixed.reshape(TOKENS, HEADS * HEAD)

def run_layer(rows_in, layer_side, reused, params, lengths):
    hidden = low(normed(rows_in, params[0][layer_side], params[1][layer_side]))
    queries = low(low_back(matmul(hidden, params[2][layer_side]) + params[3][layer_side]))
    key_rows = low(low_back(matmul(hidden, params[4][layer_side])))
    fresh_values = low(low_back(matmul(hidden, params[5][layer_side]) + params[6][layer_side]))
    if layer_side == 0:
        shared = low(low_back(matmul(hidden, params[7]) + params[8]))
    else:
        shared = reused
    values = jnp.concatenate([shared, fresh_values], axis=1)
    attended = low(low_back(attention_all(queries, key_rows, values, lengths)))
    middle = rows_in + low_back(matmul(attended, params[9][layer_side]) + params[10][layer_side])
    second = low(normed(middle, params[11][layer_side], params[12][layer_side]))
    pre_active = low_back(matmul(second, params[13][layer_side]) + params[14][layer_side])
    active = low(jax.nn.gelu(pre_active, approximate=True))
    return (middle + low_back(matmul(active, params[15][layer_side]) + params[16][layer_side]), shared)

def reference(boundary, lengths, norm_one_gain, norm_one_bias, query_weight, query_bias, key_weight, value_weight, value_bias, first_value_weight, first_value_bias, out_weight, out_bias, norm_two_gain, norm_two_bias, up_weight, up_bias, down_weight, down_bias):
    params = tuple((item.astype(jnp.float32) for item in (norm_one_gain, norm_one_bias, query_weight, query_bias, key_weight, value_weight, value_bias, first_value_weight, first_value_bias, out_weight, out_bias, norm_two_gain, norm_two_bias, up_weight, up_bias, down_weight, down_bias)))
    block_input = boundary[0].astype(jnp.float32)
    cotangent = boundary[1].astype(jnp.float32)

    def forward(rows_in, *layer_params):
        first_out, shared = run_layer(rows_in, 0, None, layer_params, lengths)
        passed = low(low_back(first_out))
        final_out, unused = run_layer(passed, 1, shared, layer_params, lengths)
        return final_out
    block_output, pull_back = jax.vjp(forward, block_input, *params)
    grads = pull_back(cotangent)
    block_ends = jnp.stack([grads[0].astype(jnp.bfloat16), block_output.astype(jnp.bfloat16)])
    return (block_ends, grads[1], grads[2], grads[3], grads[4], grads[5], grads[6], grads[7], grads[8], grads[9], grads[10], grads[11], grads[12], grads[13], grads[14], grads[15], grads[16], grads[17])
```

```python
import functools

import jax
import jax.numpy as jnp
from jax import lax
from jax.experimental import pallas as pl
from jax.experimental.pallas import tpu as pltpu
from jax.sharding import PartitionSpec as P

HEADS = 12
HEAD = 64
PAIR = 2 * HEAD
VMEM_BYTES = 48 * 1024 * 1024

eps_norm = 1e-05
neg_fill = -1e30

f32 = jnp.float32
bf16 = jnp.bfloat16

NN = (((1,), (0,)), ((), ()))
NT = (((1,), (1,)), ((), ()))
TN = (((0,), (0,)), ((), ()))

ANY = pl.BlockSpec(memory_space=pl.ANY)
SMEM = pl.BlockSpec(memory_space=pltpu.SMEM)
VMEM = pl.BlockSpec(memory_space=pltpu.VMEM)

GAIN1, BIAS1, QBIAS, VBIAS, OBIAS, GAIN2, BIAS2, DBIAS, UBIAS = range(9)
VEC_ROWS = 16


def mm(left, right, dims=NN):
    return lax.dot_general(left, right, dims, preferred_element_type=f32)


def sds(shape, dtype):
    return jax.ShapeDtypeStruct(shape, dtype)


def params():
    return pltpu.CompilerParams(vmem_limit_bytes=VMEM_BYTES)


def cost(flops, nbytes, trans=0):
    return pl.CostEstimate(flops=int(flops), bytes_accessed=int(nbytes), transcendentals=int(trans))


def start_fetch(mine, own, recv, dst, sem):
    @pl.when(mine)
    def _():
        pltpu.make_async_copy(own, dst, sem).start()

    @pl.when(jnp.logical_not(mine))
    def _():
        pltpu.make_async_copy(recv, dst, sem).start()


def wait_fetch(own, dst, sem):
    pltpu.make_async_copy(own, dst, sem).wait()


def norm_parts(rows):
    centre = jnp.mean(rows, axis=-1, keepdims=True)
    centred = rows - centre
    spread = jnp.mean(centred * centred, axis=-1, keepdims=True)
    factor = lax.rsqrt(spread + eps_norm)
    return centred * factor, factor


def norm_back(grad_t, n, w):
    return w * (
        grad_t
        - jnp.mean(grad_t, axis=-1, keepdims=True)
        - n * jnp.mean(grad_t * n, axis=-1, keepdims=True)
    )


def row_sum(x):
    return jnp.sum(x, axis=0, keepdims=True)


def attn_forward_kernel(layer, sec_ref, x_ref, r_ref, start_ref, vec_ref,
                        qw_o, qw_r, kw_o, kw_r, vw_o, vw_r, fw, ow_o, ow_r,
                        h_out, q_out, k_out, v_out, o_out, m_out, e_out, lse_out,
                        wq, wk, wv, wo, h_s, q_s, k_s, v_s, o_s, m_s, e_s, lse_s, lset_s, bias_s,
                        in_sem, out_sem):
    mine = sec_ref[0] == layer
    rows = x_ref.shape[0]
    half = fw.shape[1]
    start_fetch(mine, qw_o, qw_r, wq, in_sem.at[0])
    start_fetch(mine, kw_o, kw_r, wk, in_sem.at[1])
    start_fetch(mine, vw_o, vw_r, wv.at[:, half:], in_sem.at[2])
    if layer == 0:
        pltpu.make_async_copy(fw, wv.at[:, :half], in_sem.at[3]).start()
    start_fetch(mine, ow_o, ow_r, wo, in_sem.at[4])

    def put(index, src, dst):
        pltpu.make_async_copy(src, dst, out_sem.at[index]).start()

    wide = x_ref[...].astype(f32)
    n, _ = norm_parts(wide)
    h_s[...] = (n * vec_ref[GAIN1:GAIN1 + 1, :] + vec_ref[BIAS1:BIAS1 + 1, :]).astype(bf16)
    put(0, h_s, h_out)
    at_row = lax.broadcasted_iota(jnp.int32, (rows, rows), 0)
    at_col = lax.broadcasted_iota(jnp.int32, (rows, rows), 1)
    bias_s[...] = jnp.where((at_col <= at_row) & (at_col >= start_ref[...]), 0.0, neg_fill)
    wait_fetch(qw_o, wq, in_sem.at[0])
    q_s[...] = (mm(h_s[...], wq[...]) + vec_ref[QBIAS:QBIAS + 1, :]).astype(bf16)
    put(1, q_s, q_out)
    wait_fetch(kw_o, wk, in_sem.at[1])
    k_s[...] = mm(h_s[...], wk[...]).astype(bf16)
    put(2, k_s, k_out)
    wait_fetch(vw_o, wv.at[:, half:], in_sem.at[2])
    if layer == 0:
        wait_fetch(fw, wv.at[:, :half], in_sem.at[3])
        v_s[...] = (mm(h_s[...], wv[...]) + vec_ref[VBIAS:VBIAS + 1, :]).astype(bf16)
    else:
        v_s[:, :half] = r_ref[:, :half]
        v_s[:, half:] = (mm(h_s[...], wv[:, half:]) + vec_ref[VBIAS:VBIAS + 1, half:]).astype(bf16)
    put(3, v_s, v_out)

    lane = lax.broadcasted_iota(jnp.int32, (1, PAIR), 1)
    step = rows // 2

    def pair(hp, carry):
        ls = pl.ds(pl.multiple_of(hp * PAIR, PAIR), PAIR)
        q2 = q_s[:, ls] * jnp.asarray(HEAD ** -0.5, bf16)
        k2 = k_s[:, ls]
        v2 = v_s[:, ls]
        zero = jnp.zeros((), bf16)
        for qb in range(2):
            qr = slice(qb * step, (qb + 1) * step)
            keys = (qb + 1) * step
            mixed = None
            for j in range(2):
                inside = (lane >= j * HEAD) & (lane < (j + 1) * HEAD)
                kh = jnp.where(inside, k2[:keys], zero)
                vh = jnp.where(inside, v2[:keys], zero)
                s = mm(q2[qr], kh, NT) + bias_s[qr, :keys]
                peak = jnp.max(s, axis=-1, keepdims=True)
                p = jnp.exp(s - peak)
                total = jnp.sum(p, axis=-1, keepdims=True)
                low = (p * (1.0 / total)).astype(bf16)
                part = mm(low, vh)
                mixed = part if mixed is None else mixed + part
                lse_s[qr, :] = jnp.where(lane == 2 * hp + j, peak + jnp.log(total), lse_s[qr, :])
            o_s[qr, ls] = mixed.astype(bf16)
        return carry

    lse_s[...] = jnp.zeros(lse_s.shape, f32)
    lax.fori_loop(0, HEADS // 2, pair, 0)
    put(4, o_s, o_out)
    lset_s[...] = jnp.transpose(lse_s[...])[:VEC_ROWS, :]
    put(7, lset_s, lse_out)
    wait_fetch(ow_o, wo, in_sem.at[4])
    m = x_ref[...].astype(f32) + (mm(o_s[...], wo[...]) + vec_ref[OBIAS:OBIAS + 1, :])
    m_s[...] = m
    put(5, m_s, m_out)
    n, _ = norm_parts(m)
    e_s[...] = (n * vec_ref[GAIN2:GAIN2 + 1, :] + vec_ref[BIAS2:BIAS2 + 1, :]).astype(bf16)
    put(6, e_s, e_out)
    for index, (src, dst) in enumerate(((h_s, h_out), (q_s, q_out), (k_s, k_out), (v_s, v_out),
                                        (o_s, o_out), (m_s, m_out), (e_s, e_out), (lset_s, lse_out))):
        pltpu.make_async_copy(src, dst, out_sem.at[index]).wait()


def attn_forward(layer, sec, x, r, start, vec, w):
    rows, d = x.shape
    act = sds((rows, d), bf16)
    wbuf = pltpu.VMEM((d, d), bf16)
    abuf = pltpu.VMEM((rows, d), bf16)
    return pl.pallas_call(
        functools.partial(attn_forward_kernel, layer),
        out_shape=[act, act, act, act, act, sds((rows, d), f32), act, sds((VEC_ROWS, rows), f32)],
        in_specs=[SMEM, VMEM, VMEM, VMEM, VMEM] + [ANY] * 9,
        out_specs=[ANY] * 8,
        scratch_shapes=[wbuf, wbuf, wbuf, wbuf, abuf, abuf, abuf, abuf, abuf,
                        pltpu.VMEM((rows, d), f32), abuf, pltpu.VMEM((rows, PAIR), f32),
                        pltpu.VMEM((VEC_ROWS, rows), f32), pltpu.VMEM((rows, rows), f32),
                        pltpu.SemaphoreType.DMA((5,)), pltpu.SemaphoreType.DMA((8,))],
        compiler_params=params(),
        cost_estimate=cost(10 * rows * d * d, 12 * rows * d * 2, HEADS * rows * rows),
        name="attn_forward",
    )(sec, x, r, start, vec, w["qo"], w["qr"], w["ko"], w["kr"], w["vo"], w["vr"], w["f"], w["oo"], w["or"])


def feed_forward_kernel(layer, blk, sec_ref, e_ref, m_ref, vec_ref, up_o, up_r, dn_o, dn_r,
                        u_ref, a_ref, z_ref, wu, wd, acc, sem):
    j = pl.program_id(0)
    steps = pl.num_programs(0)
    mine = sec_ref[0] == layer

    @pl.when(j == 0)
    def _():
        for b in range(up_o.shape[1] // blk):
            cols = pl.ds(b * blk, blk)
            start_fetch(mine, up_o.at[:, cols], up_r.at[:, cols], wu.at[b], sem.at[0, b])
            start_fetch(mine, dn_o.at[cols, :], dn_r.at[cols, :], wd.at[b], sem.at[1, b])

    wait_fetch(up_o.at[:, pl.ds(0, blk)], wu.at[j], sem.at[0, j])
    u = mm(e_ref[...], wu[j]) + vec_ref[pl.ds(UBIAS + j, 1), :]
    u_ref[...] = u.astype(bf16)
    half_u = 0.5 * u
    th = jnp.tanh(u * (0.7978845608028654 + 0.035677408136300125 * (u * u)))
    a = (half_u + half_u * th).astype(bf16)
    a_ref[...] = a
    wait_fetch(dn_o.at[pl.ds(0, blk), :], wd.at[j], sem.at[1, j])
    part = mm(a, wd[j])

    @pl.when(j == 0)
    def _():
        acc[...] = part

    @pl.when((j > 0) & (j < steps - 1))
    def _():
        acc[...] += part

    @pl.when(j == steps - 1)
    def _():
        z_ref[...] = (m_ref[...] + (acc[...] + part + vec_ref[DBIAS:DBIAS + 1, :])).astype(bf16)


def feed_forward(layer, sec, e, m, vec, w):
    rows, d = e.shape
    ff = w["uo"].shape[1]
    blk = d
    n = ff // blk
    return pl.pallas_call(
        functools.partial(feed_forward_kernel, layer, blk),
        grid=(n,),
        out_shape=[sds((rows, ff), bf16), sds((rows, ff), bf16), sds((rows, d), bf16)],
        in_specs=[SMEM, VMEM, VMEM, VMEM, ANY, ANY, ANY, ANY],
        out_specs=[pl.BlockSpec((rows, blk), lambda j: (0, j)), pl.BlockSpec((rows, blk), lambda j: (0, j)),
                   pl.BlockSpec((rows, d), lambda j: (0, 0))],
        scratch_shapes=[pltpu.VMEM((n, d, blk), bf16), pltpu.VMEM((n, blk, d), bf16), pltpu.VMEM((rows, d), f32),
                        pltpu.SemaphoreType.DMA((2, n))],
        compiler_params=params(),
        cost_estimate=cost(4 * rows * d * ff, 4 * d * ff + 4 * rows * ff, rows * ff),
        name="feed_forward",
    )(sec, e, m, vec, w["uo"], w["ur"], w["do"], w["dr"])


def feed_backward_kernel(layer, blk, sec_ref, dz_ref, u_ref, m_ref, vec_ref, up_o, up_r, dn_o, dn_r,
                         du_ref, dm_ref, low_ref, small_ref, wu, wd, acc, sem):
    j = pl.program_id(0)
    steps = pl.num_programs(0)
    mine = sec_ref[0] == layer

    @pl.when(j == 0)
    def _():
        for b in range(up_o.shape[1] // blk):
            cols = pl.ds(b * blk, blk)
            start_fetch(mine, dn_o.at[cols, :], dn_r.at[cols, :], wd.at[b], sem.at[1, b])
            start_fetch(mine, up_o.at[:, cols], up_r.at[:, cols], wu.at[b], sem.at[0, b])
        acc[...] = jnp.zeros(acc.shape, f32)
        small_ref[...] = jnp.zeros(small_ref.shape, f32)

    wait_fetch(dn_o.at[pl.ds(0, blk), :], wd.at[j], sem.at[1, j])
    da = mm(dz_ref[...], wd[j], NT)
    u = u_ref[...].astype(f32)
    sq = u * u
    th = jnp.tanh(u * (0.7978845608028654 + 0.035677408136300125 * sq))
    slope = 0.5 + 0.5 * th + (0.5 * u) * (1.0 - th * th) * (0.7978845608028654 + 0.10703222440890037 * sq)
    du = (slope * da).astype(bf16)
    du_ref[...] = du
    small_ref[pl.ds(UBIAS + j, 1), :] = row_sum(du.astype(f32))
    wait_fetch(up_o.at[:, pl.ds(0, blk)], wu.at[j], sem.at[0, j])
    acc[...] += mm(du, wu[j], NT)

    @pl.when(j == steps - 1)
    def _():
        de = acc[...]
        n, w = norm_parts(m_ref[...])
        dz = dz_ref[...].astype(f32)
        dm = dz + norm_back(de * vec_ref[GAIN2:GAIN2 + 1, :], n, w)
        dm_ref[...] = dm
        low_ref[...] = dm.astype(bf16)
        small_ref[GAIN2:GAIN2 + 1, :] = row_sum(de * n)
        small_ref[BIAS2:BIAS2 + 1, :] = row_sum(de)
        small_ref[DBIAS:DBIAS + 1, :] = row_sum(dz)


def feed_backward(layer, sec, dz, u, m, vec, w):
    rows, d = dz.shape
    ff = u.shape[1]
    blk = d
    n = ff // blk
    whole = lambda j: (0, 0)
    return pl.pallas_call(
        functools.partial(feed_backward_kernel, layer, blk),
        grid=(n,),
        out_shape=[sds((rows, ff), bf16), sds((rows, d), f32), sds((rows, d), bf16), sds((VEC_ROWS, d), f32)],
        in_specs=[SMEM, VMEM, pl.BlockSpec((rows, blk), lambda j: (0, j)), VMEM, VMEM, ANY, ANY, ANY, ANY],
        out_specs=[pl.BlockSpec((rows, blk), lambda j: (0, j)), pl.BlockSpec((rows, d), whole),
                   pl.BlockSpec((rows, d), whole), pl.BlockSpec((VEC_ROWS, d), whole)],
        scratch_shapes=[pltpu.VMEM((n, d, blk), bf16), pltpu.VMEM((n, blk, d), bf16), pltpu.VMEM((rows, d), f32),
                        pltpu.SemaphoreType.DMA((2, n))],
        compiler_params=params(),
        cost_estimate=cost(4 * rows * d * ff, 4 * d * ff + 4 * rows * ff, rows * ff),
        name="feed_backward",
    )(sec, dz, u, m, vec, w["uo"], w["ur"], w["do"], w["dr"])


def attn_backward_kernel(layer, sec_ref, x_ref, dm_ref, low_ref, q_ref, k_ref, v_ref, o_ref, lse_ref,
                         start_ref, vec_ref, dr2_ref,
                         qw_o, qw_r, kw_o, kw_r, vw_o, vw_r, fw, ow_o, ow_r,
                         dx_ref, dq_ref, dk_ref, dv_ref, shared_ref, small_ref,
                         wq, wk, wv, wo, do_s, delta_s, bias_s, sem):
    mine = sec_ref[0] == layer
    rows, d = x_ref.shape
    half = fw.shape[1]
    start_fetch(mine, ow_o, ow_r, wo, sem.at[4])
    start_fetch(mine, qw_o, qw_r, wq, sem.at[0])
    start_fetch(mine, kw_o, kw_r, wk, sem.at[1])
    start_fetch(mine, vw_o, vw_r, wv.at[:, half:], sem.at[2])
    if layer == 0:
        pltpu.make_async_copy(fw, wv.at[:, :half], sem.at[3]).start()

    at_key = lax.broadcasted_iota(jnp.int32, (rows, rows), 0)
    at_query = lax.broadcasted_iota(jnp.int32, (rows, rows), 1)
    bias_s[...] = jnp.where((at_key <= at_query) & (at_key >= start_ref[...]), 0.0, neg_fill)
    wait_fetch(ow_o, wo, sem.at[4])
    do = mm(low_ref[...], wo[...], NT).astype(bf16)
    do_s[...] = do
    head_row = lax.broadcasted_iota(jnp.int32, (VEC_ROWS, d), 0)
    head_col = lax.broadcasted_iota(jnp.int32, (VEC_ROWS, d), 1) // HEAD
    pick = (head_row == head_col).astype(f32)
    delta_s[...] = lax.dot_general(pick, do.astype(f32) * o_ref[...].astype(f32), NT,
                                   precision=lax.Precision.HIGHEST, preferred_element_type=f32)
    lane = lax.broadcasted_iota(jnp.int32, (1, PAIR), 1)
    step = rows // 2
    scale = HEAD ** -0.5
    zero = jnp.zeros((), bf16)

    def pair(hp, carry):
        ls = pl.ds(pl.multiple_of(hp * PAIR, PAIR), PAIR)
        q2 = q_ref[:, ls] * jnp.asarray(scale, bf16)
        k2 = k_ref[:, ls]
        v2 = v_ref[:, ls]
        do2 = do_s[:, ls]
        dq_parts = []
        for kb in range(2):
            kr = slice(kb * step, (kb + 1) * step)
            first = kb * step
            dk = dv = dq = None
            for j in range(2):
                inside = (lane >= j * HEAD) & (lane < (j + 1) * HEAD)
                kh = jnp.where(inside, k2[kr], zero)
                vh = jnp.where(inside, v2[kr], zero)
                qh = jnp.where(inside, q2[first:], zero)
                doh = jnp.where(inside, do2[first:], zero)
                row = pl.ds(2 * hp + j, 1)
                st = mm(kh, qh, NT) + bias_s[kr, first:]
                pt = jnp.exp(st - lse_ref[row, first:])
                dpt = mm(vh, doh, NT)
                dst = (pt * (dpt - delta_s[row, first:])).astype(bf16)
                dv_j = mm(pt.astype(bf16), doh)
                dk_j = mm(dst, qh)
                dq_j = mm(dst, kh, TN)
                dk = dk_j if dk is None else dk + dk_j
                dv = dv_j if dv is None else dv + dv_j
                dq = dq_j if dq is None else dq + dq_j
            dk_ref[kr, ls] = dk.astype(bf16)
            if layer == 1:
                dv_ref[kr, ls] = dv.astype(bf16)

                @pl.when(hp < HEADS // 4)
                def _():
                    shared_ref[kr, ls] = dv
            else:
                extra = jnp.where(hp < HEADS // 4, dr2_ref[kr, pl.ds(pl.multiple_of((hp % (HEADS // 4)) * PAIR, PAIR), PAIR)], 0.0)
                dv_ref[kr, ls] = (dv + extra).astype(bf16)
            dq_parts.append(dq)
        dq_ref[:step, ls] = (dq_parts[0][:step] * scale).astype(bf16)
        dq_ref[step:, ls] = ((dq_parts[0][step:] + dq_parts[1]) * scale).astype(bf16)
        return carry

    if layer == 0:
        shared_ref[...] = jnp.zeros(shared_ref.shape, f32)
    lax.fori_loop(0, HEADS // 2, pair, 0)

    wait_fetch(qw_o, wq, sem.at[0])
    dh = mm(dq_ref[...], wq[...], NT)
    wait_fetch(kw_o, wk, sem.at[1])
    dh = dh + mm(dk_ref[...], wk[...], NT)
    wait_fetch(vw_o, wv.at[:, half:], sem.at[2])
    if layer == 0:
        wait_fetch(fw, wv.at[:, :half], sem.at[3])
        dh = dh + mm(dv_ref[...], wv[...], NT)
    else:
        dh = dh + mm(dv_ref[:, half:], wv[:, half:], NT)
    n, w = norm_parts(x_ref[...].astype(f32))
    dx_ref[...] = (dm_ref[...] + norm_back(dh * vec_ref[GAIN1:GAIN1 + 1, :], n, w)).astype(bf16)
    small_ref[...] = jnp.zeros(small_ref.shape, f32)
    small_ref[GAIN1:GAIN1 + 1, :] = row_sum(dh * n)
    small_ref[BIAS1:BIAS1 + 1, :] = row_sum(dh)
    small_ref[QBIAS:QBIAS + 1, :] = row_sum(dq_ref[...].astype(f32))
    small_ref[VBIAS:VBIAS + 1, :] = row_sum(dv_ref[...].astype(f32))
    small_ref[OBIAS:OBIAS + 1, :] = row_sum(low_ref[...].astype(f32))


def attn_backward(layer, sec, x, dm, low, q, k, v, o, lse, start_row, vec, dr2, w):
    rows, d = x.shape
    half = w["f"].shape[1]
    act = sds((rows, d), bf16)
    wbuf = pltpu.VMEM((d, d), bf16)
    return pl.pallas_call(
        functools.partial(attn_backward_kernel, layer),
        out_shape=[act, act, act, act, sds((rows, half), f32), sds((VEC_ROWS, d), f32)],
        in_specs=[SMEM] + [VMEM] * 11 + [ANY] * 9,
        out_specs=[VMEM] * 6,
        scratch_shapes=[wbuf, wbuf, wbuf, wbuf, pltpu.VMEM((rows, d), bf16), pltpu.VMEM((VEC_ROWS, rows), f32),
                        pltpu.VMEM((rows, rows), f32), pltpu.SemaphoreType.DMA((5,))],
        compiler_params=params(),
        cost_estimate=cost(16 * rows * d * d, 16 * rows * d * 2, HEADS * rows * rows),
        name="attn_backward",
    )(sec, x, dm, low, q, k, v, o, lse, start_row, vec, dr2,
      w["qo"], w["qr"], w["ko"], w["kr"], w["vo"], w["vr"], w["f"], w["oo"], w["or"])


def store_chunks(ref, value):
    c, r, _ = ref.shape
    for i in range(c):
        ref[i] = value[i * r:(i + 1) * r].astype(bf16)


def two_way(body, grid, in_specs, steps, chunk_rows, block_rows, width, scalars, operands, flops, nbytes, name):
    per = block_rows // chunk_rows
    total = steps * per

    def kernel(s_ref, *refs):
        g = pl.program_id(0)
        *ins, send_ref, keep_ref = refs
        value = body(g % steps, *ins)

        @pl.when(g < steps)
        def _():
            store_chunks(send_ref, value)

        @pl.when(g >= steps)
        def _():
            store_chunks(keep_ref, value)

    return pl.pallas_call(
        kernel,
        grid_spec=pltpu.PrefetchScalarGridSpec(
            num_scalar_prefetch=1, grid=(2 * steps,), in_specs=in_specs,
            out_specs=[pl.BlockSpec((per, chunk_rows, width), lambda g, s: (jnp.minimum(g, steps - 1), 0, 0)),
                       pl.BlockSpec((per, chunk_rows, width), lambda g, s: (jnp.maximum(g - steps, 0), 0, 0))]),
        out_shape=[sds((total, chunk_rows, width), bf16)] * 2,
        compiler_params=params(),
        cost_estimate=cost(flops, nbytes),
        name=name,
    )(scalars, *operands)


def part_of(g, steps, s):
    return jnp.where(g < steps, 1 - s[0], s[0])


def down_gradient(sec, a, dz, chunk_rows):
    rows, ff = a.shape
    d = dz.shape[1]
    steps = ff // d // 2

    def body(i, a_ref, dz_ref):
        return mm(a_ref[...], dz_ref[...], TN)

    return two_way(body, None,
                   [pl.BlockSpec((rows, d), lambda g, s: (0, part_of(g, steps, s) * steps + g % steps)),
                    pl.BlockSpec((rows, d), lambda g, s: (0, 0))],
                   steps, chunk_rows, d, d, sec, (a, dz), 2 * rows * ff * d, 2 * rows * ff + 2 * d * ff, "down_gradient")


def up_gradient(sec, e, du, chunk_rows):
    rows, ff = du.shape
    d = e.shape[1]
    steps = ff // d // 2

    def body(i, e_ref, du_ref):
        return mm(e_ref[...], du_ref[...], TN)

    return two_way(body, None,
                   [pl.BlockSpec((rows, d), lambda g, s: (0, 0)),
                    pl.BlockSpec((rows, d), lambda g, s: (0, part_of(g, steps, s) * steps + g % steps))],
                   steps, chunk_rows, d, d, sec, (e, du), 2 * rows * ff * d, 2 * rows * ff + 2 * d * ff, "up_gradient")


def attn_gradient(sec, o, low, h, dq, dk, dv, chunk_rows):
    rows, d = o.shape
    steps = 4

    def kernel(s_ref, o_ref, low_ref, h_ref, dq_ref, dk_ref, dv_ref, send_ref, keep_ref):
        g = pl.program_id(0)
        for i, (left, right) in enumerate(((o_ref, low_ref), (h_ref, dq_ref), (h_ref, dk_ref), (h_ref, dv_ref))):
            for side, ref in enumerate((send_ref, keep_ref)):
                @pl.when(g == side * steps + i)
                def _():
                    store_chunks(ref, mm(left[...], right[...], TN))

    half = pl.BlockSpec((rows, d // 2), lambda g, s: (0, part_of(g, steps, s)))
    full = pl.BlockSpec((rows, d), lambda g, s: (0, 0))
    per = d // 2 // chunk_rows
    return pl.pallas_call(
        kernel,
        grid_spec=pltpu.PrefetchScalarGridSpec(
            num_scalar_prefetch=1, grid=(2 * steps,), in_specs=[half, full, half, full, full, full],
            out_specs=[pl.BlockSpec((per, chunk_rows, d), lambda g, s: (jnp.minimum(g, steps - 1), 0, 0)),
                       pl.BlockSpec((per, chunk_rows, d), lambda g, s: (jnp.maximum(g - steps, 0), 0, 0))]),
        out_shape=[sds((steps * per, chunk_rows, d), bf16)] * 2,
        compiler_params=params(),
        cost_estimate=cost(8 * rows * d * d, 8 * d * d + 12 * rows * d),
        name="attn_gradient",
    )(sec, o, low, h, dq, dk, dv)


AXES = ("section", "dp")
SWAP = [(0, 1), (1, 0)]


def bit_orders(dp):
    bits = list(range(dp.bit_length() - 1))
    if len(bits) < 3:
        return bits, bits[::-1]
    return [0, 2, 1] + bits[3:], [1, 2, 0] + bits[3:]


def exchange(array, dp, step):
    first, second = bit_orders(dp)
    pairs = [(i, i ^ (1 << first[step])) for i in range(dp)]
    pairs += [(dp + i, dp + (i ^ (1 << second[step]))) for i in range(dp)]
    return lax.ppermute(array, AXES, pairs)


def block_of(chunks, rows):
    best = 1
    for c in range(1, chunks + 1):
        if chunks % c == 0 and c * rows <= 768:
            best = c
    return best


def add_split(bit, parts):
    _, c, r, w = parts[0][0].shape
    counts = [p[0].shape[0] for p in parts]
    n = sum(counts)
    h = c // 2
    cb = block_of(h, r)
    nb = h // cb
    ends = [sum(counts[:i + 1]) for i in range(len(counts))]
    begins = [e - k for e, k in zip(ends, counts)]

    def kernel(s_ref, *refs):
        send_ref, keep_ref = refs[-2:]
        g, i = pl.program_id(0), pl.program_id(1)
        for t in range(len(parts)):
            @pl.when((i >= begins[t]) & (i < ends[t]))
            def _():
                total = (refs[2 * t][...].astype(f32) + refs[2 * t + 1][...].astype(f32)).astype(bf16)

                @pl.when(g == 0)
                def _():
                    send_ref[...] = total

                @pl.when(g == 1)
                def _():
                    keep_ref[...] = total

    def source(t):
        def index(g, i, j, s):
            inside = (i >= begins[t]) & (i < ends[t])
            side = jnp.where(g == 0, 1 - s[0], s[0])
            return (jnp.clip(i - begins[t], 0, counts[t] - 1), jnp.where(inside, side * nb + j, 0), 0, 0)
        return pl.BlockSpec((1, cb, r, w), index)

    def send_at(g, i, j, s):
        return (jnp.where(g == 0, i, n - 1), jnp.where(g == 0, j, nb - 1), 0, 0)

    def keep_at(g, i, j, s):
        return (jnp.where(g == 0, 0, i), jnp.where(g == 0, 0, j), 0, 0)

    flat = [x for p in parts for x in p]
    return pl.pallas_call(
        kernel,
        grid_spec=pltpu.PrefetchScalarGridSpec(
            num_scalar_prefetch=1, grid=(2, n, nb),
            in_specs=[source(t) for t in range(len(parts)) for _ in range(2)],
            out_specs=[pl.BlockSpec((1, cb, r, w), send_at), pl.BlockSpec((1, cb, r, w), keep_at)]),
        out_shape=[sds((n, h, r, w), bf16)] * 2,
        compiler_params=params(),
        cost_estimate=cost(n * c * r * w, 6 * n * c * r * w),
        name="add_split",
    )(bit, *flat)


def merge(bit, cur, arrived):
    n, c, r, w = cur.shape
    cb = block_of(c, r)
    nb = c // cb

    def kernel(s_ref, a_ref, b_ref, out_ref):
        g = pl.program_id(1)

        @pl.when(g == s_ref[0])
        def _():
            out_ref[...] = a_ref[...]

        @pl.when(g != s_ref[0])
        def _():
            out_ref[...] = b_ref[...]

    def at(own):
        def index(i, g, j, s):
            mine = (g == s[0]) if own else (g != s[0])
            return (i, jnp.where(mine, j, 0), 0, 0)
        return pl.BlockSpec((1, cb, r, w), index)

    return pl.pallas_call(
        kernel,
        grid_spec=pltpu.PrefetchScalarGridSpec(
            num_scalar_prefetch=1, grid=(n, 2, nb), in_specs=[at(True), at(False)],
            out_specs=pl.BlockSpec((1, cb, r, w), lambda i, g, j, s: (i, g * nb + j, 0, 0))),
        out_shape=sds((n, 2 * c, r, w), bf16),
        compiler_params=params(),
        cost_estimate=cost(0, 8 * n * c * r * w),
        name="merge",
    )(bit, cur, arrived)


def assemble(scalars, sources, outs, place, name):
    c, r, w = sources[0][0][0].shape[1:]
    block = w // 2
    cb = block // r
    nb = c // cb
    flat = [item for layer in sources for item in layer]

    def chosen(g, s):
        part = g // 2
        bit = jnp.where(part == 0, s[1], s[2])
        return 4 * s[0] + jnp.where(part == s[0], 0, 2) + jnp.where(g % 2 == bit, 0, 1)

    def kernel(s_ref, *refs):
        g, j = pl.program_id(0), pl.program_id(1)
        which = chosen(g, s_ref)
        out_refs = refs[len(flat):]
        for i in range(len(flat)):
            @pl.when(which == i)
            def _():
                value = refs[i][0].astype(f32).reshape(block, w)
                if len(outs) == 1:
                    out_refs[0][...] = value
                else:
                    for t, out_ref in enumerate(out_refs):
                        @pl.when((g % 2) * nb + j == t)
                        def _():
                            out_ref[...] = value

    def source(i):
        index = flat[i][1]
        return pl.BlockSpec((1, cb, r, w), lambda g, j, s: (index, jnp.where(chosen(g, s) == i, j, 0), 0, 0))

    def out_at(t):
        def index(g, j, s):
            return place(g // 2, (g % 2) * nb + j, t)
        return pl.BlockSpec((block, w), index)

    return pl.pallas_call(
        kernel,
        grid_spec=pltpu.PrefetchScalarGridSpec(
            num_scalar_prefetch=1, grid=(4, nb), in_specs=[source(i) for i in range(len(flat))],
            out_specs=[out_at(t) for t in range(len(outs))]),
        out_shape=[sds(o, f32) for o in outs],
        compiler_params=params(),
        cost_estimate=cost(0, 6 * 4 * c * r * w),
        name=name,
    )(scalars, *[a for a, _ in flat])


def local(
    boundary,
    lengths,
    norm_one_gain,
    norm_one_bias,
    query_weight,
    query_bias,
    key_weight,
    value_weight,
    value_bias,
    first_value_weight,
    first_value_bias,
    out_weight,
    out_bias,
    norm_two_gain,
    norm_two_bias,
    up_weight,
    up_bias,
    down_weight,
    down_bias,
):
    section = lax.axis_index("section")
    spot = lax.axis_index("dp")
    dp = lax.axis_size("dp")
    on_first = section == 0
    sec = jnp.reshape(section, (1,)).astype(jnp.int32)
    rows = boundary.shape[1] // 2
    d = boundary.shape[2]
    half = value_weight.shape[2]
    ff = up_weight.shape[2]

    def swap(array):
        return lax.ppermute(array, "section", SWAP)

    def row(vector):
        return jnp.reshape(vector, (-1, d))

    vec_own = jnp.concatenate([
        norm_one_gain, norm_one_bias, query_bias,
        jnp.concatenate([first_value_bias[None], value_bias], axis=1),
        out_bias, norm_two_gain, norm_two_bias, down_bias, row(up_bias)], axis=0)
    vec_own = jnp.pad(vec_own, ((0, VEC_ROWS - vec_own.shape[0]), (0, 0)))
    top, bottom = boundary[0, :rows], boundary[0, rows:]
    arrived_rows = swap(jnp.where(on_first, bottom, top))
    kept_rows = jnp.where(on_first, top, bottom)
    x0 = jnp.where(on_first, kept_rows, arrived_rows)
    dz1 = jnp.where(on_first, arrived_rows, kept_rows)
    vec_arrived = swap(vec_own)
    vec = (jnp.where(on_first, vec_own, vec_arrived), jnp.where(on_first, vec_arrived, vec_own))
    w = {"qo": query_weight[0], "ko": key_weight[0], "vo": value_weight[0], "oo": out_weight[0],
         "uo": up_weight[0], "do": down_weight[0], "f": first_value_weight}
    for name in "qkvoud":
        w[name + "r"] = swap(w[name + "o"])

    own_lengths = jnp.where(on_first, lengths[0], lengths[1])
    cuts = jnp.cumsum(own_lengths)
    at = jnp.arange(rows, dtype=jnp.int32)
    start = jnp.max(jnp.where(at[:, None] >= cuts[None, :], cuts[None, :], 0), axis=1).astype(jnp.int32)
    start_col, start_row = start[:, None], start[None, :]

    kept = []
    x, shared = x0, x0
    for layer in range(2):
        h, q, k, v, o, m, e, lse = attn_forward(layer, sec, x, shared, start_col, vec[layer], w)
        u, a, z = feed_forward(layer, sec, e, m, vec[layer], w)
        kept.append((x, h, q, k, v, o, m, e, lse, u, a))
        x, shared = z, v
    y = x

    chunk_rows = ff // (2 * dp)
    first_bits, second_bits = bit_orders(dp)
    bits = [jnp.reshape((spot >> jnp.where(on_first, first_bits[s], second_bits[s])) & 1, (1,)).astype(jnp.int32)
            for s in range(len(first_bits))]

    def begin(pieces):
        send, keep = pieces
        arrived = swap(send)
        send, keep = add_split(bits[0], [(keep[None], arrived[None])])
        return keep, exchange(send, dp, 0)

    def reduce_rest(parts):
        for s in range(1, len(bits)):
            send, keep = add_split(bits[s], parts)
            parts = [(keep, exchange(send, dp, s))]
        keep, arrived = parts[0]
        return (keep.astype(f32) + arrived.astype(f32)).astype(bf16)

    def gather(cur):
        for s in reversed(range(1, len(bits))):
            cur = merge(bits[s], cur, exchange(cur, dp, s))
        return cur, exchange(cur, dp, 0)

    dz = dz1
    dr2 = jnp.zeros((rows, half), f32)
    started, small = [], []
    for layer in (1, 0):
        x, h, q, k, v, o, m, e, lse, u, a = kept[layer]
        started.append(begin(down_gradient(sec, a, dz, chunk_rows)))
        du, dm, low, small_feed = feed_backward(layer, sec, dz, u, m, vec[layer], w)
        started.append(begin(up_gradient(sec, e, du, chunk_rows)))
        dz, dq, dk, dv, dr2, small_attn = attn_backward(
            layer, sec, x, dm, low, q, k, v, o, lse, start_row, vec[layer], dr2, w)
        started.append(begin(attn_gradient(sec, o, low, h, dq, dk, dv, chunk_rows)))
        small.append(small_feed + small_attn)
    dx0 = dz

    to_second = lambda t: lax.ppermute(t, "section", [(0, 1)])
    to_first = lambda t: lax.ppermute(t, "section", [(1, 0)])

    cur_a, got_a = gather(reduce_rest(started[0:2]))
    cur_b, got_b = gather(reduce_rest(started[2:4]))
    cur_c, got_c = gather(reduce_rest(started[4:6]))
    other_a = (to_second(cur_a), to_second(got_a))
    other_b = tuple(swap(jnp.where(on_first, t[0], t[1]))[None] for t in (cur_b, got_b))
    other_c = (to_first(cur_c), to_first(got_c))
    scalars = jnp.stack([section, (spot >> first_bits[0]) & 1, (spot >> second_bits[0]) & 1]).astype(jnp.int32)

    down_grad, = assemble(
        scalars, (((cur_b, 1), (got_b, 1), (other_b[0], 0), (other_b[1], 0)),
                  ((cur_a, 0), (got_a, 0), (other_a[0], 0), (other_a[1], 0))),
        [(ff, d)], lambda part, block, t: (part * 4 + block, 0), "assemble_down")
    up_grad, = assemble(
        scalars, (((cur_c, 0), (got_c, 0), (other_c[0], 0), (other_c[1], 0)),
                  ((cur_a, 1), (got_a, 1), (other_a[0], 1), (other_a[1], 1))),
        [(d, ff)], lambda part, block, t: (block % 2, part * 2 + block // 2), "assemble_up")
    out_grad, query_grad, key_grad, mixed_grad = assemble(
        scalars, (((cur_c, 1), (got_c, 1), (other_c[0], 1), (other_c[1], 1)),
                  ((cur_b, 0), (got_b, 0), (other_b[0], 0), (other_b[1], 0))),
        [(d, d)] * 4, lambda part, block, t: (jnp.where(block < t, jnp.maximum(part - 1, 0), part), 0),
        "assemble_attn")
    last = jnp.where(bits[0][0] == 1, cur_c[1], got_c[1])
    first_grad = last.reshape(-1, d)[-(d // 2):, :half].astype(f32)

    own_small = jnp.where(on_first, small[1], small[0])
    total = own_small + swap(jnp.where(on_first, small[0], small[1]))
    for s in range(len(bits)):
        total = total + lax.ppermute(total, "dp", [(i, i ^ (1 << s)) for i in range(dp)])
    first_bias = to_second(total[VBIAS, :half])
    first_bias = jnp.where(on_first, total[VBIAS, :half // 2], first_bias[half // 2:])

    send_end = swap(jnp.where(on_first, y, dx0))
    keep_end = jnp.where(on_first, dx0, y)
    block_ends = jnp.where(on_first, jnp.concatenate([keep_end, send_end], axis=0),
                           jnp.concatenate([send_end, keep_end], axis=0))[None]
    return (
        block_ends,
        total[GAIN1][None],
        total[BIAS1][None],
        query_grad[None],
        total[QBIAS][None],
        key_grad[None],
        mixed_grad[None, :, half:],
        total[VBIAS, half:][None],
        first_grad,
        first_bias,
        out_grad[None],
        total[OBIAS][None],
        total[GAIN2][None],
        total[BIAS2][None],
        up_grad[None],
        total[UBIAS:UBIAS + ff // d].reshape(1, ff),
        down_grad[None],
        total[DBIAS][None],
    )


def solution(mesh):
    stacked = P("section", None, None)
    vector = P("section", None)
    return jax.shard_map(
        local,
        mesh=mesh,
        in_specs=(
            P("section", "dp", None), P("dp", None),
            vector, vector, stacked, vector, stacked, stacked, vector, P(), P(),
            stacked, vector, vector, vector, stacked, vector, stacked, vector,
        ),
        out_specs=(
            P("section", "dp", None),
            vector, vector, stacked, vector, stacked, stacked, vector, P("section"), P("section"),
            stacked, vector, vector, vector, stacked, vector, stacked, vector,
        ),
        check_vma=False,
    )
```

```python
import functools

import jax
import jax.numpy as jnp
from jax import lax
from jax.experimental import pallas as pl
from jax.experimental.pallas import tpu as pltpu
from jax.sharding import PartitionSpec as P

HEADS = 12
HEAD = 64
PAIR = 2 * HEAD
VMEM_BYTES = 64 * 1024 * 1024

eps_norm = 1e-05
neg_fill = -1e30

f32 = jnp.float32
bf16 = jnp.bfloat16

NN = (((1,), (0,)), ((), ()))
NT = (((1,), (1,)), ((), ()))
TN = (((0,), (0,)), ((), ()))

ANY = pl.BlockSpec(memory_space=pl.ANY)
SMEM = pl.BlockSpec(memory_space=pltpu.SMEM)
VMEM = pl.BlockSpec(memory_space=pltpu.VMEM)

GAIN1, BIAS1, QBIAS, VBIAS, OBIAS, GAIN2, BIAS2, DBIAS, UBIAS = range(9)
VEC_ROWS = 16

TIME_SCALE = 0.5


def mm(left, right, dims=NN):
    return lax.dot_general(left, right, dims, preferred_element_type=f32)


def sds(shape, dtype):
    return jax.ShapeDtypeStruct(shape, dtype)


def params():
    return pltpu.CompilerParams(vmem_limit_bytes=VMEM_BYTES)


def cost(micros):
    return pl.CostEstimate(flops=int(1e11), bytes_accessed=1, transcendentals=0)


def start_fetch(mine, own, recv, dst, sem):
    @pl.when(mine)
    def _():
        pltpu.make_async_copy(own, dst, sem).start()

    @pl.when(jnp.logical_not(mine))
    def _():
        pltpu.make_async_copy(recv, dst, sem).start()


def wait_fetch(own, dst, sem):
    pltpu.make_async_copy(own, dst, sem).wait()


def norm_parts(rows):
    centre = jnp.mean(rows, axis=-1, keepdims=True)
    centred = rows - centre
    spread = jnp.mean(centred * centred, axis=-1, keepdims=True)
    factor = lax.rsqrt(spread + eps_norm)
    return centred * factor, factor


def norm_back(grad_t, n, w):
    return w * (
        grad_t
        - jnp.mean(grad_t, axis=-1, keepdims=True)
        - n * jnp.mean(grad_t * n, axis=-1, keepdims=True)
    )


def row_sum(x):
    return jnp.sum(x, axis=0, keepdims=True)


def attend(rows, q_s, k_s, v_s, o_s, lse_s, bias_s):
    lane = lax.broadcasted_iota(jnp.int32, (1, PAIR), 1)
    step = rows // 2

    def pair(hp, carry):
        ls = pl.ds(pl.multiple_of(hp * PAIR, PAIR), PAIR)
        q2 = q_s[:, ls] * jnp.asarray(HEAD ** -0.5, bf16)
        k2 = k_s[:, ls]
        v2 = v_s[:, ls]
        zero = jnp.zeros((), bf16)
        for qb in range(2):
            qr = slice(qb * step, (qb + 1) * step)
            keys = (qb + 1) * step
            mixed = None
            for j in range(2):
                inside = (lane >= j * HEAD) & (lane < (j + 1) * HEAD)
                kh = jnp.where(inside, k2[:keys], zero)
                vh = jnp.where(inside, v2[:keys], zero)
                s = mm(q2[qr], kh, NT) + bias_s[qr, :keys]
                peak = jnp.max(s, axis=-1, keepdims=True)
                p = jnp.exp(s - peak)
                total = jnp.sum(p, axis=-1, keepdims=True)
                low = (p * (1.0 / total)).astype(bf16)
                part = mm(low, vh)
                mixed = part if mixed is None else mixed + part
                lse_s[qr, :] = jnp.where(lane == 2 * hp + j, peak + jnp.log(total), lse_s[qr, :])
            o_s[qr, ls] = mixed.astype(bf16)
        return carry

    lse_s[...] = jnp.zeros(lse_s.shape, f32)
    lax.fori_loop(0, HEADS // 2, pair, 0)


def attn_forward_steps(layer, sec_ref, x_ref, r_ref, start_ref, vec_ref, weights, outs, held, in_sem, out_sem):
    (qw_o, qw_r, kw_o, kw_r, vw_o, vw_r, fw, ow_o, ow_r), (wq, wk, wv, wo) = weights
    h_out, q_out, k_out, v_out, o_out, m_out, e_out, lse_out, sent_out = outs
    h_s, q_s, k_s, v_s, o_s, m_s, e_s, lse_s, lset_s, bias_s = held
    mine = sec_ref[0] == layer
    rows = x_ref.shape[0]
    half = fw.shape[1]
    copies = []

    def fetch():
        start_fetch(mine, qw_o, qw_r, wq, in_sem.at[0])
        start_fetch(mine, kw_o, kw_r, wk, in_sem.at[1])
        start_fetch(mine, vw_o, vw_r, wv.at[:, half:], in_sem.at[2])
        if layer == 0:
            pltpu.make_async_copy(fw, wv.at[:, :half], in_sem.at[3]).start()
        start_fetch(mine, ow_o, ow_r, wo, in_sem.at[4])

    def put(src, dst):
        copy = pltpu.make_async_copy(src, dst, out_sem.at[len(copies)])
        copy.start()
        copies.append(copy)

    def run():
        wide = x_ref[...].astype(f32)
        n, _ = norm_parts(wide)
        h_s[...] = (n * vec_ref[GAIN1:GAIN1 + 1, :] + vec_ref[BIAS1:BIAS1 + 1, :]).astype(bf16)
        put(h_s, h_out)
        theirs = pl.ds(pl.multiple_of((1 - sec_ref[0]) * half, half), half)
        put(h_s.at[:, theirs], sent_out.at[0, :, half:])
        at_row = lax.broadcasted_iota(jnp.int32, (rows, rows), 0)
        at_col = lax.broadcasted_iota(jnp.int32, (rows, rows), 1)
        bias_s[...] = jnp.where((at_col <= at_row) & (at_col >= start_ref[...]), 0.0, neg_fill)
        wait_fetch(qw_o, wq, in_sem.at[0])
        q_s[...] = (mm(h_s[...], wq[...]) + vec_ref[QBIAS:QBIAS + 1, :]).astype(bf16)
        put(q_s, q_out)
        wait_fetch(kw_o, wk, in_sem.at[1])
        k_s[...] = mm(h_s[...], wk[...]).astype(bf16)
        put(k_s, k_out)
        wait_fetch(vw_o, wv.at[:, half:], in_sem.at[2])
        if layer == 0:
            wait_fetch(fw, wv.at[:, :half], in_sem.at[3])
            v_s[...] = (mm(h_s[...], wv[...]) + vec_ref[VBIAS:VBIAS + 1, :]).astype(bf16)
        else:
            v_s[:, :half] = r_ref[:, :half]
            v_s[:, half:] = (mm(h_s[...], wv[:, half:]) + vec_ref[VBIAS:VBIAS + 1, half:]).astype(bf16)
        put(v_s, v_out)
        attend(rows, q_s, k_s, v_s, o_s, lse_s, bias_s)
        put(o_s, o_out)
        put(o_s.at[:, theirs], sent_out.at[0, :, :half])
        lset_s[...] = jnp.transpose(lse_s[...])[:VEC_ROWS, :]
        put(lset_s, lse_out)
        wait_fetch(ow_o, wo, in_sem.at[4])
        m = x_ref[...].astype(f32) + (mm(o_s[...], wo[...]) + vec_ref[OBIAS:OBIAS + 1, :])
        m_s[...] = m
        put(m_s, m_out)
        n, _ = norm_parts(m)
        e_s[...] = (n * vec_ref[GAIN2:GAIN2 + 1, :] + vec_ref[BIAS2:BIAS2 + 1, :]).astype(bf16)
        put(e_s, e_out)
        put(e_s, sent_out.at[1])

    return fetch, run, copies


def attn_forward_kernel(layer, sec_ref, x_ref, r_ref, start_ref, vec_ref, *refs):
    fetch, run, copies = attn_forward_steps(
        layer, sec_ref, x_ref, r_ref, start_ref, vec_ref, (refs[:9], refs[18:22]), refs[9:18], refs[22:32],
        refs[32], refs[33])
    fetch()
    run()
    for copy in copies:
        copy.wait()


def attn_forward_shapes(rows, d):
    act = sds((rows, d), bf16)
    wbuf = pltpu.VMEM((d, d), bf16)
    abuf = pltpu.VMEM((rows, d), bf16)
    outs = [act, act, act, act, act, sds((rows, d), f32), act, sds((VEC_ROWS, rows), f32), sds((2, rows, d), bf16)]
    scratch = [wbuf, wbuf, wbuf, wbuf, abuf, abuf, abuf, abuf, abuf,
               pltpu.VMEM((rows, d), f32), abuf, pltpu.VMEM((rows, PAIR), f32),
               pltpu.VMEM((VEC_ROWS, rows), f32), pltpu.VMEM((rows, rows), f32),
               pltpu.SemaphoreType.DMA((5,)), pltpu.SemaphoreType.DMA((11,))]
    return outs, scratch


def attn_forward(layer, sec, x, r, start, vec, w):
    outs, scratch = attn_forward_shapes(*x.shape)
    return pl.pallas_call(
        functools.partial(attn_forward_kernel, layer),
        out_shape=outs,
        in_specs=[SMEM, VMEM, VMEM, VMEM, VMEM] + [ANY] * 9,
        out_specs=[ANY] * 9,
        scratch_shapes=scratch,
        compiler_params=params(),
        cost_estimate=cost(15),
        name="attn_forward",
    )(sec, x, r, start, vec, w["qo"], w["qr"], w["ko"], w["kr"], w["vo"], w["vr"], w["f"], w["oo"], w["or"])


def gelu(u):
    half_u = 0.5 * u
    return half_u + half_u * jnp.tanh(u * (0.7978845608028654 + 0.035677408136300125 * (u * u)))


def middle_kernel(blk, sec_ref, e_ref, m_ref, r_ref, start_ref, vec0_ref, vec1_ref, *refs):
    up_o, up_r, dn_o, dn_r = refs[:4]
    attn_w, outs = refs[4:13], refs[13:28]
    wu0, wd0, wu1, u_s, a_s, f_s, x_s, acc, up_sem, put_sem = refs[28:38]
    wbufs, held, in_sem, out_sem = refs[38:42], refs[42:52], refs[52], refs[53]
    u0_out, a0_out, x_out, u1_out, a1_out, sent_out = outs[:6]
    steps = wu0.shape[0]
    section = sec_ref[0]
    cols = [pl.ds(b * blk, blk) for b in range(steps)]
    for b in range(steps):
        start_fetch(section == 0, up_o.at[:, cols[b]], up_r.at[:, cols[b]], wu0.at[b], up_sem.at[0, b])
    for b in range(steps):
        start_fetch(section == 0, dn_o.at[cols[b], :], dn_r.at[cols[b], :], wd0.at[b], up_sem.at[1, b])
    fetch, run, copies = attn_forward_steps(
        1, sec_ref, x_s, r_ref, start_ref, vec1_ref, (attn_w, wbufs), outs[6:], held, in_sem, out_sem)
    fetch()
    for b in range(steps):
        start_fetch(section == 1, up_o.at[:, cols[b]], up_r.at[:, cols[b]], wu1.at[b], up_sem.at[2, b])
    own = []

    def put(src, dst):
        copy = pltpu.make_async_copy(src, dst, put_sem.at[len(own)])
        copy.start()
        own.append(copy)

    def expand(layer, b, source, weights, vec_ref):
        wait_fetch(up_o.at[:, cols[0]], weights.at[b], up_sem.at[2 * layer, b])
        f_s[b % 2] = mm(source[...], weights[b]) + vec_ref[UBIAS + b:UBIAS + b + 1, :]

    def activate(layer, b, u_out, a_out):
        u = f_s[b % 2]
        u_s[layer, b] = u.astype(bf16)
        a_s[layer, b] = gelu(u).astype(bf16)
        put(u_s.at[layer, b], u_out.at[:, cols[b]])
        put(a_s.at[layer, b], a_out.at[:, cols[b]])

    expand(0, 0, e_ref, wu0, vec0_ref)
    for b in range(steps):
        if b + 1 < steps:
            expand(0, b + 1, e_ref, wu0, vec0_ref)
        activate(0, b, u0_out, a0_out)
        wait_fetch(dn_o.at[cols[0], :], wd0.at[b], up_sem.at[1, b])
        part = mm(a_s[0, b], wd0[b])
        acc[...] = part if b == 0 else acc[...] + part
    x_s[...] = (m_ref[...] + (acc[...] + vec0_ref[DBIAS:DBIAS + 1, :])).astype(bf16)
    put(x_s, x_out)
    run()
    expand(1, 0, held[6], wu1, vec1_ref)
    for b in range(steps):
        if b + 1 < steps:
            expand(1, b + 1, held[6], wu1, vec1_ref)
        activate(1, b, u1_out, a1_out)
    theirs = (1 - section) * (steps // 2)
    for b in range(steps // 2):
        for layer in range(2):
            put(a_s.at[layer, theirs + b], sent_out.at[layer, :, cols[b]])
    for copy in own + copies:
        copy.wait()


def middle(sec, e, m, r, start, vec, w):
    rows, d = e.shape
    ff = w["uo"].shape[1]
    blk = d
    n = ff // blk
    outs, scratch = attn_forward_shapes(rows, d)
    wide = sds((rows, ff), bf16)
    return pl.pallas_call(
        functools.partial(middle_kernel, blk),
        out_shape=[wide, wide, sds((rows, d), bf16), wide, wide, sds((2, rows, ff // 2), bf16)] + outs,
        in_specs=[SMEM] + [VMEM] * 6 + [ANY] * 13,
        out_specs=[ANY] * 15,
        scratch_shapes=[pltpu.VMEM((n, d, blk), bf16), pltpu.VMEM((n, blk, d), bf16), pltpu.VMEM((n, d, blk), bf16),
                        pltpu.VMEM((2, n, rows, blk), bf16), pltpu.VMEM((2, n, rows, blk), bf16),
                        pltpu.VMEM((2, rows, blk), f32), pltpu.VMEM((rows, d), bf16), pltpu.VMEM((rows, d), f32),
                        pltpu.SemaphoreType.DMA((3, n)), pltpu.SemaphoreType.DMA((4 * n + 1 + n,))] + scratch,
        compiler_params=params(),
        cost_estimate=cost(15),
        name="middle",
    )(sec, e, m, r, start, vec[0], vec[1], w["uo"], w["ur"], w["do"], w["dr"],
      w["qo"], w["qr"], w["ko"], w["kr"], w["vo"], w["vr"], w["f"], w["oo"], w["or"])


def theirs_at(steps):
    half = steps // 2

    def index(j, s):
        return (0, jnp.where(s[0] == 0, jnp.maximum(j - half, 0), jnp.minimum(j, half - 1)))
    return index


def feed_down_kernel(layer, blk, sec_ref, a_ref, m_ref, vec_ref, dn_o, dn_r, z_ref, wd, acc, sem):
    j = pl.program_id(0)
    steps = pl.num_programs(0)
    mine = sec_ref[0] == layer

    @pl.when(j == 0)
    def _():
        for b in range(dn_o.shape[0] // blk):
            cols = pl.ds(b * blk, blk)
            start_fetch(mine, dn_o.at[cols, :], dn_r.at[cols, :], wd.at[b], sem.at[b])

    wait_fetch(dn_o.at[pl.ds(0, blk), :], wd.at[j], sem.at[j])
    part = mm(a_ref[...], wd[j])

    @pl.when(j == 0)
    def _():
        acc[...] = part

    @pl.when((j > 0) & (j < steps - 1))
    def _():
        acc[...] += part

    @pl.when(j == steps - 1)
    def _():
        z_ref[...] = (m_ref[...] + (acc[...] + part + vec_ref[DBIAS:DBIAS + 1, :])).astype(bf16)


def feed_down(layer, sec, a, m, vec, w):
    rows, ff = a.shape
    d = m.shape[1]
    blk = d
    n = ff // blk
    return pl.pallas_call(
        functools.partial(feed_down_kernel, layer, blk),
        grid=(n,),
        out_shape=sds((rows, d), bf16),
        in_specs=[SMEM, pl.BlockSpec((rows, blk), lambda j: (0, j)), VMEM, VMEM, ANY, ANY],
        out_specs=pl.BlockSpec((rows, d), lambda j: (0, 0)),
        scratch_shapes=[pltpu.VMEM((n, blk, d), bf16), pltpu.VMEM((rows, d), f32), pltpu.SemaphoreType.DMA((n,))],
        compiler_params=params(),
        cost_estimate=cost(8),
        name="feed_down",
    )(sec, a, m, vec, w["do"], w["dr"])


def layer_backward_kernel(layer, blk, sec_ref, dz_ref, m_ref, lse_ref, start_ref, vec_ref, dr2_ref,
                          u_in, x_in, q_in, k_in, v_in, o_in,
                          up_o, up_r, dn_o, dn_r, qw_o, qw_r, kw_o, kw_r, vw_o, vw_r, fw, ow_o, ow_r,
                          du_out, sent_out, bundle_out, shared_ref, small_ref,
                          wu, wd, wq, wk, wv, wo, u_s, x_s, q_ref, k_ref, v_ref, o_ref, du_s, da_s, acc, dm_s,
                          bundle_ref, do_s, delta_s, bias_s, feed_sem, sem, in_sem, out_sem):
    mine = sec_ref[0] == layer
    rows, d = dz_ref.shape
    half = fw.shape[1]
    steps = wu.shape[0]
    cols = [pl.ds(b * blk, blk) for b in range(steps)]
    for b in range(steps):
        start_fetch(mine, dn_o.at[cols[b], :], dn_r.at[cols[b], :], wd.at[b], feed_sem.at[0, b])
        pltpu.make_async_copy(u_in.at[:, cols[b]], u_s.at[b], feed_sem.at[2, b]).start()
        start_fetch(mine, up_o.at[:, cols[b]], up_r.at[:, cols[b]], wu.at[b], feed_sem.at[1, b])
    start_fetch(mine, ow_o, ow_r, wo, sem.at[4])
    loads = [pltpu.make_async_copy(src, dst, in_sem.at[i]) for i, (src, dst) in enumerate(
        ((q_in, q_ref), (k_in, k_ref), (v_in, v_ref), (o_in, o_ref), (x_in, x_s)))]
    for load in loads:
        load.start()
    start_fetch(mine, qw_o, qw_r, wq, sem.at[0])
    start_fetch(mine, kw_o, kw_r, wk, sem.at[1])
    start_fetch(mine, vw_o, vw_r, wv.at[:, half:], sem.at[2])
    if layer == 0:
        pltpu.make_async_copy(fw, wv.at[:, :half], sem.at[3]).start()
    copies = []

    def put(src, dst):
        copy = pltpu.make_async_copy(src, dst, out_sem.at[len(copies)])
        copy.start()
        copies.append(copy)

    small_ref[...] = jnp.zeros(small_ref.shape, f32)

    def expand(b):
        wait_fetch(dn_o.at[cols[0], :], wd.at[b], feed_sem.at[0, b])
        da_s[b % 2] = mm(dz_ref[...], wd[b], NT)

    def activate(b):
        pltpu.make_async_copy(u_in.at[:, cols[b]], u_s.at[b], feed_sem.at[2, b]).wait()
        u = u_s[b].astype(f32)
        sq = u * u
        th = jnp.tanh(u * (0.7978845608028654 + 0.035677408136300125 * sq))
        slope = 0.5 + 0.5 * th + (0.5 * u) * (1.0 - th * th) * (0.7978845608028654 + 0.10703222440890037 * sq)
        du = (slope * da_s[b % 2]).astype(bf16)
        du_s[b] = du
        small_ref[UBIAS + b:UBIAS + b + 1, :] = row_sum(du.astype(f32))
        put(du_s.at[b], du_out.at[:, cols[b]])

    expand(0)
    for b in range(steps):
        if b + 1 < steps:
            expand(b + 1)
        activate(b)
        wait_fetch(up_o.at[:, cols[0]], wu.at[b], feed_sem.at[1, b])
        part = mm(du_s[b], wu[b], NT)
        acc[...] = part if b == 0 else acc[...] + part
    theirs = (1 - sec_ref[0]) * (steps // 2)
    for b in range(steps // 2):
        put(du_s.at[theirs + b], sent_out.at[b])
    de = acc[...]
    n, w = norm_parts(m_ref[...])
    dz = dz_ref[...].astype(f32)
    dm_s[...] = dz + norm_back(de * vec_ref[GAIN2:GAIN2 + 1, :], n, w)
    small_ref[GAIN2:GAIN2 + 1, :] = row_sum(de * n)
    small_ref[BIAS2:BIAS2 + 1, :] = row_sum(de)
    small_ref[DBIAS:DBIAS + 1, :] = row_sum(dz)

    low_ref, dq_ref, dk_ref, dv_ref, dx_ref = (bundle_ref.at[pl.ds(i * rows, rows), :] for i in range(5))
    low_ref[...] = dm_s[...].astype(bf16)
    at_key = lax.broadcasted_iota(jnp.int32, (rows, rows), 0)
    at_query = lax.broadcasted_iota(jnp.int32, (rows, rows), 1)
    bias_s[...] = jnp.where((at_key <= at_query) & (at_key >= start_ref[...]), 0.0, neg_fill)
    wait_fetch(ow_o, wo, sem.at[4])
    do = mm(low_ref[...], wo[...], NT).astype(bf16)
    do_s[...] = do
    for load in loads:
        load.wait()
    head_row = lax.broadcasted_iota(jnp.int32, (VEC_ROWS, d), 0)
    head_col = lax.broadcasted_iota(jnp.int32, (VEC_ROWS, d), 1) // HEAD
    pick = (head_row == head_col).astype(f32)
    delta_s[...] = lax.dot_general(pick, do.astype(f32) * o_ref[...].astype(f32), NT,
                                   precision=lax.Precision.HIGHEST, preferred_element_type=f32)
    lane = lax.broadcasted_iota(jnp.int32, (1, PAIR), 1)
    step = rows // 2
    scale = HEAD ** -0.5
    zero = jnp.zeros((), bf16)

    def pair(hp, carry):
        ls = pl.ds(pl.multiple_of(hp * PAIR, PAIR), PAIR)
        q2 = q_ref[:, ls] * jnp.asarray(scale, bf16)
        k2 = k_ref[:, ls]
        v2 = v_ref[:, ls]
        do2 = do_s[:, ls]
        dq_parts = []
        for kb in range(2):
            kr = slice(kb * step, (kb + 1) * step)
            first = kb * step
            dk = dv = dq = None
            for j in range(2):
                inside = (lane >= j * HEAD) & (lane < (j + 1) * HEAD)
                kh = jnp.where(inside, k2[kr], zero)
                vh = jnp.where(inside, v2[kr], zero)
                qh = jnp.where(inside, q2[first:], zero)
                doh = jnp.where(inside, do2[first:], zero)
                row = pl.ds(2 * hp + j, 1)
                st = mm(kh, qh, NT) + bias_s[kr, first:]
                pt = jnp.exp(st - lse_ref[row, first:])
                dpt = mm(vh, doh, NT)
                dst = (pt * (dpt - delta_s[row, first:])).astype(bf16)
                dv_j = mm(pt.astype(bf16), doh)
                dk_j = mm(dst, qh)
                dq_j = mm(dst, kh, TN)
                dk = dk_j if dk is None else dk + dk_j
                dv = dv_j if dv is None else dv + dv_j
                dq = dq_j if dq is None else dq + dq_j
            dk_ref[kr, ls] = dk.astype(bf16)
            if layer == 1:
                dv_ref[kr, ls] = dv.astype(bf16)

                @pl.when(hp < HEADS // 4)
                def _():
                    shared_ref[kr, ls] = dv
            else:
                extra = jnp.where(hp < HEADS // 4, dr2_ref[kr, pl.ds(pl.multiple_of((hp % (HEADS // 4)) * PAIR, PAIR), PAIR)], 0.0)
                dv_ref[kr, ls] = (dv + extra).astype(bf16)
            dq_parts.append(dq)
        dq_ref[:step, ls] = (dq_parts[0][:step] * scale).astype(bf16)
        dq_ref[step:, ls] = ((dq_parts[0][step:] + dq_parts[1]) * scale).astype(bf16)
        return carry

    if layer == 0:
        shared_ref[...] = jnp.zeros(shared_ref.shape, f32)
    lax.fori_loop(0, HEADS // 2, pair, 0)
    put(bundle_ref.at[pl.ds(0, 4 * rows), :], bundle_out.at[pl.ds(0, 4 * rows), :])

    wait_fetch(qw_o, wq, sem.at[0])
    dh = mm(dq_ref[...], wq[...], NT)
    wait_fetch(kw_o, wk, sem.at[1])
    dh = dh + mm(dk_ref[...], wk[...], NT)
    wait_fetch(vw_o, wv.at[:, half:], sem.at[2])
    if layer == 0:
        wait_fetch(fw, wv.at[:, :half], sem.at[3])
        dh = dh + mm(dv_ref[...], wv[...], NT)
    else:
        dh = dh + mm(dv_ref[:, half:], wv[:, half:], NT)
    n, w = norm_parts(x_s[...].astype(f32))
    dx_ref[...] = (dm_s[...] + norm_back(dh * vec_ref[GAIN1:GAIN1 + 1, :], n, w)).astype(bf16)
    small_ref[GAIN1:GAIN1 + 1, :] = row_sum(dh * n)
    small_ref[BIAS1:BIAS1 + 1, :] = row_sum(dh)
    small_ref[QBIAS:QBIAS + 1, :] = row_sum(dq_ref[...].astype(f32))
    small_ref[VBIAS:VBIAS + 1, :] = row_sum(dv_ref[...].astype(f32))
    small_ref[OBIAS:OBIAS + 1, :] = row_sum(low_ref[...].astype(f32))
    bundle_ref[5 * rows:, :] = small_ref[...].astype(bf16)
    put(bundle_ref.at[pl.ds(4 * rows, rows + VEC_ROWS), :], bundle_out.at[pl.ds(4 * rows, rows + VEC_ROWS), :])
    for copy in copies:
        copy.wait()


def layer_backward(layer, sec, dz, dz_at, t, start_row, vec, dr2, w):
    rows, ff = t["u"].shape
    d = t["m"].shape[1]
    half = w["f"].shape[1]
    blk = d
    n = ff // blk
    wbuf = pltpu.VMEM((d, d), bf16)
    act = pltpu.VMEM((rows, d), bf16)
    wide = pltpu.VMEM((rows, d), f32)
    blocks = pltpu.VMEM((n, rows, blk), bf16)
    dma = pltpu.SemaphoreType.DMA
    bundle = (5 * rows + VEC_ROWS, d)
    return pl.pallas_call(
        functools.partial(layer_backward_kernel, layer, blk),
        grid=(1,),
        out_shape=[sds((rows, ff), bf16), sds((n // 2, rows, blk), bf16), sds(bundle, bf16), sds((rows, half), f32),
                   sds((VEC_ROWS, d), f32)],
        in_specs=[SMEM, pl.BlockSpec((rows, d), lambda i: (dz_at, 0))] + [VMEM] * 5 + [ANY] * 19,
        out_specs=[ANY] * 3 + [VMEM] * 2,
        scratch_shapes=[pltpu.VMEM((n, d, blk), bf16), pltpu.VMEM((n, blk, d), bf16), wbuf, wbuf, wbuf, wbuf,
                        blocks, act, act, act, act, act, blocks, pltpu.VMEM((2, rows, blk), f32), wide, wide,
                        pltpu.VMEM(bundle, bf16), act, pltpu.VMEM((VEC_ROWS, rows), f32), pltpu.VMEM((rows, rows), f32),
                        dma((3, n)), dma((5,)), dma((5,)), dma((n + n // 2 + 2,))],
        compiler_params=params(),
        cost_estimate=cost(30),
        name="layer_backward",
    )(sec, dz, t["m"], t["lse"], start_row, vec, dr2, t["u"], t["x"], t["q"], t["k"], t["v"], t["o"],
      w["uo"], w["ur"], w["do"], w["dr"],
      w["qo"], w["qr"], w["ko"], w["kr"], w["vo"], w["vr"], w["f"], w["oo"], w["or"])


def store_chunks(ref, value):
    c, r, _ = ref.shape
    for i in range(c):
        ref[i] = value[i * r:(i + 1) * r].astype(bf16)


def quarter_of(g, s):
    return 2 * jnp.where(g < 2, 1 - s[1], s[1]) + g % 2


def quarters(kernel, scalars, in_specs, operands, shape, name):
    per = shape[0] // 2
    return pl.pallas_call(
        kernel,
        grid_spec=pltpu.PrefetchScalarGridSpec(
            num_scalar_prefetch=1, grid=(4,), in_specs=in_specs,
            out_specs=[pl.BlockSpec((per,) + shape[1:], lambda g, s: (jnp.minimum(g, 1), 0, 0)),
                       pl.BlockSpec((per,) + shape[1:], lambda g, s: (jnp.maximum(g - 2, 0), 0, 0))]),
        out_shape=[sds(shape, bf16)] * 2,
        compiler_params=params(),
        cost_estimate=cost(8),
        name=name,
    )(scalars, *operands)


def store_quarter(send_ref, keep_ref, value):
    g = pl.program_id(0)

    @pl.when(g < 2)
    def _():
        store_chunks(send_ref, value)

    @pl.when(g >= 2)
    def _():
        store_chunks(keep_ref, value)


def down_gradient(scalars, a, a_got, dz, dz_got, dz_at, chunk_rows):
    a_got, a_at = a_got
    rows, ff = a.shape
    d = dz.shape[1]
    q = d // 2

    def kernel(s_ref, a_ref, b_ref, x_ref, y_ref, send_ref, keep_ref):
        store_quarter(send_ref, keep_ref, mm(a_ref[...], x_ref[...], TN) + mm(b_ref[0], y_ref[...], TN))

    whole = pl.BlockSpec((rows, d), lambda g, s: (dz_at, 0))
    return quarters(
        kernel, scalars,
        [pl.BlockSpec((rows, q), lambda g, s: (0, 4 * s[0] + quarter_of(g, s))),
         pl.BlockSpec((1, rows, q), lambda g, s: (a_at, 0, quarter_of(g, s))), whole, whole],
        (a, a_got, dz, dz_got), (2 * q // chunk_rows, chunk_rows, d), "down_gradient")


def up_gradient(scalars, e, sent_got, du, du_got, chunk_rows):
    rows, ff = du.shape
    d = e.shape[1]
    q = d // 2

    def kernel(s_ref, e_ref, f_ref, du_ref, dg_ref, send_ref, keep_ref):
        store_quarter(send_ref, keep_ref, mm(e_ref[...], du_ref[...], TN) + mm(f_ref[0], dg_ref[0], TN))

    return quarters(
        kernel, scalars,
        [pl.BlockSpec((rows, q), lambda g, s: (0, g % 2)),
         pl.BlockSpec((1, rows, q), lambda g, s: (1, 0, g % 2)),
         pl.BlockSpec((rows, d), lambda g, s: (0, 2 * s[0] + quarter_of(g, s) // 2)),
         pl.BlockSpec((1, rows, d), lambda g, s: (quarter_of(g, s) // 2, 0, 0))],
        (e, sent_got, du, du_got), (2 * q // chunk_rows, chunk_rows, d), "up_gradient")


def vector_share(width, chunks):
    return max(PAIR, VEC_ROWS * width // chunks)


def attn_gradient(scalars, o, h, sent_got, bundle, bundle_got, small, chunk_rows, extra):
    rows, d = o.shape
    q = d // 2
    per = q // chunk_rows
    share = vector_share(d, 8 * per)

    def kernel(s_ref, o_ref, h_ref, l_ref, own_ref, got_ref, small_ref, small_got_ref, send_ref, keep_ref, sum_ref):
        sum_ref[...] = small_ref[...] + small_got_ref[...].astype(f32)
        g = pl.program_id(0)
        which = quarter_of(g, s_ref)
        for i in range(4):
            @pl.when(which == i)
            def _():
                left = o_ref if i == 0 else h_ref
                value = mm(left[...], own_ref[...], TN) + mm(l_ref[0], got_ref[...], TN)
                for side, ref in enumerate((send_ref, keep_ref)):
                    @pl.when(g // 2 == side)
                    def _():
                        ref[:, chunk_rows:, :] = jnp.zeros((per, extra, d), bf16)
                        for c in range(per):
                            ref[c, :chunk_rows, :] = value[c * chunk_rows:(c + 1) * chunk_rows].astype(bf16)
                        for part_index in range(2):
                            @pl.when(s_ref[0] == part_index)
                            def _():
                                for c in range(per):
                                    at = ((4 * part_index + i) * per + c) * share
                                    if at < VEC_ROWS * d:
                                        row = sum_ref[at // d:at // d + 1, at % d:at % d + share]
                                        ref[c, chunk_rows:chunk_rows + 1, :share] = row.astype(bf16)

    part = pl.BlockSpec((rows, q), lambda g, s: (0, s[0]))
    right = pl.BlockSpec((rows, d), lambda g, s: (quarter_of(g, s), 0))
    shape = (2 * per, chunk_rows + extra, d)
    return pl.pallas_call(
        kernel,
        grid_spec=pltpu.PrefetchScalarGridSpec(
            num_scalar_prefetch=1, grid=(4,),
            in_specs=[part, part,
                      pl.BlockSpec((1, rows, q), lambda g, s: (0, 0, jnp.minimum(quarter_of(g, s), 1))),
                      right, right, pl.BlockSpec((VEC_ROWS, d), lambda g, s: (0, 0)),
                      pl.BlockSpec((VEC_ROWS, d), lambda g, s: (5 * rows // VEC_ROWS, 0))],
            out_specs=[pl.BlockSpec((per,) + shape[1:], lambda g, s: (jnp.minimum(g, 1), 0, 0)),
                       pl.BlockSpec((per,) + shape[1:], lambda g, s: (jnp.maximum(g - 2, 0), 0, 0))],
            scratch_shapes=[pltpu.VMEM((VEC_ROWS, d), f32)]),
        out_shape=[sds(shape, bf16)] * 2,
        compiler_params=params(),
        cost_estimate=cost(9),
        name="attn_gradient",
    )(scalars, o, h, sent_got, bundle, bundle_got, small, bundle_got)


AXES = ("section", "dp")
SWAP = [(0, 1), (1, 0)]


def bit_orders(dp):
    bits = list(range(dp.bit_length() - 1))
    if len(bits) < 3:
        return bits, bits[::-1]
    return [0, 2, 1] + bits[3:], [1, 2, 0] + bits[3:]


def exchange(array, dp, step):
    first, second = bit_orders(dp)
    pairs = [(i, i ^ (1 << first[step])) for i in range(dp)]
    pairs += [(dp + i, dp + (i ^ (1 << second[step]))) for i in range(dp)]
    return lax.ppermute(array, AXES, pairs)


def block_of(chunks, rows):
    best = 1
    for c in range(1, chunks + 1):
        if chunks % c == 0 and c * rows <= 768:
            best = c
    return best


def add_split(bit, parts):
    _, c, r, w = parts[0][0].shape
    counts = [p[0].shape[0] for p in parts]
    n = sum(counts)
    h = c // 2
    cb = block_of(h, r)
    nb = h // cb
    ends = [sum(counts[:i + 1]) for i in range(len(counts))]
    begins = [e - k for e, k in zip(ends, counts)]

    def kernel(s_ref, *refs):
        send_ref, keep_ref = refs[-2:]
        g, i = pl.program_id(0), pl.program_id(1)
        for t in range(len(parts)):
            @pl.when((i >= begins[t]) & (i < ends[t]))
            def _():
                total = (refs[2 * t][...].astype(f32) + refs[2 * t + 1][...].astype(f32)).astype(bf16)

                @pl.when(g == 0)
                def _():
                    send_ref[...] = total

                @pl.when(g == 1)
                def _():
                    keep_ref[...] = total

    def source(t):
        def index(g, i, j, s):
            inside = (i >= begins[t]) & (i < ends[t])
            side = jnp.where(g == 0, 1 - s[0], s[0])
            return (jnp.clip(i - begins[t], 0, counts[t] - 1), jnp.where(inside, side * nb + j, 0), 0, 0)
        return pl.BlockSpec((1, cb, r, w), index)

    def send_at(g, i, j, s):
        return (jnp.where(g == 0, i, n - 1), jnp.where(g == 0, j, nb - 1), 0, 0)

    def keep_at(g, i, j, s):
        return (jnp.where(g == 0, 0, i), jnp.where(g == 0, 0, j), 0, 0)

    flat = [x for p in parts for x in p]
    return pl.pallas_call(
        kernel,
        grid_spec=pltpu.PrefetchScalarGridSpec(
            num_scalar_prefetch=1, grid=(2, n, nb),
            in_specs=[source(t) for t in range(len(parts)) for _ in range(2)],
            out_specs=[pl.BlockSpec((1, cb, r, w), send_at), pl.BlockSpec((1, cb, r, w), keep_at)]),
        out_shape=[sds((n, h, r, w), bf16)] * 2,
        compiler_params=params(),
        cost_estimate=cost(1.5 + 3.5 * n * c / 8),
        name="add_split",
    )(bit, *flat)


def merge(bit, cur, arrived):
    n, c, r, w = cur.shape
    cb = block_of(c, r)
    nb = c // cb

    def kernel(s_ref, a_ref, b_ref, out_ref):
        g = pl.program_id(1)

        @pl.when(g == s_ref[0])
        def _():
            out_ref[...] = a_ref[...]

        @pl.when(g != s_ref[0])
        def _():
            out_ref[...] = b_ref[...]

    def at(own):
        def index(i, g, j, s):
            mine = (g == s[0]) if own else (g != s[0])
            return (i, jnp.where(mine, j, 0), 0, 0)
        return pl.BlockSpec((1, cb, r, w), index)

    return pl.pallas_call(
        kernel,
        grid_spec=pltpu.PrefetchScalarGridSpec(
            num_scalar_prefetch=1, grid=(n, 2, nb), in_specs=[at(True), at(False)],
            out_specs=pl.BlockSpec((1, cb, r, w), lambda i, g, j, s: (i, g * nb + j, 0, 0))),
        out_shape=sds((n, 2 * c, r, w), bf16),
        compiler_params=params(),
        cost_estimate=cost(1.5 + 2 * n * c / 8),
        name="merge",
    )(bit, cur, arrived)


def assemble(scalars, sources, chunk_rows, outs, place, name, extra=0):
    _, c, r, w = sources[0].shape
    cb = c // 2
    block = cb * chunk_rows

    def position(g, s):
        part, t = g // 8, g % 8
        own = part == s[0]
        top, mid, low = t // 4, (t // 2) % 2, t % 2
        return jnp.where(own, top, low), mid, jnp.where(own, low, top)

    def chosen(g, s):
        top, mid, _ = position(g, s)
        return 2 * jnp.where(top == s[1], 0, 1) + jnp.where(mid == s[2], 0, 1)

    def kernel(s_ref, *refs):
        g = pl.program_id(0)
        which = chosen(g, s_ref)
        out_refs = refs[4:]
        for i in range(4):
            @pl.when(which == i)
            def _():
                held = refs[i][0].astype(f32)
                value = held[:, :chunk_rows].reshape(block, w)
                if len(outs) == 1:
                    out_refs[0][...] = value
                else:
                    for t in range(len(outs)):
                        @pl.when((g % 8) // 2 == t)
                        def _():
                            out_refs[t][...] = value
                if extra:
                    out_refs[len(outs)][0] = held[:, chunk_rows, :]

    def source(i):
        def index(g, s):
            return (jnp.where(chosen(g, s) == i, g // 8, 0), jnp.where(chosen(g, s) == i, position(g, s)[2], 0), 0, 0)
        return pl.BlockSpec((1, cb, r, w), index)

    def out_at(t):
        return pl.BlockSpec((block, w), lambda g, s: place(g // 8, g % 8, t))

    out_specs = [out_at(t) for t in range(len(outs))]
    out_shape = [sds(o, f32) for o in outs]
    if extra:
        out_specs.append(pl.BlockSpec((1, cb, w), lambda g, s: (g, 0, 0)))
        out_shape.append(sds((16, cb, w), f32))
    return pl.pallas_call(
        kernel,
        grid_spec=pltpu.PrefetchScalarGridSpec(
            num_scalar_prefetch=1, grid=(16,), in_specs=[source(i) for i in range(4)], out_specs=out_specs),
        out_shape=out_shape,
        compiler_params=params(),
        cost_estimate=cost(12),
        name=name,
    )(scalars, *sources)


def after(array, *earlier):
    return lax.optimization_barrier((array,) + earlier)[0]


class Order:
    def __init__(self):
        self.last = ()

    def mark(self, *arrays):
        self.last = arrays

    def also(self, *arrays):
        self.last = self.last + arrays

    def tie(self, array):
        return after(array, *self.last) if self.last else array


def local(
    boundary,
    lengths,
    norm_one_gain,
    norm_one_bias,
    query_weight,
    query_bias,
    key_weight,
    value_weight,
    value_bias,
    first_value_weight,
    first_value_bias,
    out_weight,
    out_bias,
    norm_two_gain,
    norm_two_bias,
    up_weight,
    up_bias,
    down_weight,
    down_bias,
):
    section = lax.axis_index("section")
    spot = lax.axis_index("dp")
    dp = lax.axis_size("dp")
    on_first = section == 0
    sec = jnp.reshape(section, (1,)).astype(jnp.int32)
    rows = boundary.shape[1] // 2
    d = boundary.shape[2]
    half = value_weight.shape[2]
    ff = up_weight.shape[2]

    def swap(array):
        return lax.ppermute(array, "section", SWAP)

    def row(vector):
        return jnp.reshape(vector, (-1, d))

    vec_own = jnp.concatenate([
        norm_one_gain, norm_one_bias, query_bias,
        jnp.concatenate([first_value_bias[None], value_bias], axis=1),
        out_bias, norm_two_gain, norm_two_bias, down_bias, row(up_bias)], axis=0)
    vec_own = jnp.pad(vec_own, ((0, VEC_ROWS - vec_own.shape[0]), (0, 0)))
    top, bottom = boundary[0, :rows], boundary[0, rows:]
    arrived_rows = swap(jnp.where(on_first, bottom, top))
    kept_rows = jnp.where(on_first, top, bottom)
    x0 = jnp.where(on_first, kept_rows, arrived_rows)
    dz1 = jnp.where(on_first, arrived_rows, kept_rows)
    dz1_moved = lax.ppermute(bottom, "section", [(1, 0)])
    dz1_got = jnp.where(on_first, dz1_moved, top)
    vec_arrived = swap(vec_own)
    vec = (jnp.where(on_first, vec_own, vec_arrived), jnp.where(on_first, vec_arrived, vec_own))
    w = {"qo": query_weight[0], "ko": key_weight[0], "vo": value_weight[0], "oo": out_weight[0],
         "uo": up_weight[0], "do": down_weight[0], "f": first_value_weight}
    for name in "qkvo":
        w[name + "r"] = swap(w[name + "o"])
    w["ur"] = swap(after(w["uo"], w["qr"]))
    w["dr"] = swap(after(w["do"], w["kr"]))

    own_lengths = jnp.where(on_first, lengths[0], lengths[1])
    cuts = jnp.cumsum(own_lengths)
    at = jnp.arange(rows, dtype=jnp.int32)
    start = jnp.max(jnp.where(at[:, None] >= cuts[None, :], cuts[None, :], 0), axis=1).astype(jnp.int32)
    start_col, start_row = start[:, None], start[None, :]

    chunk_rows = ff // (2 * dp)
    extra = 16
    first_bits, second_bits = bit_orders(dp)
    levels = len(first_bits)
    bit = [((spot >> jnp.where(on_first, first_bits[s], second_bits[s])) & 1).astype(jnp.int32) for s in range(levels)]
    bits = [jnp.reshape(b, (1,)) for b in bit]
    scalars = jnp.stack([sec[0], bit[0], bit[1]])
    order = Order()

    h, q, k, v, o, m, e, lse, sent = attn_forward(0, sec, x0, x0, start_col, vec[0], w)
    kept = [dict(x=x0, h=h, q=q, k=k, v=v, o=o, m=m, e=e, lse=lse, sent_got=swap(sent))]
    u0, a0, x1, u1, a1, a_sent, h, q, k, v, o, m, e, lse, sent = middle(sec, e, m, v, start_col, vec, w)
    a_got = swap(a_sent)
    kept[0].update(u=u0, a=a0, a_got=(a_got, 0))
    kept.append(dict(x=x1, h=h, q=q, k=k, v=v, o=o, m=m, e=e, lse=lse, u=u1, a=a1, sent_got=swap(sent), a_got=(a_got, 1)))
    order.mark(x1)
    y = feed_down(1, sec, a1, order.tie(m), vec[1], w)
    order.mark(y, a_got, kept[0]["sent_got"], kept[1]["sent_got"])

    def cut(level, parts):
        (first_keep, first_got), *rest = parts
        send, keep = add_split(bits[level], [(order.tie(first_keep), first_got)] + rest)
        order.mark(send)
        return keep, exchange(send, dp, level)

    def deep(part):
        for s in range(4, levels):
            part = cut(s, [part])
        return part

    def add_last(part):
        keep, got = part
        total = (order.tie(keep).astype(f32) + got.astype(f32)).astype(bf16)
        order.mark(total)
        return total

    def grow(level, cur, got):
        cur = merge(bits[level], order.tie(cur), got)
        order.mark(cur)
        return cur

    def first_sent(grads):
        send, keep = grads
        order.mark(send)
        return keep[None], exchange(send[None], dp, 0)

    def down_step(layer, dz, dz_got, dz_at):
        t = kept[layer]
        return first_sent(down_gradient(scalars, order.tie(t["a"]), t["a_got"], dz, dz_got, dz_at, chunk_rows))

    def back_step(layer, dz, dz_at, dr2):
        du, sent, bundle, dr2, small = layer_backward(
            layer, sec, dz, dz_at, dict(kept[layer], u=order.tie(kept[layer]["u"])), start_row, vec[layer], dr2, w)
        order.mark(dr2)
        return bundle, swap(bundle), dr2, small, du, swap(sent)

    def up_step(layer, back):
        t = kept[layer]
        return first_sent(up_gradient(scalars, order.tie(t["e"]), t["sent_got"], back[4], back[5], chunk_rows))

    def attn_grad_step(layer, attn):
        t = kept[layer]
        return first_sent(attn_gradient(scalars, order.tie(t["o"]), t["h"], t["sent_got"], attn[0], attn[1], attn[3],
                                        chunk_rows, extra))

    to_second = lambda t: lax.ppermute(t, "section", [(0, 1)])

    def hand_over(second, first):
        sent = jnp.where(on_first, second, first)
        own = jnp.where(on_first, first, second)
        return own, swap(sent)

    def both_parts(pair):
        own, got = pair
        cur = merge(sec, order.tie(own), got)
        order.mark(cur)
        cur = jnp.swapaxes(cur, 0, 1)
        for s in range(levels - 1, 3, -1):
            cur = grow(s, cur, exchange(cur, dp, s))
        return cur, exchange(cur, dp, 3)

    y_moved = to_second(y)
    back1 = back_step(1, dz1, 0, jnp.zeros((rows, half), f32))
    order.also(y_moved)
    down1 = down_step(1, dz1, dz1_got, 0)
    up1 = up_step(1, back1)
    square1 = attn_grad_step(1, back1)
    down0 = down_step(0, back1[0], back1[1], 4)
    down1 = cut(1, [down1])
    back0 = back_step(0, back1[0], 4, back1[2])
    dx0, dx_moved = (t[4 * rows:5 * rows] for t in back0[:2])
    up1 = cut(1, [up1])
    square1 = cut(1, [square1])
    down1 = cut(2, [down1])
    up0 = up_step(0, back0)
    square0 = attn_grad_step(0, back0)
    down0 = cut(1, [down0])
    up1 = cut(2, [up1])
    down1 = deep(cut(3, [down1]))
    square1 = cut(2, [square1])
    up1 = deep(cut(3, [up1]))
    up0 = cut(1, [up0])
    down0 = cut(2, [down0])
    down1 = add_last(down1)
    square1 = deep(cut(3, [square1]))
    up1 = add_last(up1)
    down0 = deep(cut(3, [down0]))
    square1 = add_last(square1)
    up0 = cut(2, [up0])
    down0 = add_last(down0)
    pair_d = hand_over(down1, down0)
    square0 = cut(1, [square0])
    up0 = deep(cut(3, [up0]))
    cur_d, got_d = both_parts(pair_d)
    square0 = cut(2, [square0])
    up0 = add_last(up0)
    pair_u = hand_over(up1, up0)
    cur_d = grow(3, cur_d, got_d)
    got_d = exchange(cur_d, dp, 2)
    square0 = deep(cut(3, [square0]))
    cur_u, got_u = both_parts(pair_u)
    cur_d = grow(2, cur_d, got_d)
    far_d = exchange(cur_d, dp, 1)
    side_d = exchange(cur_d, dp, 0)
    square0 = add_last(square0)
    b, e = square1, square0

    chunk = sum(bit[s] << (levels - 1 - s) for s in range(levels))
    at_row = lax.broadcasted_iota(jnp.int32, e.shape, 2)
    at_col = lax.broadcasted_iota(jnp.int32, e.shape, 3)
    share = vector_share(d, 2 * dp)
    matrix_rows = (at_row < chunk_rows) & (at_col < half) & (chunk >= 3 * dp // 4)
    vector_row = (at_row >= chunk_rows) & (chunk * share >= VBIAS * d) & (chunk * share < VBIAS * d + half)
    b = jnp.where(matrix_rows | (vector_row & on_first), e, b)
    pair_a = hand_over(b, e)

    cur_u = grow(3, cur_u, got_u)
    got_u = exchange(cur_u, dp, 2)
    cur_a, got_a = both_parts(pair_a)
    cur_u = grow(2, cur_u, got_u)
    far_u = exchange(cur_u, dp, 1)
    side_u = exchange(cur_u, dp, 0)
    cur_a = grow(3, cur_a, got_a)
    got_a = exchange(cur_a, dp, 2)
    order.also(far_d)
    last_d = exchange(order.tie(far_d), dp, 0)
    cur_a = grow(2, cur_a, got_a)
    far_a = exchange(cur_a, dp, 1)
    side_a = exchange(cur_a, dp, 0)
    order.also(far_u)
    last_u = exchange(order.tie(far_u), dp, 0)
    down_grad, = assemble(scalars, (order.tie(cur_d), far_d, side_d, last_d), chunk_rows, [(ff, d)],
                          lambda part, block, t: (part * 8 + block, 0), "assemble_down")
    order.mark(down_grad, far_a)
    last_a = exchange(far_a, dp, 0)
    up_grad, = assemble(scalars, (order.tie(cur_u), far_u, side_u, last_u), chunk_rows, [(d, ff)],
                        lambda part, block, t: (block % 4, part * 2 + block // 4), "assemble_up")
    order.mark(up_grad)
    out_grad, query_grad, key_grad, mixed_grad, vectors = assemble(
        scalars, (order.tie(cur_a), far_a, side_a, last_a), chunk_rows, [(d, d)] * 4,
        lambda part, block, t: (jnp.where(block // 2 == t, part * 2 + block % 2,
                                          jnp.where(block // 2 < t, jnp.maximum(part * 2 - 1, 0), part * 2 + 1)), 0),
        "assemble_attn", extra)
    total = vectors[:, :, :share].reshape(-1)[:VEC_ROWS * d].reshape(VEC_ROWS, d)

    spot_half = lambda t: jnp.where(on_first, t[:t.shape[0] // 2], t[t.shape[0] // 2:])
    block_ends = jnp.where(on_first, jnp.concatenate([dx0, dx_moved], axis=0),
                           jnp.concatenate([y_moved, y], axis=0))[None]
    return (
        block_ends,
        total[GAIN1][None],
        total[BIAS1][None],
        query_grad[None],
        total[QBIAS][None],
        key_grad[None],
        mixed_grad[None, :, half:],
        total[VBIAS, half:][None],
        spot_half(mixed_grad[:, :half]),
        spot_half(total[VBIAS, :half]),
        out_grad[None],
        total[OBIAS][None],
        total[GAIN2][None],
        total[BIAS2][None],
        up_grad[None],
        total[UBIAS:UBIAS + ff // d].reshape(1, ff),
        down_grad[None],
        total[DBIAS][None],
    )


def solution(mesh):
    stacked = P("section", None, None)
    vector = P("section", None)
    return jax.shard_map(
        local,
        mesh=mesh,
        in_specs=(
            P("section", "dp", None), P("dp", None),
            vector, vector, stacked, vector, stacked, stacked, vector, P(), P(),
            stacked, vector, vector, vector, stacked, vector, stacked, vector,
        ),
        out_specs=(
            P("section", "dp", None),
            vector, vector, stacked, vector, stacked, stacked, vector, P("section"), P("section"),
            stacked, vector, vector, vector, stacked, vector, stacked, vector,
        ),
        check_vma=False,
    )
```

```python
import functools

import jax
import jax.numpy as jnp
from jax import lax
from jax.experimental import pallas as pl
from jax.experimental.pallas import tpu as pltpu
from jax.sharding import PartitionSpec as P

HEADS = 12
HEAD = 64
PAIR = 2 * HEAD
VMEM_BYTES = 64 * 1024 * 1024

eps_norm = 1e-05
neg_fill = -1e30

f32 = jnp.float32
bf16 = jnp.bfloat16

NN = (((1,), (0,)), ((), ()))
NT = (((1,), (1,)), ((), ()))
TN = (((0,), (0,)), ((), ()))

ANY = pl.BlockSpec(memory_space=pl.ANY)
SMEM = pl.BlockSpec(memory_space=pltpu.SMEM)
VMEM = pl.BlockSpec(memory_space=pltpu.VMEM)

GAIN1, BIAS1, QBIAS, VBIAS, OBIAS, GAIN2, BIAS2, DBIAS, UBIAS = range(9)
VEC_ROWS = 16

SMALL_STEP = 8


def mm(left, right, dims=NN):
    return lax.dot_general(left, right, dims, preferred_element_type=f32)


def sds(shape, dtype):
    return jax.ShapeDtypeStruct(shape, dtype)


def params():
    return pltpu.CompilerParams(vmem_limit_bytes=VMEM_BYTES)


def cost(micros):
    return pl.CostEstimate(flops=int(micros * 1.15e9), bytes_accessed=1, transcendentals=0)


def start_fetch(mine, own, recv, dst, sem):
    @pl.when(mine)
    def _():
        pltpu.make_async_copy(own, dst, sem).start()

    @pl.when(jnp.logical_not(mine))
    def _():
        pltpu.make_async_copy(recv, dst, sem).start()


def wait_fetch(own, dst, sem):
    pltpu.make_async_copy(own, dst, sem).wait()


def norm_parts(rows):
    centre = jnp.mean(rows, axis=-1, keepdims=True)
    centred = rows - centre
    spread = jnp.mean(centred * centred, axis=-1, keepdims=True)
    factor = lax.rsqrt(spread + eps_norm)
    return centred * factor, factor


def norm_back(grad_t, n, w):
    return w * (
        grad_t
        - jnp.mean(grad_t, axis=-1, keepdims=True)
        - n * jnp.mean(grad_t * n, axis=-1, keepdims=True)
    )


def row_sum(x):
    return jnp.sum(x, axis=0, keepdims=True)


def attend(rows, q_s, k_s, v_s, o_s, lse_s, bias_s):
    lane = lax.broadcasted_iota(jnp.int32, (1, PAIR), 1)
    step = rows // 2

    def pair(hp, carry):
        ls = pl.ds(pl.multiple_of(hp * PAIR, PAIR), PAIR)
        q2 = q_s[:, ls] * jnp.asarray(HEAD ** -0.5, bf16)
        k2 = k_s[:, ls]
        v2 = v_s[:, ls]
        zero = jnp.zeros((), bf16)
        for qb in range(2):
            qr = slice(qb * step, (qb + 1) * step)
            keys = (qb + 1) * step
            mixed = None
            for j in range(2):
                inside = (lane >= j * HEAD) & (lane < (j + 1) * HEAD)
                kh = jnp.where(inside, k2[:keys], zero)
                vh = jnp.where(inside, v2[:keys], zero)
                s = mm(q2[qr], kh, NT) + bias_s[qr, :keys]
                peak = jnp.max(s, axis=-1, keepdims=True)
                p = jnp.exp(s - peak)
                total = jnp.sum(p, axis=-1, keepdims=True)
                low = (p * (1.0 / total)).astype(bf16)
                part = mm(low, vh)
                mixed = part if mixed is None else mixed + part
                lse_s[qr, :] = jnp.where(lane == 2 * hp + j, peak + jnp.log(total), lse_s[qr, :])
            o_s[qr, ls] = mixed.astype(bf16)
        return carry

    lse_s[...] = jnp.zeros(lse_s.shape, f32)
    lax.fori_loop(0, HEADS // 2, pair, 0)


def attn_forward_steps(layer, sec_ref, x_ref, r_ref, start_ref, vec_ref, weights, outs, held, in_sem, out_sem):
    (qw_o, qw_r, kw_o, kw_r, vw_o, vw_r, fw, ow_o, ow_r), (wq, wk, wv, wo) = weights
    h_out, q_out, k_out, v_out, o_out, m_out, e_out, lse_out, sent_out = outs
    h_s, q_s, k_s, v_s, o_s, m_s, e_s, lse_s, lset_s, bias_s = held
    mine = sec_ref[0] == layer
    rows = x_ref.shape[0]
    half = fw.shape[1]
    copies = []

    def fetch():
        start_fetch(mine, qw_o, qw_r, wq, in_sem.at[0])
        start_fetch(mine, kw_o, kw_r, wk, in_sem.at[1])
        start_fetch(mine, vw_o, vw_r, wv.at[:, half:], in_sem.at[2])
        if layer == 0:
            pltpu.make_async_copy(fw, wv.at[:, :half], in_sem.at[3]).start()
        start_fetch(mine, ow_o, ow_r, wo, in_sem.at[4])

    def put(src, dst):
        copy = pltpu.make_async_copy(src, dst, out_sem.at[len(copies)])
        copy.start()
        copies.append(copy)

    def run():
        wide = x_ref[...].astype(f32)
        n, _ = norm_parts(wide)
        h_s[...] = (n * vec_ref[GAIN1:GAIN1 + 1, :] + vec_ref[BIAS1:BIAS1 + 1, :]).astype(bf16)
        put(h_s, h_out)
        theirs = pl.ds(pl.multiple_of((1 - sec_ref[0]) * half, half), half)
        put(h_s.at[:, theirs], sent_out.at[0, :, half:])
        at_row = lax.broadcasted_iota(jnp.int32, (rows, rows), 0)
        at_col = lax.broadcasted_iota(jnp.int32, (rows, rows), 1)
        bias_s[...] = jnp.where((at_col <= at_row) & (at_col >= start_ref[...]), 0.0, neg_fill)
        wait_fetch(qw_o, wq, in_sem.at[0])
        q_s[...] = (mm(h_s[...], wq[...]) + vec_ref[QBIAS:QBIAS + 1, :]).astype(bf16)
        put(q_s, q_out)
        wait_fetch(kw_o, wk, in_sem.at[1])
        k_s[...] = mm(h_s[...], wk[...]).astype(bf16)
        put(k_s, k_out)
        wait_fetch(vw_o, wv.at[:, half:], in_sem.at[2])
        if layer == 0:
            wait_fetch(fw, wv.at[:, :half], in_sem.at[3])
            v_s[...] = (mm(h_s[...], wv[...]) + vec_ref[VBIAS:VBIAS + 1, :]).astype(bf16)
        else:
            v_s[:, :half] = r_ref[:, :half]
            v_s[:, half:] = (mm(h_s[...], wv[:, half:]) + vec_ref[VBIAS:VBIAS + 1, half:]).astype(bf16)
        put(v_s, v_out)
        attend(rows, q_s, k_s, v_s, o_s, lse_s, bias_s)
        put(o_s, o_out)
        put(o_s.at[:, theirs], sent_out.at[0, :, :half])
        lset_s[...] = jnp.transpose(lse_s[...])[:VEC_ROWS, :]
        put(lset_s, lse_out)
        wait_fetch(ow_o, wo, in_sem.at[4])
        m = x_ref[...].astype(f32) + (mm(o_s[...], wo[...]) + vec_ref[OBIAS:OBIAS + 1, :])
        m_s[...] = m
        put(m_s, m_out)
        n, _ = norm_parts(m)
        e_s[...] = (n * vec_ref[GAIN2:GAIN2 + 1, :] + vec_ref[BIAS2:BIAS2 + 1, :]).astype(bf16)
        put(e_s, e_out)
        put(e_s, sent_out.at[1])

    return fetch, run, copies


def attn_forward_kernel(layer, sec_ref, x_ref, r_ref, start_ref, vec_ref, *refs):
    fetch, run, copies = attn_forward_steps(
        layer, sec_ref, x_ref, r_ref, start_ref, vec_ref, (refs[:9], refs[18:22]), refs[9:18], refs[22:32],
        refs[32], refs[33])
    fetch()
    run()
    for copy in copies:
        copy.wait()


def attn_forward_shapes(rows, d):
    act = sds((rows, d), bf16)
    wbuf = pltpu.VMEM((d, d), bf16)
    abuf = pltpu.VMEM((rows, d), bf16)
    outs = [act, act, act, act, act, sds((rows, d), f32), act, sds((VEC_ROWS, rows), f32), sds((2, rows, d), bf16)]
    scratch = [wbuf, wbuf, wbuf, wbuf, abuf, abuf, abuf, abuf, abuf,
               pltpu.VMEM((rows, d), f32), abuf, pltpu.VMEM((rows, PAIR), f32),
               pltpu.VMEM((VEC_ROWS, rows), f32), pltpu.VMEM((rows, rows), f32),
               pltpu.SemaphoreType.DMA((5,)), pltpu.SemaphoreType.DMA((11,))]
    return outs, scratch


def attn_forward(layer, sec, x, r, start, vec, w):
    outs, scratch = attn_forward_shapes(*x.shape)
    return pl.pallas_call(
        functools.partial(attn_forward_kernel, layer),
        out_shape=outs,
        in_specs=[SMEM, VMEM, VMEM, VMEM, VMEM] + [ANY] * 9,
        out_specs=[ANY] * 9,
        scratch_shapes=scratch,
        compiler_params=params(),
        cost_estimate=cost(80),
        name="attn_forward",
    )(sec, x, r, start, vec, w["qo"], w["qr"], w["ko"], w["kr"], w["vo"], w["vr"], w["f"], w["oo"], w["or"])


def gelu(u):
    half_u = 0.5 * u
    return half_u + half_u * jnp.tanh(u * (0.7978845608028654 + 0.035677408136300125 * (u * u)))


def middle_kernel(blk, sec_ref, e_ref, m_ref, r_ref, start_ref, vec0_ref, vec1_ref, *refs):
    up_o, up_r, dn_o, dn_r = refs[:4]
    attn_w, outs = refs[4:13], refs[13:28]
    wu0, wd0, wu1, u_s, a_s, f_s, x_s, acc, up_sem, put_sem = refs[28:38]
    wbufs, held, in_sem, out_sem = refs[38:42], refs[42:52], refs[52], refs[53]
    u0_out, a0_out, x_out, u1_out, a1_out, sent_out = outs[:6]
    steps = wu0.shape[0]
    section = sec_ref[0]
    cols = [pl.ds(b * blk, blk) for b in range(steps)]
    for b in range(steps):
        start_fetch(section == 0, up_o.at[:, cols[b]], up_r.at[:, cols[b]], wu0.at[b], up_sem.at[0, b])
    for b in range(steps):
        start_fetch(section == 0, dn_o.at[cols[b], :], dn_r.at[cols[b], :], wd0.at[b], up_sem.at[1, b])
    fetch, run, copies = attn_forward_steps(
        1, sec_ref, x_s, r_ref, start_ref, vec1_ref, (attn_w, wbufs), outs[6:], held, in_sem, out_sem)
    fetch()
    for b in range(steps):
        start_fetch(section == 1, up_o.at[:, cols[b]], up_r.at[:, cols[b]], wu1.at[b], up_sem.at[2, b])
    own = []

    def put(src, dst):
        copy = pltpu.make_async_copy(src, dst, put_sem.at[len(own)])
        copy.start()
        own.append(copy)

    def expand(layer, b, source, weights, vec_ref):
        wait_fetch(up_o.at[:, cols[0]], weights.at[b], up_sem.at[2 * layer, b])
        f_s[b % 2] = mm(source[...], weights[b]) + vec_ref[UBIAS + b:UBIAS + b + 1, :]

    def activate(layer, b, u_out, a_out):
        u = f_s[b % 2]
        u_s[layer, b] = u.astype(bf16)
        a_s[layer, b] = gelu(u).astype(bf16)
        put(u_s.at[layer, b], u_out.at[:, cols[b]])
        put(a_s.at[layer, b], a_out.at[:, cols[b]])

    expand(0, 0, e_ref, wu0, vec0_ref)
    for b in range(steps):
        if b + 1 < steps:
            expand(0, b + 1, e_ref, wu0, vec0_ref)
        activate(0, b, u0_out, a0_out)
        wait_fetch(dn_o.at[cols[0], :], wd0.at[b], up_sem.at[1, b])
        part = mm(a_s[0, b], wd0[b])
        acc[...] = part if b == 0 else acc[...] + part
    x_s[...] = (m_ref[...] + (acc[...] + vec0_ref[DBIAS:DBIAS + 1, :])).astype(bf16)
    put(x_s, x_out)
    run()
    expand(1, 0, held[6], wu1, vec1_ref)
    for b in range(steps):
        if b + 1 < steps:
            expand(1, b + 1, held[6], wu1, vec1_ref)
        activate(1, b, u1_out, a1_out)
    theirs = (1 - section) * (steps // 2)
    for b in range(steps // 2):
        for layer in range(2):
            put(a_s.at[layer, theirs + b], sent_out.at[layer, :, cols[b]])
    for copy in own + copies:
        copy.wait()


def middle(sec, e, m, r, start, vec, w):
    rows, d = e.shape
    ff = w["uo"].shape[1]
    blk = d
    n = ff // blk
    outs, scratch = attn_forward_shapes(rows, d)
    wide = sds((rows, ff), bf16)
    return pl.pallas_call(
        functools.partial(middle_kernel, blk),
        out_shape=[wide, wide, sds((rows, d), bf16), wide, wide, sds((2, rows, ff // 2), bf16)] + outs,
        in_specs=[SMEM] + [VMEM] * 6 + [ANY] * 13,
        out_specs=[ANY] * 15,
        scratch_shapes=[pltpu.VMEM((n, d, blk), bf16), pltpu.VMEM((n, blk, d), bf16), pltpu.VMEM((n, d, blk), bf16),
                        pltpu.VMEM((2, n, rows, blk), bf16), pltpu.VMEM((2, n, rows, blk), bf16),
                        pltpu.VMEM((2, rows, blk), f32), pltpu.VMEM((rows, d), bf16), pltpu.VMEM((rows, d), f32),
                        pltpu.SemaphoreType.DMA((3, n)), pltpu.SemaphoreType.DMA((4 * n + 1 + n,))] + scratch,
        compiler_params=params(),
        cost_estimate=cost(80),
        name="middle",
    )(sec, e, m, r, start, vec[0], vec[1], w["uo"], w["ur"], w["do"], w["dr"],
      w["qo"], w["qr"], w["ko"], w["kr"], w["vo"], w["vr"], w["f"], w["oo"], w["or"])


def theirs_at(steps):
    half = steps // 2

    def index(j, s):
        return (0, jnp.where(s[0] == 0, jnp.maximum(j - half, 0), jnp.minimum(j, half - 1)))
    return index


def feed_down_kernel(layer, blk, sec_ref, a_ref, m_ref, vec_ref, dn_o, dn_r, z_ref, wd, acc, sem):
    j = pl.program_id(0)
    steps = pl.num_programs(0)
    mine = sec_ref[0] == layer

    @pl.when(j == 0)
    def _():
        for b in range(dn_o.shape[0] // blk):
            cols = pl.ds(b * blk, blk)
            start_fetch(mine, dn_o.at[cols, :], dn_r.at[cols, :], wd.at[b], sem.at[b])

    wait_fetch(dn_o.at[pl.ds(0, blk), :], wd.at[j], sem.at[j])
    part = mm(a_ref[...], wd[j])

    @pl.when(j == 0)
    def _():
        acc[...] = part

    @pl.when((j > 0) & (j < steps - 1))
    def _():
        acc[...] += part

    @pl.when(j == steps - 1)
    def _():
        z_ref[...] = (m_ref[...] + (acc[...] + part + vec_ref[DBIAS:DBIAS + 1, :])).astype(bf16)


def feed_down(layer, sec, a, m, vec, w):
    rows, ff = a.shape
    d = m.shape[1]
    blk = d
    n = ff // blk
    return pl.pallas_call(
        functools.partial(feed_down_kernel, layer, blk),
        grid=(n,),
        out_shape=sds((rows, d), bf16),
        in_specs=[SMEM, pl.BlockSpec((rows, blk), lambda j: (0, j)), VMEM, VMEM, ANY, ANY],
        out_specs=pl.BlockSpec((rows, d), lambda j: (0, 0)),
        scratch_shapes=[pltpu.VMEM((n, blk, d), bf16), pltpu.VMEM((rows, d), f32), pltpu.SemaphoreType.DMA((n,))],
        compiler_params=params(),
        cost_estimate=cost(80),
        name="feed_down",
    )(sec, a, m, vec, w["do"], w["dr"])


def layer_backward_kernel(layer, blk, sec_ref, dz_ref, m_ref, lse_ref, start_ref, vec_ref, dr2_ref,
                          u_in, x_in, q_in, k_in, v_in, o_in,
                          up_o, up_r, dn_o, dn_r, qw_o, qw_r, kw_o, kw_r, vw_o, vw_r, fw, ow_o, ow_r,
                          du_out, sent_out, bundle_out, shared_ref, small_ref,
                          wu, wd, wq, wk, wv, wo, u_s, x_s, q_ref, k_ref, v_ref, o_ref, du_s, da_s, acc, dm_s,
                          bundle_ref, do_s, delta_s, bias_s, feed_sem, sem, in_sem, out_sem):
    mine = sec_ref[0] == layer
    rows, d = dz_ref.shape
    half = fw.shape[1]
    steps = wu.shape[0]
    cols = [pl.ds(b * blk, blk) for b in range(steps)]
    for b in range(steps):
        start_fetch(mine, dn_o.at[cols[b], :], dn_r.at[cols[b], :], wd.at[b], feed_sem.at[0, b])
        pltpu.make_async_copy(u_in.at[:, cols[b]], u_s.at[b], feed_sem.at[2, b]).start()
        start_fetch(mine, up_o.at[:, cols[b]], up_r.at[:, cols[b]], wu.at[b], feed_sem.at[1, b])
    start_fetch(mine, ow_o, ow_r, wo, sem.at[4])
    loads = [pltpu.make_async_copy(src, dst, in_sem.at[i]) for i, (src, dst) in enumerate(
        ((q_in, q_ref), (k_in, k_ref), (v_in, v_ref), (o_in, o_ref), (x_in, x_s)))]
    for load in loads:
        load.start()
    start_fetch(mine, qw_o, qw_r, wq, sem.at[0])
    start_fetch(mine, kw_o, kw_r, wk, sem.at[1])
    start_fetch(mine, vw_o, vw_r, wv.at[:, half:], sem.at[2])
    if layer == 0:
        pltpu.make_async_copy(fw, wv.at[:, :half], sem.at[3]).start()
    copies = []

    def put(src, dst):
        copy = pltpu.make_async_copy(src, dst, out_sem.at[len(copies)])
        copy.start()
        copies.append(copy)

    small_ref[...] = jnp.zeros(small_ref.shape, f32)

    def expand(b):
        wait_fetch(dn_o.at[cols[0], :], wd.at[b], feed_sem.at[0, b])
        da_s[b % 2] = mm(dz_ref[...], wd[b], NT)

    def activate(b):
        pltpu.make_async_copy(u_in.at[:, cols[b]], u_s.at[b], feed_sem.at[2, b]).wait()
        u = u_s[b].astype(f32)
        sq = u * u
        th = jnp.tanh(u * (0.7978845608028654 + 0.035677408136300125 * sq))
        slope = 0.5 + 0.5 * th + (0.5 * u) * (1.0 - th * th) * (0.7978845608028654 + 0.10703222440890037 * sq)
        du = (slope * da_s[b % 2]).astype(bf16)
        du_s[b] = du
        small_ref[UBIAS + b:UBIAS + b + 1, :] = row_sum(du.astype(f32))
        put(du_s.at[b], du_out.at[:, cols[b]])

    expand(0)
    for b in range(steps):
        if b + 1 < steps:
            expand(b + 1)
        activate(b)
        wait_fetch(up_o.at[:, cols[0]], wu.at[b], feed_sem.at[1, b])
        part = mm(du_s[b], wu[b], NT)
        acc[...] = part if b == 0 else acc[...] + part
    theirs = (1 - sec_ref[0]) * (steps // 2)
    for b in range(steps // 2):
        put(du_s.at[theirs + b], sent_out.at[b])
    de = acc[...]
    n, w = norm_parts(m_ref[...])
    dz = dz_ref[...].astype(f32)
    dm_s[...] = dz + norm_back(de * vec_ref[GAIN2:GAIN2 + 1, :], n, w)
    small_ref[GAIN2:GAIN2 + 1, :] = row_sum(de * n)
    small_ref[BIAS2:BIAS2 + 1, :] = row_sum(de)
    small_ref[DBIAS:DBIAS + 1, :] = row_sum(dz)

    low_ref, dq_ref, dk_ref, dv_ref, dx_ref = (bundle_ref.at[pl.ds(i * rows, rows), :] for i in range(5))
    low_ref[...] = dm_s[...].astype(bf16)
    at_key = lax.broadcasted_iota(jnp.int32, (rows, rows), 0)
    at_query = lax.broadcasted_iota(jnp.int32, (rows, rows), 1)
    bias_s[...] = jnp.where((at_key <= at_query) & (at_key >= start_ref[...]), 0.0, neg_fill)
    wait_fetch(ow_o, wo, sem.at[4])
    do = mm(low_ref[...], wo[...], NT).astype(bf16)
    do_s[...] = do
    for load in loads:
        load.wait()
    head_row = lax.broadcasted_iota(jnp.int32, (VEC_ROWS, d), 0)
    head_col = lax.broadcasted_iota(jnp.int32, (VEC_ROWS, d), 1) // HEAD
    pick = (head_row == head_col).astype(f32)
    delta_s[...] = lax.dot_general(pick, do.astype(f32) * o_ref[...].astype(f32), NT,
                                   precision=lax.Precision.HIGHEST, preferred_element_type=f32)
    lane = lax.broadcasted_iota(jnp.int32, (1, PAIR), 1)
    step = rows // 2
    scale = HEAD ** -0.5
    zero = jnp.zeros((), bf16)

    def pair(hp, carry):
        ls = pl.ds(pl.multiple_of(hp * PAIR, PAIR), PAIR)
        q2 = q_ref[:, ls] * jnp.asarray(scale, bf16)
        k2 = k_ref[:, ls]
        v2 = v_ref[:, ls]
        do2 = do_s[:, ls]
        dq_parts = []
        for kb in range(2):
            kr = slice(kb * step, (kb + 1) * step)
            first = kb * step
            dk = dv = dq = None
            for j in range(2):
                inside = (lane >= j * HEAD) & (lane < (j + 1) * HEAD)
                kh = jnp.where(inside, k2[kr], zero)
                vh = jnp.where(inside, v2[kr], zero)
                qh = jnp.where(inside, q2[first:], zero)
                doh = jnp.where(inside, do2[first:], zero)
                row = pl.ds(2 * hp + j, 1)
                st = mm(kh, qh, NT) + bias_s[kr, first:]
                pt = jnp.exp(st - lse_ref[row, first:])
                dpt = mm(vh, doh, NT)
                dst = (pt * (dpt - delta_s[row, first:])).astype(bf16)
                dv_j = mm(pt.astype(bf16), doh)
                dk_j = mm(dst, qh)
                dq_j = mm(dst, kh, TN)
                dk = dk_j if dk is None else dk + dk_j
                dv = dv_j if dv is None else dv + dv_j
                dq = dq_j if dq is None else dq + dq_j
            dk_ref[kr, ls] = dk.astype(bf16)
            if layer == 1:
                dv_ref[kr, ls] = dv.astype(bf16)

                @pl.when(hp < HEADS // 4)
                def _():
                    shared_ref[kr, ls] = dv
            else:
                extra = jnp.where(hp < HEADS // 4, dr2_ref[kr, pl.ds(pl.multiple_of((hp % (HEADS // 4)) * PAIR, PAIR), PAIR)], 0.0)
                dv_ref[kr, ls] = (dv + extra).astype(bf16)
            dq_parts.append(dq)
        dq_ref[:step, ls] = (dq_parts[0][:step] * scale).astype(bf16)
        dq_ref[step:, ls] = ((dq_parts[0][step:] + dq_parts[1]) * scale).astype(bf16)
        return carry

    if layer == 0:
        shared_ref[...] = jnp.zeros(shared_ref.shape, f32)
    lax.fori_loop(0, HEADS // 2, pair, 0)
    put(bundle_ref.at[pl.ds(0, 4 * rows), :], bundle_out.at[pl.ds(0, 4 * rows), :])

    wait_fetch(qw_o, wq, sem.at[0])
    dh = mm(dq_ref[...], wq[...], NT)
    wait_fetch(kw_o, wk, sem.at[1])
    dh = dh + mm(dk_ref[...], wk[...], NT)
    wait_fetch(vw_o, wv.at[:, half:], sem.at[2])
    if layer == 0:
        wait_fetch(fw, wv.at[:, :half], sem.at[3])
        dh = dh + mm(dv_ref[...], wv[...], NT)
    else:
        dh = dh + mm(dv_ref[:, half:], wv[:, half:], NT)
    n, w = norm_parts(x_s[...].astype(f32))
    dx_ref[...] = (dm_s[...] + norm_back(dh * vec_ref[GAIN1:GAIN1 + 1, :], n, w)).astype(bf16)
    small_ref[GAIN1:GAIN1 + 1, :] = row_sum(dh * n)
    small_ref[BIAS1:BIAS1 + 1, :] = row_sum(dh)
    small_ref[QBIAS:QBIAS + 1, :] = row_sum(dq_ref[...].astype(f32))
    small_ref[VBIAS:VBIAS + 1, :] = row_sum(dv_ref[...].astype(f32))
    small_ref[OBIAS:OBIAS + 1, :] = row_sum(low_ref[...].astype(f32))
    bundle_ref[5 * rows:, :] = small_ref[...].astype(bf16)
    put(bundle_ref.at[pl.ds(4 * rows, rows + VEC_ROWS), :], bundle_out.at[pl.ds(4 * rows, rows + VEC_ROWS), :])
    for copy in copies:
        copy.wait()


def layer_backward(layer, sec, dz, dz_at, t, start_row, vec, dr2, w):
    rows, ff = t["u"].shape
    d = t["m"].shape[1]
    half = w["f"].shape[1]
    blk = d
    n = ff // blk
    wbuf = pltpu.VMEM((d, d), bf16)
    act = pltpu.VMEM((rows, d), bf16)
    wide = pltpu.VMEM((rows, d), f32)
    blocks = pltpu.VMEM((n, rows, blk), bf16)
    dma = pltpu.SemaphoreType.DMA
    bundle = (5 * rows + VEC_ROWS, d)
    return pl.pallas_call(
        functools.partial(layer_backward_kernel, layer, blk),
        grid=(1,),
        out_shape=[sds((rows, ff), bf16), sds((n // 2, rows, blk), bf16), sds(bundle, bf16), sds((rows, half), f32),
                   sds((VEC_ROWS, d), f32)],
        in_specs=[SMEM, pl.BlockSpec((rows, d), lambda i: (dz_at, 0))] + [VMEM] * 5 + [ANY] * 19,
        out_specs=[ANY] * 3 + [VMEM] * 2,
        scratch_shapes=[pltpu.VMEM((n, d, blk), bf16), pltpu.VMEM((n, blk, d), bf16), wbuf, wbuf, wbuf, wbuf,
                        blocks, act, act, act, act, act, blocks, pltpu.VMEM((2, rows, blk), f32), wide, wide,
                        pltpu.VMEM(bundle, bf16), act, pltpu.VMEM((VEC_ROWS, rows), f32), pltpu.VMEM((rows, rows), f32),
                        dma((3, n)), dma((5,)), dma((5,)), dma((n + n // 2 + 2,))],
        compiler_params=params(),
        cost_estimate=cost(80),
        name="layer_backward",
    )(sec, dz, t["m"], t["lse"], start_row, vec, dr2, t["u"], t["x"], t["q"], t["k"], t["v"], t["o"],
      w["uo"], w["ur"], w["do"], w["dr"],
      w["qo"], w["qr"], w["ko"], w["kr"], w["vo"], w["vr"], w["f"], w["oo"], w["or"])


def store_chunks(ref, value):
    c, r, _ = ref.shape
    for i in range(c):
        ref[i] = value[i * r:(i + 1) * r].astype(bf16)


def quarter_of(g, s):
    return 2 * jnp.where(g < 2, 1 - s[1], s[1]) + g % 2


def quarters(kernel, scalars, in_specs, operands, shape, name):
    per = shape[0] // 2
    return pl.pallas_call(
        kernel,
        grid_spec=pltpu.PrefetchScalarGridSpec(
            num_scalar_prefetch=1, grid=(4,), in_specs=in_specs,
            out_specs=[pl.BlockSpec((per,) + shape[1:], lambda g, s: (jnp.minimum(g, 1), 0, 0)),
                       pl.BlockSpec((per,) + shape[1:], lambda g, s: (jnp.maximum(g - 2, 0), 0, 0))]),
        out_shape=[sds(shape, bf16)] * 2,
        compiler_params=params(),
        cost_estimate=cost(80),
        name=name,
    )(scalars, *operands)


def store_quarter(send_ref, keep_ref, value):
    g = pl.program_id(0)

    @pl.when(g < 2)
    def _():
        store_chunks(send_ref, value)

    @pl.when(g >= 2)
    def _():
        store_chunks(keep_ref, value)


def down_gradient(scalars, a, a_got, dz, dz_got, dz_at, chunk_rows):
    a_got, a_at = a_got
    rows, ff = a.shape
    d = dz.shape[1]
    q = d // 2

    def kernel(s_ref, a_ref, b_ref, x_ref, y_ref, send_ref, keep_ref):
        store_quarter(send_ref, keep_ref, mm(a_ref[...], x_ref[...], TN) + mm(b_ref[0], y_ref[...], TN))

    whole = pl.BlockSpec((rows, d), lambda g, s: (dz_at, 0))
    return quarters(
        kernel, scalars,
        [pl.BlockSpec((rows, q), lambda g, s: (0, 4 * s[0] + quarter_of(g, s))),
         pl.BlockSpec((1, rows, q), lambda g, s: (a_at, 0, quarter_of(g, s))), whole, whole],
        (a, a_got, dz, dz_got), (2 * q // chunk_rows, chunk_rows, d), "down_gradient")


def up_gradient(scalars, e, sent_got, du, du_got, chunk_rows):
    rows, ff = du.shape
    d = e.shape[1]
    q = d // 2

    def kernel(s_ref, e_ref, f_ref, du_ref, dg_ref, send_ref, keep_ref):
        store_quarter(send_ref, keep_ref, mm(e_ref[...], du_ref[...], TN) + mm(f_ref[0], dg_ref[0], TN))

    return quarters(
        kernel, scalars,
        [pl.BlockSpec((rows, q), lambda g, s: (0, g % 2)),
         pl.BlockSpec((1, rows, q), lambda g, s: (1, 0, g % 2)),
         pl.BlockSpec((rows, d), lambda g, s: (0, 2 * s[0] + quarter_of(g, s) // 2)),
         pl.BlockSpec((1, rows, d), lambda g, s: (quarter_of(g, s) // 2, 0, 0))],
        (e, sent_got, du, du_got), (2 * q // chunk_rows, chunk_rows, d), "up_gradient")


def vector_share(width, chunks):
    return max(PAIR, VEC_ROWS * width // chunks)


def attn_gradient(scalars, o, h, sent_got, bundle, bundle_got, small, chunk_rows, extra):
    rows, d = o.shape
    q = d // 2
    per = q // chunk_rows
    share = vector_share(d, 8 * per)

    def kernel(s_ref, o_ref, h_ref, l_ref, own_ref, got_ref, small_ref, small_got_ref, send_ref, keep_ref, sum_ref):
        sum_ref[...] = small_ref[...] + small_got_ref[...].astype(f32)
        g = pl.program_id(0)
        which = quarter_of(g, s_ref)
        for i in range(4):
            @pl.when(which == i)
            def _():
                left = o_ref if i == 0 else h_ref
                value = mm(left[...], own_ref[...], TN) + mm(l_ref[0], got_ref[...], TN)
                for side, ref in enumerate((send_ref, keep_ref)):
                    @pl.when(g // 2 == side)
                    def _():
                        ref[:, chunk_rows:, :] = jnp.zeros((per, extra, d), bf16)
                        for c in range(per):
                            ref[c, :chunk_rows, :] = value[c * chunk_rows:(c + 1) * chunk_rows].astype(bf16)
                        for part_index in range(2):
                            @pl.when(s_ref[0] == part_index)
                            def _():
                                for c in range(per):
                                    at = ((4 * part_index + i) * per + c) * share
                                    if at < VEC_ROWS * d:
                                        row = sum_ref[at // d:at // d + 1, at % d:at % d + share]
                                        ref[c, chunk_rows:chunk_rows + 1, :share] = row.astype(bf16)

    part = pl.BlockSpec((rows, q), lambda g, s: (0, s[0]))
    right = pl.BlockSpec((rows, d), lambda g, s: (quarter_of(g, s), 0))
    shape = (2 * per, chunk_rows + extra, d)
    return pl.pallas_call(
        kernel,
        grid_spec=pltpu.PrefetchScalarGridSpec(
            num_scalar_prefetch=1, grid=(4,),
            in_specs=[part, part,
                      pl.BlockSpec((1, rows, q), lambda g, s: (0, 0, jnp.minimum(quarter_of(g, s), 1))),
                      right, right, pl.BlockSpec((VEC_ROWS, d), lambda g, s: (0, 0)),
                      pl.BlockSpec((VEC_ROWS, d), lambda g, s: (5 * rows // VEC_ROWS, 0))],
            out_specs=[pl.BlockSpec((per,) + shape[1:], lambda g, s: (jnp.minimum(g, 1), 0, 0)),
                       pl.BlockSpec((per,) + shape[1:], lambda g, s: (jnp.maximum(g - 2, 0), 0, 0))],
            scratch_shapes=[pltpu.VMEM((VEC_ROWS, d), f32)]),
        out_shape=[sds(shape, bf16)] * 2,
        compiler_params=params(),
        cost_estimate=cost(80),
        name="attn_gradient",
    )(scalars, o, h, sent_got, bundle, bundle_got, small, bundle_got)


AXES = ("section", "dp")
SWAP = [(0, 1), (1, 0)]


def bit_orders(dp):
    bits = list(range(dp.bit_length() - 1))
    return bits, [1, 0] + bits[2:]


def exchange(array, dp, step):
    first, second = bit_orders(dp)
    pairs = [(i, i ^ (1 << first[step])) for i in range(dp)]
    pairs += [(dp + i, dp + (i ^ (1 << second[step]))) for i in range(dp)]
    return lax.ppermute(array, AXES, pairs)


def block_of(chunks, rows):
    best = 1
    for c in range(1, chunks + 1):
        if chunks % c == 0 and c * rows <= 768:
            best = c
    return best


def add_split(bit, parts):
    _, c, r, w = parts[0][0].shape
    counts = [p[0].shape[0] for p in parts]
    n = sum(counts)
    h = c // 2
    cb = block_of(h, r)
    nb = h // cb
    ends = [sum(counts[:i + 1]) for i in range(len(counts))]
    begins = [e - k for e, k in zip(ends, counts)]

    def kernel(s_ref, *refs):
        send_ref, keep_ref = refs[-2:]
        g, i = pl.program_id(0), pl.program_id(1)
        for t in range(len(parts)):
            @pl.when((i >= begins[t]) & (i < ends[t]))
            def _():
                total = (refs[2 * t][...].astype(f32) + refs[2 * t + 1][...].astype(f32)).astype(bf16)

                @pl.when(g == 0)
                def _():
                    send_ref[...] = total

                @pl.when(g == 1)
                def _():
                    keep_ref[...] = total

    def source(t):
        def index(g, i, j, s):
            inside = (i >= begins[t]) & (i < ends[t])
            side = jnp.where(g == 0, 1 - s[0], s[0])
            return (jnp.clip(i - begins[t], 0, counts[t] - 1), jnp.where(inside, side * nb + j, 0), 0, 0)
        return pl.BlockSpec((1, cb, r, w), index)

    def send_at(g, i, j, s):
        return (jnp.where(g == 0, i, n - 1), jnp.where(g == 0, j, nb - 1), 0, 0)

    def keep_at(g, i, j, s):
        return (jnp.where(g == 0, 0, i), jnp.where(g == 0, 0, j), 0, 0)

    flat = [x for p in parts for x in p]
    return pl.pallas_call(
        kernel,
        grid_spec=pltpu.PrefetchScalarGridSpec(
            num_scalar_prefetch=1, grid=(2, n, nb),
            in_specs=[source(t) for t in range(len(parts)) for _ in range(2)],
            out_specs=[pl.BlockSpec((1, cb, r, w), send_at), pl.BlockSpec((1, cb, r, w), keep_at)]),
        out_shape=[sds((n, h, r, w), bf16)] * 2,
        compiler_params=params(),
        cost_estimate=cost(SMALL_STEP),
        name="add_split",
    )(bit, *flat)


def merge(bit, cur, arrived):
    n, c, r, w = cur.shape
    cb = block_of(c, r)
    nb = c // cb

    def kernel(s_ref, a_ref, b_ref, out_ref):
        g = pl.program_id(1)

        @pl.when(g == s_ref[0])
        def _():
            out_ref[...] = a_ref[...]

        @pl.when(g != s_ref[0])
        def _():
            out_ref[...] = b_ref[...]

    def at(own):
        def index(i, g, j, s):
            mine = (g == s[0]) if own else (g != s[0])
            return (i, jnp.where(mine, j, 0), 0, 0)
        return pl.BlockSpec((1, cb, r, w), index)

    return pl.pallas_call(
        kernel,
        grid_spec=pltpu.PrefetchScalarGridSpec(
            num_scalar_prefetch=1, grid=(n, 2, nb), in_specs=[at(True), at(False)],
            out_specs=pl.BlockSpec((1, cb, r, w), lambda i, g, j, s: (i, g * nb + j, 0, 0))),
        out_shape=sds((n, 2 * c, r, w), bf16),
        compiler_params=params(),
        cost_estimate=cost(SMALL_STEP),
        name="merge",
    )(bit, cur, arrived)


def assemble(scalars, sources, chunk_rows, out_shapes, targets, name, finish=None, extra_specs=()):
    _, c, r, w = sources[0].shape
    cb = c // 2
    block = cb * chunk_rows

    def kernel(s_ref, *refs):
        ins, outs = refs[:4], refs[4:4 + len(out_shapes)]
        held, wide, in_sem, out_sem = refs[4 + len(out_shapes):]
        loads = [pltpu.make_async_copy(ins[i], held.at[i], in_sem.at[i]) for i in range(4)]
        for load in loads:
            load.start()
        for load in loads:
            load.wait()

        def chunks(part, t):
            own = s_ref[0] == part
            top, mid, low = t // 4, (t // 2) % 2, t % 2
            first = jnp.where(own, top, mid)
            second = jnp.where(own, mid, top)
            which = 2 * jnp.where(first == s_ref[1], 0, 1) + jnp.where(low == s_ref[2], 0, 1)
            return held.at[which, part, pl.ds(second * cb, cb)]

        copies = []
        for part in range(2):
            for t in range(8):
                at = part * 8 + t
                rows = chunks(part, t)
                for i in range(cb):
                    wide[at, i * chunk_rows:(i + 1) * chunk_rows, :] = rows[i, :chunk_rows, :].astype(f32)
                for source, target in targets(outs, part, t):
                    copy = pltpu.make_async_copy(wide.at[at, :, source], target, out_sem.at[len(copies)])
                    copy.start()
                    copies.append(copy)
        if finish is not None:
            finish(s_ref, chunks, wide, outs)
        for copy in copies:
            copy.wait()

    out_specs = [ANY] * (len(out_shapes) - len(extra_specs)) + list(extra_specs)
    return pl.pallas_call(
        kernel,
        out_shape=[sds(o, f32) for o in out_shapes],
        in_specs=[SMEM] + [ANY] * 4,
        out_specs=out_specs,
        scratch_shapes=[pltpu.VMEM((4, 2, c, r, w), bf16), pltpu.VMEM((16, block, w), f32),
                        pltpu.SemaphoreType.DMA((4,)), pltpu.SemaphoreType.DMA((20,))],
        compiler_params=params(),
        cost_estimate=cost(16),
        name=name,
    )(scalars, *sources)


def after(array, *earlier):
    return lax.optimization_barrier((array,) + earlier)[0]


class Order:
    def __init__(self):
        self.last = ()

    def mark(self, *arrays):
        self.last = arrays

    def also(self, *arrays):
        self.last = self.last + arrays

    def tie(self, array):
        return after(array, *self.last) if self.last else array


def local(
    boundary,
    lengths,
    norm_one_gain,
    norm_one_bias,
    query_weight,
    query_bias,
    key_weight,
    value_weight,
    value_bias,
    first_value_weight,
    first_value_bias,
    out_weight,
    out_bias,
    norm_two_gain,
    norm_two_bias,
    up_weight,
    up_bias,
    down_weight,
    down_bias,
):
    section = lax.axis_index("section")
    spot = lax.axis_index("dp")
    dp = lax.axis_size("dp")
    on_first = section == 0
    sec = jnp.reshape(section, (1,)).astype(jnp.int32)
    rows = boundary.shape[1] // 2
    d = boundary.shape[2]
    half = value_weight.shape[2]
    ff = up_weight.shape[2]

    def swap(array):
        return lax.ppermute(array, "section", SWAP)

    def row(vector):
        return jnp.reshape(vector, (-1, d))

    vec_own = jnp.concatenate([
        norm_one_gain, norm_one_bias, query_bias,
        jnp.concatenate([first_value_bias[None], value_bias], axis=1),
        out_bias, norm_two_gain, norm_two_bias, down_bias, row(up_bias)], axis=0)
    vec_own = jnp.pad(vec_own, ((0, VEC_ROWS - vec_own.shape[0]), (0, 0)))
    top, bottom = boundary[0, :rows], boundary[0, rows:]
    arrived_rows = swap(jnp.where(on_first, bottom, top))
    kept_rows = jnp.where(on_first, top, bottom)
    x0 = jnp.where(on_first, kept_rows, arrived_rows)
    dz1 = jnp.where(on_first, arrived_rows, kept_rows)
    dz1_moved = lax.ppermute(bottom, "section", [(1, 0)])
    dz1_got = jnp.where(on_first, dz1_moved, top)
    vec_arrived = swap(vec_own)
    vec = (jnp.where(on_first, vec_own, vec_arrived), jnp.where(on_first, vec_arrived, vec_own))
    w = {"qo": query_weight[0], "ko": key_weight[0], "vo": value_weight[0], "oo": out_weight[0],
         "uo": up_weight[0], "do": down_weight[0], "f": first_value_weight}
    for name in "qkvo":
        w[name + "r"] = swap(w[name + "o"])
    w["ur"] = swap(after(w["uo"], w["qr"]))
    w["dr"] = swap(after(w["do"], w["kr"]))

    own_lengths = jnp.where(on_first, lengths[0], lengths[1])
    cuts = jnp.cumsum(own_lengths)
    at = jnp.arange(rows, dtype=jnp.int32)
    start = jnp.max(jnp.where(at[:, None] >= cuts[None, :], cuts[None, :], 0), axis=1).astype(jnp.int32)
    start_col, start_row = start[:, None], start[None, :]

    chunk_rows = ff // (2 * dp)
    extra = 16
    first_bits, second_bits = bit_orders(dp)
    levels = len(first_bits)
    bit = [((spot >> jnp.where(on_first, first_bits[s], second_bits[s])) & 1).astype(jnp.int32) for s in range(levels)]
    bits = [jnp.reshape(b, (1,)) for b in bit]
    scalars = jnp.stack([sec[0], bit[0], bit[2]])
    order = Order()

    h, q, k, v, o, m, e, lse, sent = attn_forward(0, sec, x0, x0, start_col, vec[0], w)
    kept = [dict(x=x0, h=h, q=q, k=k, v=v, o=o, m=m, e=e, lse=lse, sent_got=swap(sent))]
    u0, a0, x1, u1, a1, a_sent, h, q, k, v, o, m, e, lse, sent = middle(sec, e, m, v, start_col, vec, w)
    a_got = swap(a_sent)
    kept[0].update(u=u0, a=a0, a_got=(a_got, 0))
    kept.append(dict(x=x1, h=h, q=q, k=k, v=v, o=o, m=m, e=e, lse=lse, u=u1, a=a1, sent_got=swap(sent), a_got=(a_got, 1)))
    order.mark(x1)
    order.mark(x1)

    def cut(level, parts):
        (first_keep, first_got), *rest = parts
        send, keep = add_split(bits[level], [(order.tie(first_keep), first_got)] + rest)
        order.mark(send)
        return keep, exchange(send, dp, level)

    def deep(part):
        for s in range(4, levels):
            part = cut(s, [part])
        return part

    def grow(level, cur, got):
        cur = merge(bits[level], order.tie(cur), got)
        order.mark(cur)
        return cur

    def first_sent(grads):
        send, keep = grads
        order.mark(send)
        return keep[None], exchange(send[None], dp, 0)

    def down_step(layer, dz, dz_got, dz_at):
        t = kept[layer]
        return first_sent(down_gradient(scalars, order.tie(t["a"]), t["a_got"], dz, dz_got, dz_at, chunk_rows))

    def back_step(layer, dz, dz_at, dr2):
        du, sent, bundle, dr2, small = layer_backward(
            layer, sec, dz, dz_at, dict(kept[layer], u=order.tie(kept[layer]["u"])), start_row, vec[layer], dr2, w)
        order.mark(bundle)
        return bundle, swap(bundle), dr2, small, du, swap(sent)

    def up_step(layer, back):
        t = kept[layer]
        return first_sent(up_gradient(scalars, order.tie(t["e"]), t["sent_got"], back[4], back[5], chunk_rows))

    def attn_grad_step(layer, attn):
        t = kept[layer]
        return first_sent(attn_gradient(scalars, order.tie(t["o"]), t["h"], t["sent_got"], attn[0], attn[1], attn[3],
                                        chunk_rows, extra))

    to_second = lambda t: lax.ppermute(t, "section", [(0, 1)])

    def summed(part, i):
        keep, got = part
        return (keep[i:i + 1].astype(f32) + got[i:i + 1].astype(f32)).astype(bf16)

    def hand_over(second, first):
        own = order.tie(jnp.where(on_first, first, second))
        sent = jnp.where(on_first, second, first)
        order.mark(sent)
        return own, swap(sent)

    def both_parts(pair):
        own, got = pair
        cur = merge(sec, order.tie(own), got)
        order.mark(cur)
        cur = jnp.swapaxes(cur, 0, 1)
        for s in range(levels - 1, 3, -1):
            cur = grow(s, cur, exchange(cur, dp, s))
        return cur, exchange(cur, dp, 3)

    back1 = back_step(1, dz1, 0, jnp.zeros((rows, half), f32))
    order.also(kept[0]["sent_got"], kept[1]["sent_got"])
    down1 = down_step(1, dz1, dz1_got, 0)
    up1 = up_step(1, back1)
    square1 = attn_grad_step(1, back1)
    down0 = down_step(0, back1[0], back1[1], 4)
    down1 = cut(1, [down1])
    back0 = back_step(0, back1[0], 4, back1[2])
    dx0, dx_moved = (t[4 * rows:5 * rows] for t in back0[:2])
    up1 = cut(1, [up1])
    square1 = cut(1, [square1])
    down0 = cut(1, [down0])
    up0 = up_step(0, back0)
    feed = cut(2, [down1, up1, down0])
    square0 = attn_grad_step(0, back0)
    square1 = cut(2, [square1])
    up0 = cut(1, [up0])
    feed = deep(cut(3, [feed]))
    square1 = deep(cut(3, [square1]))
    up0 = cut(2, [up0])
    square0 = cut(1, [square0])
    up0 = deep(cut(3, [up0]))
    square0 = cut(2, [square0])
    pair_d = hand_over(summed(feed, 0), summed(feed, 2))
    order.also(square1[1])
    square0 = deep(cut(3, [square0]))
    cur_d, got_d = both_parts(pair_d)
    pair_u = hand_over(summed(feed, 1), summed(up0, 0))
    b, e = summed(square1, 0), summed(square0, 0)

    chunk = sum(bit[s] << (levels - 1 - s) for s in range(levels))
    at_row = lax.broadcasted_iota(jnp.int32, e.shape, 2)
    at_col = lax.broadcasted_iota(jnp.int32, e.shape, 3)
    share = vector_share(d, 2 * dp)
    matrix_rows = (at_row < chunk_rows) & (at_col < half) & (chunk >= 3 * dp // 4)
    vector_row = (at_row >= chunk_rows) & (chunk * share >= VBIAS * d) & (chunk * share < VBIAS * d + half)
    b = jnp.where(matrix_rows | (vector_row & on_first), e, b)
    pair_a = hand_over(b, e)

    cur_d = grow(3, cur_d, got_d)
    got_d = exchange(cur_d, dp, 1)
    cur_u, got_u = both_parts(pair_u)
    cur_d = grow(1, cur_d, got_d)
    far_d = exchange(cur_d, dp, 2)
    side_d = exchange(cur_d, dp, 0)
    cur_a, got_a = both_parts(pair_a)
    cur_u = grow(3, cur_u, got_u)
    got_u = exchange(cur_u, dp, 1)
    y = feed_down(1, sec, a1, order.tie(m), vec[1], w)
    order.mark(y)
    y_moved = to_second(y)
    cur_a = grow(3, cur_a, got_a)
    got_a = exchange(cur_a, dp, 1)
    order.also(far_d, side_d)
    last_d = exchange(order.tie(far_d), dp, 0)
    cur_u = grow(1, cur_u, got_u)
    far_u = exchange(cur_u, dp, 2)
    side_u = exchange(cur_u, dp, 0)
    order.also(y_moved)
    cur_a = grow(1, cur_a, got_a)
    far_a = exchange(cur_a, dp, 2)
    side_a = exchange(cur_a, dp, 0)

    all_columns = slice(None)
    block = ff // 16
    order.also(far_u, side_u)
    last_u = exchange(order.tie(far_u), dp, 0)
    down_grad, = assemble(
        scalars, (order.tie(cur_d), far_d, side_d, last_d), chunk_rows, [(ff, d)],
        lambda outs, part, t: [(all_columns, outs[0].at[pl.ds((8 * part + t) * block, block), :])], "assemble_down")
    order.mark(down_grad, far_a, side_a)
    last_a = exchange(order.tie(far_a), dp, 0)
    up_grad, = assemble(
        scalars, (order.tie(cur_u), far_u, side_u, last_u), chunk_rows, [(d, ff)],
        lambda outs, part, t: [(all_columns, outs[0].at[pl.ds(t % 4 * block, block), pl.ds((2 * part + t // 4) * d, d)])],
        "assemble_up")
    order.mark(up_grad)

    def square_targets(outs, part, t):
        at = pl.ds((2 * part + t % 2) * block, block)
        if t // 2 < 3:
            return [(all_columns, outs[t // 2].at[at, :])]
        return [(pl.ds(half, half), outs[3].at[at, :]), (pl.ds(0, half), outs[4].at[at, :])]

    def vectors(s_ref, chunks, wide, outs):
        lines = outs[5]
        for part in range(2):
            for t in range(8):
                rows_of = chunks(part, t)
                for i in range(dp // 8):
                    at = ((part * 8 + t) * (dp // 8) + i) * share
                    if at < VEC_ROWS * d:
                        lines[at // d:at // d + 1, at % d:at % d + share] = rows_of[i, chunk_rows:chunk_rows + 1, :share].astype(f32)
        for i, row in enumerate((GAIN1, BIAS1, QBIAS, OBIAS, GAIN2, BIAS2, DBIAS)):
            outs[6 + i][...] = lines[row:row + 1, :]
        outs[13][...] = lines[VBIAS:VBIAS + 1, half:]
        for i in range(ff // d):
            outs[14][:, i * d:(i + 1) * d] = lines[UBIAS + i:UBIAS + i + 1, :]

    (out_grad, query_grad, key_grad, value_grad, first_full, lines, gain1_grad, bias1_grad, qbias_grad, obias_grad,
     gain2_grad, bias2_grad, dbias_grad, vbias_grad, ubias_grad) = assemble(
        scalars, (order.tie(cur_a), far_a, side_a, last_a), chunk_rows,
        [(d, d)] * 3 + [(d, half)] * 2 + [(VEC_ROWS, d)] + [(1, d)] * 7 + [(1, half), (1, ff)],
        square_targets, "assemble_attn", vectors, [VMEM] * 10)

    spot_half = lambda t: jnp.where(on_first, t[:t.shape[0] // 2], t[t.shape[0] // 2:])
    block_ends = jnp.where(on_first, jnp.concatenate([dx0, dx_moved], axis=0),
                           jnp.concatenate([y_moved, y], axis=0))[None]
    return (
        block_ends,
        gain1_grad,
        bias1_grad,
        query_grad[None],
        qbias_grad,
        key_grad[None],
        value_grad[None],
        vbias_grad,
        spot_half(first_full),
        spot_half(lines[VBIAS, :half]),
        out_grad[None],
        obias_grad,
        gain2_grad,
        bias2_grad,
        up_grad[None],
        ubias_grad,
        down_grad[None],
        dbias_grad,
    )


def solution(mesh):
    stacked = P("section", None, None)
    vector = P("section", None)
    return jax.shard_map(
        local,
        mesh=mesh,
        in_specs=(
            P("section", "dp", None), P("dp", None),
            vector, vector, stacked, vector, stacked, stacked, vector, P(), P(),
            stacked, vector, vector, vector, stacked, vector, stacked, vector,
        ),
        out_specs=(
            P("section", "dp", None),
            vector, vector, stacked, vector, stacked, stacked, vector, P("section"), P("section"),
            stacked, vector, vector, vector, stacked, vector, stacked, vector,
        ),
        check_vma=False,
    )
```

```python
import functools

import jax
import jax.numpy as jnp
from jax import lax
from jax.experimental import pallas as pl
from jax.experimental.pallas import tpu as pltpu
from jax.sharding import PartitionSpec as P

HEADS = 12
HEAD = 64
PAIR = 2 * HEAD
VMEM_BYTES = 64 * 1024 * 1024

eps_norm = 1e-05
neg_fill = -1e30

f32 = jnp.float32
bf16 = jnp.bfloat16

NN = (((1,), (0,)), ((), ()))
NT = (((1,), (1,)), ((), ()))
TN = (((0,), (0,)), ((), ()))

ANY = pl.BlockSpec(memory_space=pl.ANY)
SMEM = pl.BlockSpec(memory_space=pltpu.SMEM)
VMEM = pl.BlockSpec(memory_space=pltpu.VMEM)

GAIN1, BIAS1, QBIAS, VBIAS, OBIAS, GAIN2, BIAS2, DBIAS, UBIAS = range(9)
VEC_ROWS = 16

SMALL_STEP = 8


def mm(left, right, dims=NN):
    return lax.dot_general(left, right, dims, preferred_element_type=f32)


def sds(shape, dtype):
    return jax.ShapeDtypeStruct(shape, dtype)


def params():
    return pltpu.CompilerParams(vmem_limit_bytes=VMEM_BYTES)


def cost(micros):
    return pl.CostEstimate(flops=int(micros * 1.15e9), bytes_accessed=1, transcendentals=0)


def start_fetch(mine, own, recv, dst, sem):
    @pl.when(mine)
    def _():
        pltpu.make_async_copy(own, dst, sem).start()

    @pl.when(jnp.logical_not(mine))
    def _():
        pltpu.make_async_copy(recv, dst, sem).start()


def wait_fetch(own, dst, sem):
    pltpu.make_async_copy(own, dst, sem).wait()


def norm_parts(rows):
    centre = jnp.mean(rows, axis=-1, keepdims=True)
    centred = rows - centre
    spread = jnp.mean(centred * centred, axis=-1, keepdims=True)
    factor = lax.rsqrt(spread + eps_norm)
    return centred * factor, factor


def norm_back(grad_t, n, w):
    return w * (
        grad_t
        - jnp.mean(grad_t, axis=-1, keepdims=True)
        - n * jnp.mean(grad_t * n, axis=-1, keepdims=True)
    )


def first_keys(sec_ref, lengths_ref, shape, dim):
    at = lax.broadcasted_iota(jnp.int32, shape, dim)
    begin = jnp.zeros(shape, jnp.int32)
    cut = 0
    for i in range(lengths_ref.shape[1]):
        cut = cut + lengths_ref[sec_ref[0], i]
        begin = jnp.where(at >= cut, cut, begin)
    return begin


def row_sum(x):
    return jnp.sum(x, axis=0, keepdims=True)


def attend(rows, q_s, k_s, v_s, o_s, lse_s, bias_s):
    lane = lax.broadcasted_iota(jnp.int32, (1, PAIR), 1)
    step = rows // 2

    def pair(hp, carry):
        ls = pl.ds(pl.multiple_of(hp * PAIR, PAIR), PAIR)
        q2 = q_s[:, ls] * jnp.asarray(HEAD ** -0.5, bf16)
        k2 = k_s[:, ls]
        v2 = v_s[:, ls]
        zero = jnp.zeros((), bf16)
        for qb in range(2):
            qr = slice(qb * step, (qb + 1) * step)
            keys = (qb + 1) * step
            mixed = None
            for j in range(2):
                inside = (lane >= j * HEAD) & (lane < (j + 1) * HEAD)
                kh = jnp.where(inside, k2[:keys], zero)
                vh = jnp.where(inside, v2[:keys], zero)
                s = mm(q2[qr], kh, NT) + bias_s[qr, :keys]
                peak = jnp.max(s, axis=-1, keepdims=True)
                p = jnp.exp(s - peak)
                total = jnp.sum(p, axis=-1, keepdims=True)
                low = (p * (1.0 / total)).astype(bf16)
                part = mm(low, vh)
                mixed = part if mixed is None else mixed + part
                lse_s[qr, :] = jnp.where(lane == 2 * hp + j, peak + jnp.log(total), lse_s[qr, :])
            o_s[qr, ls] = mixed.astype(bf16)
        return carry

    lse_s[...] = jnp.zeros(lse_s.shape, f32)
    lax.fori_loop(0, HEADS // 2, pair, 0)


def attn_forward_steps(layer, sec_ref, x_ref, r_ref, start_ref, vec_ref, weights, outs, held, in_sem, out_sem):
    (qw_o, qw_r, kw_o, kw_r, vw_o, vw_r, fw, ow_o, ow_r), (wq, wk, wv, wo) = weights
    h_out, q_out, k_out, v_out, o_out, m_out, e_out, lse_out, sent_out = outs
    h_s, q_s, k_s, v_s, o_s, m_s, e_s, lse_s, lset_s, bias_s = held
    mine = sec_ref[0] == layer
    rows = x_ref.shape[0]
    half = fw.shape[1]
    copies = []

    def fetch():
        start_fetch(mine, qw_o, qw_r, wq, in_sem.at[0])
        start_fetch(mine, kw_o, kw_r, wk, in_sem.at[1])
        start_fetch(mine, vw_o, vw_r, wv.at[:, half:], in_sem.at[2])
        if layer == 0:
            pltpu.make_async_copy(fw, wv.at[:, :half], in_sem.at[3]).start()
        start_fetch(mine, ow_o, ow_r, wo, in_sem.at[4])

    def put(src, dst):
        copy = pltpu.make_async_copy(src, dst, out_sem.at[len(copies)])
        copy.start()
        copies.append(copy)

    def run():
        wide = x_ref[...].astype(f32)
        n, _ = norm_parts(wide)
        h_s[...] = (n * vec_ref[GAIN1:GAIN1 + 1, :] + vec_ref[BIAS1:BIAS1 + 1, :]).astype(bf16)
        put(h_s, h_out)
        theirs = pl.ds(pl.multiple_of((1 - sec_ref[0]) * half, half), half)
        put(h_s.at[:, theirs], sent_out.at[0, :, half:])
        at_row = lax.broadcasted_iota(jnp.int32, (rows, rows), 0)
        at_col = lax.broadcasted_iota(jnp.int32, (rows, rows), 1)
        bias_s[...] = jnp.where((at_col <= at_row) & (at_col >= first_keys(sec_ref, start_ref, (rows, 1), 0)), 0.0, neg_fill)
        wait_fetch(qw_o, wq, in_sem.at[0])
        q_s[...] = (mm(h_s[...], wq[...]) + vec_ref[QBIAS:QBIAS + 1, :]).astype(bf16)
        put(q_s, q_out)
        wait_fetch(kw_o, wk, in_sem.at[1])
        k_s[...] = mm(h_s[...], wk[...]).astype(bf16)
        put(k_s, k_out)
        wait_fetch(vw_o, wv.at[:, half:], in_sem.at[2])
        if layer == 0:
            wait_fetch(fw, wv.at[:, :half], in_sem.at[3])
            v_s[...] = (mm(h_s[...], wv[...]) + vec_ref[VBIAS:VBIAS + 1, :]).astype(bf16)
        else:
            v_s[:, :half] = r_ref[:, :half]
            v_s[:, half:] = (mm(h_s[...], wv[:, half:]) + vec_ref[VBIAS:VBIAS + 1, half:]).astype(bf16)
        put(v_s, v_out)
        attend(rows, q_s, k_s, v_s, o_s, lse_s, bias_s)
        put(o_s, o_out)
        put(o_s.at[:, theirs], sent_out.at[0, :, :half])
        lset_s[...] = jnp.transpose(lse_s[...])[:VEC_ROWS, :]
        put(lset_s, lse_out)
        wait_fetch(ow_o, wo, in_sem.at[4])
        m = x_ref[...].astype(f32) + (mm(o_s[...], wo[...]) + vec_ref[OBIAS:OBIAS + 1, :])
        m_s[...] = m
        put(m_s, m_out)
        n, _ = norm_parts(m)
        e_s[...] = (n * vec_ref[GAIN2:GAIN2 + 1, :] + vec_ref[BIAS2:BIAS2 + 1, :]).astype(bf16)
        put(e_s, e_out)
        put(e_s, sent_out.at[1])

    return fetch, run, copies


def attn_forward_kernel(layer, sec_ref, start_ref, vec_ref, own_ref, arrived_ref, *refs):
    x_out, x_s, x_sem = refs[18], refs[33], refs[34]
    rows = x_s.shape[0]
    slot = pl.ds(pl.multiple_of(sec_ref[0] * rows, rows), rows)
    start_fetch(sec_ref[0] == 0, own_ref.at[slot, :], arrived_ref.at[slot, :], x_s, x_sem.at[0])
    fetch, run, copies = attn_forward_steps(
        layer, sec_ref, x_s, None, start_ref, vec_ref, (refs[:9], refs[19:23]), refs[9:18], refs[23:33],
        refs[35], refs[36])
    fetch()
    wait_fetch(own_ref.at[slot, :], x_s, x_sem.at[0])
    keep = pltpu.make_async_copy(x_s, x_out, x_sem.at[1])
    keep.start()
    run()
    for copy in copies:
        copy.wait()
    keep.wait()


def attn_forward_shapes(rows, d):
    act = sds((rows, d), bf16)
    wbuf = pltpu.VMEM((d, d), bf16)
    abuf = pltpu.VMEM((rows, d), bf16)
    outs = [act, act, act, act, act, sds((rows, d), f32), act, sds((VEC_ROWS, rows), f32), sds((2, rows, d), bf16)]
    scratch = [wbuf, wbuf, wbuf, wbuf, abuf, abuf, abuf, abuf, abuf,
               pltpu.VMEM((rows, d), f32), abuf, pltpu.VMEM((rows, PAIR), f32),
               pltpu.VMEM((VEC_ROWS, rows), f32), pltpu.VMEM((rows, rows), f32),
               pltpu.SemaphoreType.DMA((5,)), pltpu.SemaphoreType.DMA((11,))]
    return outs, scratch


def attn_forward(layer, sec, start, vec, own, arrived, w):
    rows, d = own.shape[0] // 2, own.shape[1]
    outs, scratch = attn_forward_shapes(rows, d)
    return pl.pallas_call(
        functools.partial(attn_forward_kernel, layer),
        out_shape=outs + [sds((rows, d), bf16)],
        in_specs=[SMEM, SMEM, VMEM] + [ANY] * 11,
        out_specs=[ANY] * 10,
        scratch_shapes=scratch[:-2] + [pltpu.VMEM((rows, d), bf16), pltpu.SemaphoreType.DMA((2,))] + scratch[-2:],
        compiler_params=params(),
        cost_estimate=cost(80),
        name="attn_forward",
    )(sec, start, vec, own, arrived, w["qo"], w["qr"], w["ko"], w["kr"], w["vo"], w["vr"], w["f"], w["oo"], w["or"])


def gelu(u):
    half_u = 0.5 * u
    return half_u + half_u * jnp.tanh(u * (0.7978845608028654 + 0.035677408136300125 * (u * u)))


def middle_kernel(blk, sec_ref, e_ref, m_ref, r_ref, start_ref, vec0_ref, vec1_ref, *refs):
    up_o, up_r, dn_o, dn_r = refs[:4]
    attn_w, outs = refs[4:13], refs[13:28]
    wu0, wd0, wu1, u_s, a_s, f_s, x_s, acc, up_sem, put_sem = refs[28:38]
    wbufs, held, in_sem, out_sem = refs[38:42], refs[42:52], refs[52], refs[53]
    u0_out, a0_out, x_out, u1_out, a1_out, sent_out = outs[:6]
    steps = wu0.shape[0]
    section = sec_ref[0]
    cols = [pl.ds(b * blk, blk) for b in range(steps)]
    for b in range(steps):
        start_fetch(section == 0, up_o.at[:, cols[b]], up_r.at[:, cols[b]], wu0.at[b], up_sem.at[0, b])
    for b in range(steps):
        start_fetch(section == 0, dn_o.at[cols[b], :], dn_r.at[cols[b], :], wd0.at[b], up_sem.at[1, b])
    fetch, run, copies = attn_forward_steps(
        1, sec_ref, x_s, r_ref, start_ref, vec1_ref, (attn_w, wbufs), outs[6:], held, in_sem, out_sem)
    fetch()
    for b in range(steps):
        start_fetch(section == 1, up_o.at[:, cols[b]], up_r.at[:, cols[b]], wu1.at[b], up_sem.at[2, b])
    own = []

    def put(src, dst):
        copy = pltpu.make_async_copy(src, dst, put_sem.at[len(own)])
        copy.start()
        own.append(copy)

    def expand(layer, b, source, weights, vec_ref):
        wait_fetch(up_o.at[:, cols[0]], weights.at[b], up_sem.at[2 * layer, b])
        f_s[b % 2] = mm(source[...], weights[b]) + vec_ref[UBIAS + b:UBIAS + b + 1, :]

    def activate(layer, b, u_out, a_out):
        u = f_s[b % 2]
        u_s[layer, b] = u.astype(bf16)
        a_s[layer, b] = gelu(u).astype(bf16)
        put(u_s.at[layer, b], u_out.at[:, cols[b]])
        put(a_s.at[layer, b], a_out.at[:, cols[b]])

    expand(0, 0, e_ref, wu0, vec0_ref)
    for b in range(steps):
        if b + 1 < steps:
            expand(0, b + 1, e_ref, wu0, vec0_ref)
        activate(0, b, u0_out, a0_out)
        wait_fetch(dn_o.at[cols[0], :], wd0.at[b], up_sem.at[1, b])
        part = mm(a_s[0, b], wd0[b])
        acc[...] = part if b == 0 else acc[...] + part
    x_s[...] = (m_ref[...] + (acc[...] + vec0_ref[DBIAS:DBIAS + 1, :])).astype(bf16)
    put(x_s, x_out)
    run()
    expand(1, 0, held[6], wu1, vec1_ref)
    for b in range(steps):
        if b + 1 < steps:
            expand(1, b + 1, held[6], wu1, vec1_ref)
        activate(1, b, u1_out, a1_out)
    theirs = (1 - section) * (steps // 2)
    for b in range(steps // 2):
        for layer in range(2):
            put(a_s.at[layer, theirs + b], sent_out.at[layer, :, cols[b]])
    for copy in own + copies:
        copy.wait()


def middle(sec, e, m, r, start, vec, w):
    rows, d = e.shape
    ff = w["uo"].shape[1]
    blk = d
    n = ff // blk
    outs, scratch = attn_forward_shapes(rows, d)
    wide = sds((rows, ff), bf16)
    return pl.pallas_call(
        functools.partial(middle_kernel, blk),
        out_shape=[wide, wide, sds((rows, d), bf16), wide, wide, sds((2, rows, ff // 2), bf16)] + outs,
        in_specs=[SMEM] + [VMEM] * 3 + [SMEM] + [VMEM] * 2 + [ANY] * 13,
        out_specs=[ANY] * 15,
        scratch_shapes=[pltpu.VMEM((n, d, blk), bf16), pltpu.VMEM((n, blk, d), bf16), pltpu.VMEM((n, d, blk), bf16),
                        pltpu.VMEM((2, n, rows, blk), bf16), pltpu.VMEM((2, n, rows, blk), bf16),
                        pltpu.VMEM((2, rows, blk), f32), pltpu.VMEM((rows, d), bf16), pltpu.VMEM((rows, d), f32),
                        pltpu.SemaphoreType.DMA((3, n)), pltpu.SemaphoreType.DMA((4 * n + 1 + n,))] + scratch,
        compiler_params=params(),
        cost_estimate=cost(80),
        name="middle",
    )(sec, e, m, r, start, vec[0], vec[1], w["uo"], w["ur"], w["do"], w["dr"],
      w["qo"], w["qr"], w["ko"], w["kr"], w["vo"], w["vr"], w["f"], w["oo"], w["or"])


def theirs_at(steps):
    half = steps // 2

    def index(j, s):
        return (0, jnp.where(s[0] == 0, jnp.maximum(j - half, 0), jnp.minimum(j, half - 1)))
    return index


def feed_down_kernel(layer, blk, sec_ref, a_ref, m_ref, vec_ref, dn_o, dn_r, z_ref, wd, acc, sem):
    j = pl.program_id(0)
    steps = pl.num_programs(0)
    mine = sec_ref[0] == layer

    @pl.when(j == 0)
    def _():
        for b in range(dn_o.shape[0] // blk):
            cols = pl.ds(b * blk, blk)
            start_fetch(mine, dn_o.at[cols, :], dn_r.at[cols, :], wd.at[b], sem.at[b])

    wait_fetch(dn_o.at[pl.ds(0, blk), :], wd.at[j], sem.at[j])
    part = mm(a_ref[...], wd[j])

    @pl.when(j == 0)
    def _():
        acc[...] = part

    @pl.when((j > 0) & (j < steps - 1))
    def _():
        acc[...] += part

    @pl.when(j == steps - 1)
    def _():
        z_ref[...] = (m_ref[...] + (acc[...] + part + vec_ref[DBIAS:DBIAS + 1, :])).astype(bf16)


def feed_down(layer, sec, a, m, vec, w):
    rows, ff = a.shape
    d = m.shape[1]
    blk = d
    n = ff // blk
    return pl.pallas_call(
        functools.partial(feed_down_kernel, layer, blk),
        grid=(n,),
        out_shape=sds((rows, d), bf16),
        in_specs=[SMEM, pl.BlockSpec((rows, blk), lambda j: (0, j)), VMEM, VMEM, ANY, ANY],
        out_specs=pl.BlockSpec((rows, d), lambda j: (0, 0)),
        scratch_shapes=[pltpu.VMEM((n, blk, d), bf16), pltpu.VMEM((rows, d), f32), pltpu.SemaphoreType.DMA((n,))],
        compiler_params=params(),
        cost_estimate=cost(2),
        name="feed_down",
    )(sec, a, m, vec, w["do"], w["dr"])


def layer_backward_kernel(layer, blk, sec_ref, dz_ref, m_ref, lse_ref, start_ref, vec_ref, dr2_ref,
                          u_in, x_in, q_in, k_in, v_in, o_in,
                          up_o, up_r, dn_o, dn_r, qw_o, qw_r, kw_o, kw_r, vw_o, vw_r, fw, ow_o, ow_r,
                          du_out, sent_out, bundle_out, shared_ref, small_ref,
                          wu, wd, wq, wk, wv, wo, u_s, x_s, q_ref, k_ref, v_ref, o_ref, du_s, da_s, acc, dm_s,
                          bundle_ref, do_s, delta_s, bias_s, feed_sem, sem, in_sem, out_sem):
    mine = sec_ref[0] == layer
    rows, d = dz_ref.shape
    half = fw.shape[1]
    steps = wu.shape[0]
    cols = [pl.ds(b * blk, blk) for b in range(steps)]
    for b in range(steps):
        start_fetch(mine, dn_o.at[cols[b], :], dn_r.at[cols[b], :], wd.at[b], feed_sem.at[0, b])
        pltpu.make_async_copy(u_in.at[:, cols[b]], u_s.at[b], feed_sem.at[2, b]).start()
        start_fetch(mine, up_o.at[:, cols[b]], up_r.at[:, cols[b]], wu.at[b], feed_sem.at[1, b])
    start_fetch(mine, ow_o, ow_r, wo, sem.at[4])
    loads = [pltpu.make_async_copy(src, dst, in_sem.at[i]) for i, (src, dst) in enumerate(
        ((q_in, q_ref), (k_in, k_ref), (v_in, v_ref), (o_in, o_ref), (x_in, x_s)))]
    for load in loads:
        load.start()
    start_fetch(mine, qw_o, qw_r, wq, sem.at[0])
    start_fetch(mine, kw_o, kw_r, wk, sem.at[1])
    start_fetch(mine, vw_o, vw_r, wv.at[:, half:], sem.at[2])
    if layer == 0:
        pltpu.make_async_copy(fw, wv.at[:, :half], sem.at[3]).start()
    copies = []

    def put(src, dst):
        copy = pltpu.make_async_copy(src, dst, out_sem.at[len(copies)])
        copy.start()
        copies.append(copy)

    small_ref[...] = jnp.zeros(small_ref.shape, f32)

    def expand(b):
        wait_fetch(dn_o.at[cols[0], :], wd.at[b], feed_sem.at[0, b])
        da_s[b % 2] = mm(dz_ref[...], wd[b], NT)

    def activate(b):
        pltpu.make_async_copy(u_in.at[:, cols[b]], u_s.at[b], feed_sem.at[2, b]).wait()
        u = u_s[b].astype(f32)
        sq = u * u
        th = jnp.tanh(u * (0.7978845608028654 + 0.035677408136300125 * sq))
        slope = 0.5 + 0.5 * th + (0.5 * u) * (1.0 - th * th) * (0.7978845608028654 + 0.10703222440890037 * sq)
        du = (slope * da_s[b % 2]).astype(bf16)
        du_s[b] = du
        small_ref[UBIAS + b:UBIAS + b + 1, :] = row_sum(du.astype(f32))
        put(du_s.at[b], du_out.at[:, cols[b]])

    expand(0)
    for b in range(steps):
        if b + 1 < steps:
            expand(b + 1)
        activate(b)
        wait_fetch(up_o.at[:, cols[0]], wu.at[b], feed_sem.at[1, b])
        part = mm(du_s[b], wu[b], NT)
        acc[...] = part if b == 0 else acc[...] + part
    theirs = (1 - sec_ref[0]) * (steps // 2)
    for b in range(steps // 2):
        put(du_s.at[theirs + b], sent_out.at[b])
    de = acc[...]
    n, w = norm_parts(m_ref[...])
    dz = dz_ref[...].astype(f32)
    dm_s[...] = dz + norm_back(de * vec_ref[GAIN2:GAIN2 + 1, :], n, w)
    small_ref[GAIN2:GAIN2 + 1, :] = row_sum(de * n)
    small_ref[BIAS2:BIAS2 + 1, :] = row_sum(de)
    small_ref[DBIAS:DBIAS + 1, :] = row_sum(dz)

    low_ref, dq_ref, dk_ref, dv_ref, dx_ref = (bundle_ref.at[pl.ds(i * rows, rows), :] for i in range(5))
    low_ref[...] = dm_s[...].astype(bf16)
    at_key = lax.broadcasted_iota(jnp.int32, (rows, rows), 0)
    at_query = lax.broadcasted_iota(jnp.int32, (rows, rows), 1)
    bias_s[...] = jnp.where((at_key <= at_query) & (at_key >= first_keys(sec_ref, start_ref, (1, rows), 1)), 0.0, neg_fill)
    wait_fetch(ow_o, wo, sem.at[4])
    do = mm(low_ref[...], wo[...], NT).astype(bf16)
    do_s[...] = do
    for load in loads:
        load.wait()
    head_row = lax.broadcasted_iota(jnp.int32, (VEC_ROWS, d), 0)
    head_col = lax.broadcasted_iota(jnp.int32, (VEC_ROWS, d), 1) // HEAD
    pick = (head_row == head_col).astype(f32)
    delta_s[...] = lax.dot_general(pick, do.astype(f32) * o_ref[...].astype(f32), NT,
                                   precision=lax.Precision.HIGHEST, preferred_element_type=f32)
    lane = lax.broadcasted_iota(jnp.int32, (1, PAIR), 1)
    step = rows // 2
    scale = HEAD ** -0.5
    zero = jnp.zeros((), bf16)

    def pair(hp, carry):
        ls = pl.ds(pl.multiple_of(hp * PAIR, PAIR), PAIR)
        q2 = q_ref[:, ls] * jnp.asarray(scale, bf16)
        k2 = k_ref[:, ls]
        v2 = v_ref[:, ls]
        do2 = do_s[:, ls]
        dq_parts = []
        for kb in range(2):
            kr = slice(kb * step, (kb + 1) * step)
            first = kb * step
            dk = dv = dq = None
            for j in range(2):
                inside = (lane >= j * HEAD) & (lane < (j + 1) * HEAD)
                kh = jnp.where(inside, k2[kr], zero)
                vh = jnp.where(inside, v2[kr], zero)
                qh = jnp.where(inside, q2[first:], zero)
                doh = jnp.where(inside, do2[first:], zero)
                row = pl.ds(2 * hp + j, 1)
                st = mm(kh, qh, NT) + bias_s[kr, first:]
                pt = jnp.exp(st - lse_ref[row, first:])
                dpt = mm(vh, doh, NT)
                dst = (pt * (dpt - delta_s[row, first:])).astype(bf16)
                dv_j = mm(pt.astype(bf16), doh)
                dk_j = mm(dst, qh)
                dq_j = mm(dst, kh, TN)
                dk = dk_j if dk is None else dk + dk_j
                dv = dv_j if dv is None else dv + dv_j
                dq = dq_j if dq is None else dq + dq_j
            dk_ref[kr, ls] = dk.astype(bf16)
            if layer == 1:
                dv_ref[kr, ls] = dv.astype(bf16)

                @pl.when(hp < HEADS // 4)
                def _():
                    shared_ref[kr, ls] = dv
            else:
                extra = jnp.where(hp < HEADS // 4, dr2_ref[kr, pl.ds(pl.multiple_of((hp % (HEADS // 4)) * PAIR, PAIR), PAIR)], 0.0)
                dv_ref[kr, ls] = (dv + extra).astype(bf16)
            dq_parts.append(dq)
        dq_ref[:step, ls] = (dq_parts[0][:step] * scale).astype(bf16)
        dq_ref[step:, ls] = ((dq_parts[0][step:] + dq_parts[1]) * scale).astype(bf16)
        return carry

    if layer == 0:
        shared_ref[...] = jnp.zeros(shared_ref.shape, f32)
    lax.fori_loop(0, HEADS // 2, pair, 0)
    put(bundle_ref.at[pl.ds(0, 4 * rows), :], bundle_out.at[pl.ds(0, 4 * rows), :])

    wait_fetch(qw_o, wq, sem.at[0])
    dh = mm(dq_ref[...], wq[...], NT)
    wait_fetch(kw_o, wk, sem.at[1])
    dh = dh + mm(dk_ref[...], wk[...], NT)
    wait_fetch(vw_o, wv.at[:, half:], sem.at[2])
    if layer == 0:
        wait_fetch(fw, wv.at[:, :half], sem.at[3])
        dh = dh + mm(dv_ref[...], wv[...], NT)
    else:
        dh = dh + mm(dv_ref[:, half:], wv[:, half:], NT)
    n, w = norm_parts(x_s[...].astype(f32))
    dx_ref[...] = (dm_s[...] + norm_back(dh * vec_ref[GAIN1:GAIN1 + 1, :], n, w)).astype(bf16)
    small_ref[GAIN1:GAIN1 + 1, :] = row_sum(dh * n)
    small_ref[BIAS1:BIAS1 + 1, :] = row_sum(dh)
    small_ref[QBIAS:QBIAS + 1, :] = row_sum(dq_ref[...].astype(f32))
    small_ref[VBIAS:VBIAS + 1, :] = row_sum(dv_ref[...].astype(f32))
    small_ref[OBIAS:OBIAS + 1, :] = row_sum(low_ref[...].astype(f32))
    bundle_ref[5 * rows:, :] = small_ref[...].astype(bf16)
    put(bundle_ref.at[pl.ds(4 * rows, rows + VEC_ROWS), :], bundle_out.at[pl.ds(4 * rows, rows + VEC_ROWS), :])
    for copy in copies:
        copy.wait()


def layer_backward(layer, sec, dz, dz_at, t, start_row, vec, dr2, w):
    rows, ff = t["u"].shape
    d = t["m"].shape[1]
    half = w["f"].shape[1]
    blk = d
    n = ff // blk
    wbuf = pltpu.VMEM((d, d), bf16)
    act = pltpu.VMEM((rows, d), bf16)
    wide = pltpu.VMEM((rows, d), f32)
    blocks = pltpu.VMEM((n, rows, blk), bf16)
    dma = pltpu.SemaphoreType.DMA
    bundle = (5 * rows + VEC_ROWS, d)
    return pl.pallas_call(
        functools.partial(layer_backward_kernel, layer, blk),
        grid=(1,),
        out_shape=[sds((rows, ff), bf16), sds((n // 2, rows, blk), bf16), sds(bundle, bf16), sds((rows, half), f32),
                   sds((VEC_ROWS, d), f32)],
        in_specs=[SMEM, pl.BlockSpec((rows, d), lambda i: (dz_at, 0)), VMEM, VMEM, SMEM, VMEM, VMEM] + [ANY] * 19,
        out_specs=[ANY] * 3 + [VMEM] * 2,
        scratch_shapes=[pltpu.VMEM((n, d, blk), bf16), pltpu.VMEM((n, blk, d), bf16), wbuf, wbuf, wbuf, wbuf,
                        blocks, act, act, act, act, act, blocks, pltpu.VMEM((2, rows, blk), f32), wide, wide,
                        pltpu.VMEM(bundle, bf16), act, pltpu.VMEM((VEC_ROWS, rows), f32), pltpu.VMEM((rows, rows), f32),
                        dma((3, n)), dma((5,)), dma((5,)), dma((n + n // 2 + 2,))],
        compiler_params=params(),
        cost_estimate=cost(80),
        name="layer_backward",
    )(sec, dz, t["m"], t["lse"], start_row, vec, dr2, t["u"], t["x"], t["q"], t["k"], t["v"], t["o"],
      w["uo"], w["ur"], w["do"], w["dr"],
      w["qo"], w["qr"], w["ko"], w["kr"], w["vo"], w["vr"], w["f"], w["oo"], w["or"])


def store_chunks(ref, value):
    c, r, _ = ref.shape
    for i in range(c):
        ref[i] = value[i * r:(i + 1) * r].astype(bf16)


def quarter_of(g, s):
    return 2 * jnp.where(g < 2, 1 - s[1], s[1]) + g % 2


def quarters(kernel, scalars, in_specs, operands, shape, name):
    per = shape[0] // 2
    return pl.pallas_call(
        kernel,
        grid_spec=pltpu.PrefetchScalarGridSpec(
            num_scalar_prefetch=1, grid=(4,), in_specs=in_specs,
            out_specs=[pl.BlockSpec((per,) + shape[1:], lambda g, s: (jnp.minimum(g, 1), 0, 0)),
                       pl.BlockSpec((per,) + shape[1:], lambda g, s: (jnp.maximum(g - 2, 0), 0, 0))]),
        out_shape=[sds(shape, bf16)] * 2,
        compiler_params=params(),
        cost_estimate=cost(80),
        name=name,
    )(scalars, *operands)


def store_quarter(send_ref, keep_ref, value):
    g = pl.program_id(0)

    @pl.when(g < 2)
    def _():
        store_chunks(send_ref, value)

    @pl.when(g >= 2)
    def _():
        store_chunks(keep_ref, value)


def down_gradient(scalars, a, a_got, dz, dz_got, dz_at, chunk_rows):
    a_got, a_at = a_got
    rows, ff = a.shape
    d = dz.shape[1]
    q = d // 2

    def kernel(s_ref, a_ref, b_ref, x_ref, y_ref, send_ref, keep_ref):
        store_quarter(send_ref, keep_ref, mm(a_ref[...], x_ref[...], TN) + mm(b_ref[0], y_ref[...], TN))

    whole = pl.BlockSpec((rows, d), lambda g, s: (dz_at, 0))
    return quarters(
        kernel, scalars,
        [pl.BlockSpec((rows, q), lambda g, s: (0, 4 * s[0] + quarter_of(g, s))),
         pl.BlockSpec((1, rows, q), lambda g, s: (a_at, 0, quarter_of(g, s))), whole, whole],
        (a, a_got, dz, dz_got), (2 * q // chunk_rows, chunk_rows, d), "down_gradient")


def up_gradient(scalars, e, sent_got, du, du_got, chunk_rows):
    rows, ff = du.shape
    d = e.shape[1]
    q = d // 2

    def kernel(s_ref, e_ref, f_ref, du_ref, dg_ref, send_ref, keep_ref):
        store_quarter(send_ref, keep_ref, mm(e_ref[...], du_ref[...], TN) + mm(f_ref[0], dg_ref[0], TN))

    return quarters(
        kernel, scalars,
        [pl.BlockSpec((rows, q), lambda g, s: (0, g % 2)),
         pl.BlockSpec((1, rows, q), lambda g, s: (1, 0, g % 2)),
         pl.BlockSpec((rows, d), lambda g, s: (0, 2 * s[0] + quarter_of(g, s) // 2)),
         pl.BlockSpec((1, rows, d), lambda g, s: (quarter_of(g, s) // 2, 0, 0))],
        (e, sent_got, du, du_got), (2 * q // chunk_rows, chunk_rows, d), "up_gradient")


def vector_share(width, chunks):
    return max(PAIR, VEC_ROWS * width // chunks)


def attn_gradient(scalars, o, h, sent_got, bundle, bundle_got, small, chunk_rows, extra):
    rows, d = o.shape
    q = d // 2
    per = q // chunk_rows
    share = vector_share(d, 8 * per)

    def kernel(s_ref, o_ref, h_ref, l_ref, own_ref, got_ref, small_ref, small_got_ref, send_ref, keep_ref, sum_ref):
        sum_ref[...] = small_ref[...] + small_got_ref[...].astype(f32)
        g = pl.program_id(0)
        which = quarter_of(g, s_ref)
        for i in range(4):
            @pl.when(which == i)
            def _():
                left = o_ref if i == 0 else h_ref
                value = mm(left[...], own_ref[...], TN) + mm(l_ref[0], got_ref[...], TN)
                for side, ref in enumerate((send_ref, keep_ref)):
                    @pl.when(g // 2 == side)
                    def _():
                        ref[:, chunk_rows:, :] = jnp.zeros((per, extra, d), bf16)
                        for c in range(per):
                            ref[c, :chunk_rows, :] = value[c * chunk_rows:(c + 1) * chunk_rows].astype(bf16)
                        for part_index in range(2):
                            @pl.when(s_ref[0] == part_index)
                            def _():
                                for c in range(per):
                                    at = ((4 * part_index + i) * per + c) * share
                                    if at < VEC_ROWS * d:
                                        row = sum_ref[at // d:at // d + 1, at % d:at % d + share]
                                        ref[c, chunk_rows:chunk_rows + 1, :share] = row.astype(bf16)

    part = pl.BlockSpec((rows, q), lambda g, s: (0, s[0]))
    right = pl.BlockSpec((rows, d), lambda g, s: (quarter_of(g, s), 0))
    shape = (2 * per, chunk_rows + extra, d)
    return pl.pallas_call(
        kernel,
        grid_spec=pltpu.PrefetchScalarGridSpec(
            num_scalar_prefetch=1, grid=(4,),
            in_specs=[part, part,
                      pl.BlockSpec((1, rows, q), lambda g, s: (0, 0, jnp.minimum(quarter_of(g, s), 1))),
                      right, right, pl.BlockSpec((VEC_ROWS, d), lambda g, s: (0, 0)),
                      pl.BlockSpec((VEC_ROWS, d), lambda g, s: (5 * rows // VEC_ROWS, 0))],
            out_specs=[pl.BlockSpec((per,) + shape[1:], lambda g, s: (jnp.minimum(g, 1), 0, 0)),
                       pl.BlockSpec((per,) + shape[1:], lambda g, s: (jnp.maximum(g - 2, 0), 0, 0))],
            scratch_shapes=[pltpu.VMEM((VEC_ROWS, d), f32)]),
        out_shape=[sds(shape, bf16)] * 2,
        compiler_params=params(),
        cost_estimate=cost(80),
        name="attn_gradient",
    )(scalars, o, h, sent_got, bundle, bundle_got, small, bundle_got)


AXES = ("section", "dp")
SWAP = [(0, 1), (1, 0)]


def bit_orders(dp):
    bits = list(range(dp.bit_length() - 1))
    return bits, [1, 0] + bits[2:]


def exchange(array, dp, step):
    first, second = bit_orders(dp)
    pairs = [(i, i ^ (1 << first[step])) for i in range(dp)]
    pairs += [(dp + i, dp + (i ^ (1 << second[step]))) for i in range(dp)]
    return lax.ppermute(array, AXES, pairs)


def block_of(chunks, rows):
    best = 1
    for c in range(1, chunks + 1):
        if chunks % c == 0 and c * rows <= 768:
            best = c
    return best


def add_split(bit, parts):
    _, c, r, w = parts[0][0].shape
    counts = [p[0].shape[0] for p in parts]
    n = sum(counts)
    h = c // 2
    cb = block_of(h, r)
    nb = h // cb
    ends = [sum(counts[:i + 1]) for i in range(len(counts))]
    begins = [e - k for e, k in zip(ends, counts)]

    def kernel(s_ref, *refs):
        send_ref, keep_ref = refs[-2:]
        g, i = pl.program_id(0), pl.program_id(1)
        for t in range(len(parts)):
            @pl.when((i >= begins[t]) & (i < ends[t]))
            def _():
                total = (refs[2 * t][...].astype(f32) + refs[2 * t + 1][...].astype(f32)).astype(bf16)

                @pl.when(g == 0)
                def _():
                    send_ref[...] = total

                @pl.when(g == 1)
                def _():
                    keep_ref[...] = total

    def source(t):
        def index(g, i, j, s):
            inside = (i >= begins[t]) & (i < ends[t])
            side = jnp.where(g == 0, 1 - s[0], s[0])
            return (jnp.clip(i - begins[t], 0, counts[t] - 1), jnp.where(inside, side * nb + j, 0), 0, 0)
        return pl.BlockSpec((1, cb, r, w), index)

    def send_at(g, i, j, s):
        return (jnp.where(g == 0, i, n - 1), jnp.where(g == 0, j, nb - 1), 0, 0)

    def keep_at(g, i, j, s):
        return (jnp.where(g == 0, 0, i), jnp.where(g == 0, 0, j), 0, 0)

    flat = [x for p in parts for x in p]
    return pl.pallas_call(
        kernel,
        grid_spec=pltpu.PrefetchScalarGridSpec(
            num_scalar_prefetch=1, grid=(2, n, nb),
            in_specs=[source(t) for t in range(len(parts)) for _ in range(2)],
            out_specs=[pl.BlockSpec((1, cb, r, w), send_at), pl.BlockSpec((1, cb, r, w), keep_at)]),
        out_shape=[sds((n, h, r, w), bf16)] * 2,
        compiler_params=params(),
        cost_estimate=cost(SMALL_STEP),
        name="add_split",
    )(bit, *flat)


def merge(bit, cur, arrived):
    n, c, r, w = cur.shape
    cb = block_of(c, r)
    nb = c // cb

    def kernel(s_ref, a_ref, b_ref, out_ref):
        g = pl.program_id(1)

        @pl.when(g == s_ref[0])
        def _():
            out_ref[...] = a_ref[...]

        @pl.when(g != s_ref[0])
        def _():
            out_ref[...] = b_ref[...]

    def at(own):
        def index(i, g, j, s):
            mine = (g == s[0]) if own else (g != s[0])
            return (i, jnp.where(mine, j, 0), 0, 0)
        return pl.BlockSpec((1, cb, r, w), index)

    return pl.pallas_call(
        kernel,
        grid_spec=pltpu.PrefetchScalarGridSpec(
            num_scalar_prefetch=1, grid=(n, 2, nb), in_specs=[at(True), at(False)],
            out_specs=pl.BlockSpec((1, cb, r, w), lambda i, g, j, s: (i, g * nb + j, 0, 0))),
        out_shape=sds((n, 2 * c, r, w), bf16),
        compiler_params=params(),
        cost_estimate=cost(SMALL_STEP),
        name="merge",
    )(bit, cur, arrived)


def assemble(scalars, sources, chunk_rows, out_shapes, targets, name, finish=None, extra_specs=()):
    _, c, r, w = sources[0].shape
    cb = c // 2
    block = cb * chunk_rows

    def kernel(s_ref, *refs):
        ins, outs = refs[:4], refs[4:4 + len(out_shapes)]
        held, wide, in_sem, out_sem = refs[4 + len(out_shapes):]
        loads = [pltpu.make_async_copy(ins[i], held.at[i], in_sem.at[i]) for i in range(4)]
        for load in loads:
            load.start()
        for load in loads:
            load.wait()

        def chunks(part, t):
            own = s_ref[0] == part
            top, mid, low = t // 4, (t // 2) % 2, t % 2
            first = jnp.where(own, top, mid)
            second = jnp.where(own, mid, top)
            which = 2 * jnp.where(first == s_ref[1], 0, 1) + jnp.where(low == s_ref[2], 0, 1)
            return held.at[which, part, pl.ds(second * cb, cb)]

        copies = []
        for part in range(2):
            for t in range(8):
                at = part * 8 + t
                rows = chunks(part, t)
                for i in range(cb):
                    wide[at, i * chunk_rows:(i + 1) * chunk_rows, :] = rows[i, :chunk_rows, :].astype(f32)
                for source, target in targets(outs, part, t):
                    copy = pltpu.make_async_copy(wide.at[at, :, source], target, out_sem.at[len(copies)])
                    copy.start()
                    copies.append(copy)
        if finish is not None:
            finish(s_ref, chunks, wide, outs, [out_sem.at[len(copies) + i] for i in range(2)])
        for copy in copies:
            copy.wait()

    out_specs = [ANY] * (len(out_shapes) - len(extra_specs)) + list(extra_specs)
    return pl.pallas_call(
        kernel,
        out_shape=[sds(o, f32) for o in out_shapes],
        in_specs=[SMEM] + [ANY] * 4,
        out_specs=out_specs,
        scratch_shapes=[pltpu.VMEM((4, 2, c, r, w), bf16), pltpu.VMEM((16, block, w), f32),
                        pltpu.SemaphoreType.DMA((4,)), pltpu.SemaphoreType.DMA((20,))],
        compiler_params=params(),
        cost_estimate=cost(16),
        name=name,
    )(scalars, *sources)


def after(array, *earlier):
    return lax.optimization_barrier((array,) + earlier)[0]


class Order:
    def __init__(self):
        self.last = ()

    def mark(self, *arrays):
        self.last = arrays

    def also(self, *arrays):
        self.last = self.last + arrays

    def tie(self, array):
        return after(array, *self.last) if self.last else array


def pack_kernel(gain1, bias1, qbias, first_bias, vbias, obias, gain2, bias2, dbias, ubias, out_ref):
    d = out_ref.shape[1]
    half = first_bias.shape[1]
    out_ref[...] = jnp.zeros(out_ref.shape, f32)
    for row, ref in ((GAIN1, gain1), (BIAS1, bias1), (QBIAS, qbias), (OBIAS, obias), (GAIN2, gain2), (BIAS2, bias2),
                     (DBIAS, dbias)):
        out_ref[row:row + 1, :] = ref[...]
    out_ref[VBIAS:VBIAS + 1, :half] = first_bias[...]
    out_ref[VBIAS:VBIAS + 1, half:] = vbias[...]
    for i in range(ubias.shape[1] // d):
        out_ref[UBIAS + i:UBIAS + i + 1, :] = ubias[:, i * d:(i + 1) * d]


def pack_vectors(*vectors):
    return pl.pallas_call(
        pack_kernel,
        out_shape=sds((VEC_ROWS, vectors[0].shape[1]), f32),
        in_specs=[VMEM] * len(vectors),
        out_specs=VMEM,
        compiler_params=params(),
        cost_estimate=cost(2),
        name="pack_vectors",
    )(*vectors)


def local(
    boundary,
    lengths,
    norm_one_gain,
    norm_one_bias,
    query_weight,
    query_bias,
    key_weight,
    value_weight,
    value_bias,
    first_value_weight,
    first_value_bias,
    out_weight,
    out_bias,
    norm_two_gain,
    norm_two_bias,
    up_weight,
    up_bias,
    down_weight,
    down_bias,
):
    section = lax.axis_index("section")
    spot = lax.axis_index("dp")
    dp = lax.axis_size("dp")
    on_first = section == 0
    sec = jnp.reshape(section, (1,)).astype(jnp.int32)
    rows = boundary.shape[1] // 2
    d = boundary.shape[2]
    half = value_weight.shape[2]
    ff = up_weight.shape[2]

    def swap(array):
        return lax.ppermute(array, "section", SWAP)

    vec_own = pack_vectors(norm_one_gain, norm_one_bias, query_bias, first_value_bias[None], value_bias, out_bias,
                           norm_two_gain, norm_two_bias, down_bias, up_bias)
    own_rows = boundary[0]
    arrived_rows = swap(own_rows)
    vec_arrived = swap(vec_own)
    vec = (jnp.where(on_first, vec_own, vec_arrived), jnp.where(on_first, vec_arrived, vec_own))
    w = {"qo": query_weight[0], "ko": key_weight[0], "vo": value_weight[0], "oo": out_weight[0],
         "uo": up_weight[0], "do": down_weight[0], "f": first_value_weight}
    for name in "qkvo":
        w[name + "r"] = swap(w[name + "o"])
    w["ur"] = swap(after(w["uo"], w["qr"]))
    w["dr"] = swap(after(w["do"], w["kr"]))

    chunk_rows = ff // (2 * dp)
    extra = 16
    first_bits, second_bits = bit_orders(dp)
    levels = len(first_bits)
    bit = [((spot >> jnp.where(on_first, first_bits[s], second_bits[s])) & 1).astype(jnp.int32) for s in range(levels)]
    bits = [jnp.reshape(b, (1,)) for b in bit]
    scalars = jnp.stack([sec[0], bit[0], bit[2]])
    order = Order()

    h, q, k, v, o, m, e, lse, sent, x0 = attn_forward(0, sec, lengths, vec[0], own_rows, arrived_rows, w)
    kept = [dict(x=x0, h=h, q=q, k=k, v=v, o=o, m=m, e=e, lse=lse, sent_got=swap(sent))]
    u0, a0, x1, u1, a1, a_sent, h, q, k, v, o, m, e, lse, sent = middle(sec, e, m, v, lengths, vec, w)
    a_got = swap(a_sent)
    kept[0].update(u=u0, a=a0, a_got=(a_got, 0))
    kept.append(dict(x=x1, h=h, q=q, k=k, v=v, o=o, m=m, e=e, lse=lse, u=u1, a=a1, sent_got=swap(sent), a_got=(a_got, 1)))
    order.mark(x1)
    own_late = order.tie(own_rows)
    dz1 = jnp.where(on_first, arrived_rows[:rows], own_late[rows:])
    dz1_got = jnp.where(on_first, arrived_rows[rows:], own_late[:rows])
    order.mark(x1)

    def cut(level, parts):
        (first_keep, first_got), *rest = parts
        send, keep = add_split(bits[level], [(order.tie(first_keep), first_got)] + rest)
        order.mark(send)
        return keep, exchange(send, dp, level)

    def deep(part):
        for s in range(4, levels):
            part = cut(s, [part])
        return part

    def grow(level, cur, got):
        cur = merge(bits[level], order.tie(cur), got)
        order.mark(cur)
        return cur

    def first_sent(grads):
        send, keep = grads
        order.mark(send)
        return keep[None], exchange(send[None], dp, 0)

    def down_step(layer, dz, dz_got, dz_at):
        t = kept[layer]
        return first_sent(down_gradient(scalars, order.tie(t["a"]), t["a_got"], dz, dz_got, dz_at, chunk_rows))

    def back_step(layer, dz, dz_at, dr2):
        du, sent, bundle, dr2, small = layer_backward(
            layer, sec, dz, dz_at, dict(kept[layer], u=order.tie(kept[layer]["u"])), lengths, vec[layer], dr2, w)
        order.mark(bundle)
        return bundle, swap(bundle), dr2, small, du, swap(sent)

    def up_step(layer, back):
        t = kept[layer]
        return first_sent(up_gradient(scalars, order.tie(t["e"]), t["sent_got"], back[4], back[5], chunk_rows))

    def attn_grad_step(layer, attn):
        t = kept[layer]
        return first_sent(attn_gradient(scalars, order.tie(t["o"]), t["h"], t["sent_got"], attn[0], attn[1], attn[3],
                                        chunk_rows, extra))

    to_second = lambda t: lax.ppermute(t, "section", [(0, 1)])

    def summed(part, i):
        keep, got = part
        return (keep[i:i + 1].astype(f32) + got[i:i + 1].astype(f32)).astype(bf16)

    def hand_over(second, first):
        own = order.tie(jnp.where(on_first, first, second))
        sent = jnp.where(on_first, second, first)
        order.mark(sent)
        return own, swap(sent)

    def both_parts(pair):
        own, got = pair
        cur = merge(sec, order.tie(own), got)
        order.mark(cur)
        cur = jnp.swapaxes(cur, 0, 1)
        for s in range(levels - 1, 3, -1):
            cur = grow(s, cur, exchange(cur, dp, s))
        return cur, exchange(cur, dp, 3)

    back1 = back_step(1, dz1, 0, jnp.zeros((rows, half), f32))
    order.also(kept[0]["sent_got"], kept[1]["sent_got"])
    down1 = down_step(1, dz1, dz1_got, 0)
    up1 = up_step(1, back1)
    square1 = attn_grad_step(1, back1)
    down0 = down_step(0, back1[0], back1[1], 4)
    down1 = cut(1, [down1])
    back0 = back_step(0, back1[0], 4, back1[2])
    dx0, dx_moved = (t[4 * rows:5 * rows] for t in back0[:2])
    up1 = cut(1, [up1])
    square1 = cut(1, [square1])
    down0 = cut(1, [down0])
    up0 = up_step(0, back0)
    feed = cut(2, [down1, up1, down0])
    square0 = attn_grad_step(0, back0)
    square1 = cut(2, [square1])
    up0 = cut(1, [up0])
    feed = deep(cut(3, [feed]))
    square1 = deep(cut(3, [square1]))
    up0 = cut(2, [up0])
    square0 = cut(1, [square0])
    up0 = deep(cut(3, [up0]))
    square0 = cut(2, [square0])
    pair_d = hand_over(summed(feed, 0), summed(feed, 2))
    order.also(square1[1])
    square0 = deep(cut(3, [square0]))
    cur_d, got_d = both_parts(pair_d)
    pair_u = hand_over(summed(feed, 1), summed(up0, 0))
    b, e = summed(square1, 0), summed(square0, 0)

    chunk = sum(bit[s] << (levels - 1 - s) for s in range(levels))
    at_row = lax.broadcasted_iota(jnp.int32, e.shape, 2)
    at_col = lax.broadcasted_iota(jnp.int32, e.shape, 3)
    share = vector_share(d, 2 * dp)
    matrix_rows = (at_row < chunk_rows) & (at_col < half) & (chunk >= 3 * dp // 4)
    vector_row = (at_row >= chunk_rows) & (chunk * share >= VBIAS * d) & (chunk * share < VBIAS * d + half)
    b = jnp.where(matrix_rows | (vector_row & on_first), e, b)
    pair_a = hand_over(b, e)

    cur_d = grow(3, cur_d, got_d)
    got_d = exchange(cur_d, dp, 1)
    cur_u, got_u = both_parts(pair_u)
    cur_d = grow(1, cur_d, got_d)
    far_d = exchange(cur_d, dp, 2)
    side_d = exchange(cur_d, dp, 0)
    cur_a, got_a = both_parts(pair_a)
    cur_u = grow(3, cur_u, got_u)
    got_u = exchange(cur_u, dp, 1)
    y = feed_down(1, sec, a1, order.tie(m), vec[1], w)
    order.mark(y)
    y_moved = to_second(y)
    cur_a = grow(3, cur_a, got_a)
    got_a = exchange(cur_a, dp, 1)
    order.also(far_d, side_d)
    last_d = exchange(order.tie(far_d), dp, 0)
    cur_u = grow(1, cur_u, got_u)
    far_u = exchange(cur_u, dp, 2)
    side_u = exchange(cur_u, dp, 0)
    order.also(y_moved)
    cur_a = grow(1, cur_a, got_a)
    far_a = exchange(cur_a, dp, 2)
    side_a = exchange(cur_a, dp, 0)

    all_columns = slice(None)
    block = ff // 16
    order.also(far_u, side_u)
    last_u = exchange(order.tie(far_u), dp, 0)
    down_grad, = assemble(
        scalars, (order.tie(cur_d), far_d, side_d, last_d), chunk_rows, [(ff, d)],
        lambda outs, part, t: [(all_columns, outs[0].at[pl.ds((8 * part + t) * block, block), :])], "assemble_down")
    order.mark(down_grad, far_a, side_a)
    last_a = exchange(order.tie(far_a), dp, 0)
    up_grad, = assemble(
        scalars, (order.tie(cur_u), far_u, side_u, last_u), chunk_rows, [(d, ff)],
        lambda outs, part, t: [(all_columns, outs[0].at[pl.ds(t % 4 * block, block), pl.ds((2 * part + t // 4) * d, d)])],
        "assemble_up")
    order.mark(up_grad)

    def square_targets(outs, part, t):
        at = pl.ds((2 * part + t % 2) * block, block)
        if t // 2 < 3:
            return [(all_columns, outs[t // 2].at[at, :])]
        return [(pl.ds(half, half), outs[3].at[at, :])]

    def vectors(s_ref, chunks, wide, outs, sems):
        for part in range(2):
            @pl.when(s_ref[0] == part)
            def _():
                moves = [pltpu.make_async_copy(wide.at[8 * part + 6 + i, :, pl.ds(0, half)],
                                               outs[4].at[pl.ds(i * block, block), :], sems[i]) for i in range(2)]
                for move in moves:
                    move.start()
                for move in moves:
                    move.wait()
        lines = outs[5]
        for part in range(2):
            for t in range(8):
                rows_of = chunks(part, t)
                for i in range(dp // 8):
                    at = ((part * 8 + t) * (dp // 8) + i) * share
                    if at < VEC_ROWS * d:
                        lines[at // d:at // d + 1, at % d:at % d + share] = rows_of[i, chunk_rows:chunk_rows + 1, :share].astype(f32)
        for i, row in enumerate((GAIN1, BIAS1, QBIAS, OBIAS, GAIN2, BIAS2, DBIAS)):
            outs[6 + i][...] = lines[row:row + 1, :]
        outs[13][...] = lines[VBIAS:VBIAS + 1, half:]
        for i in range(ff // d):
            outs[14][:, i * d:(i + 1) * d] = lines[UBIAS + i:UBIAS + i + 1, :]

    (out_grad, query_grad, key_grad, value_grad, first_full, lines, gain1_grad, bias1_grad, qbias_grad, obias_grad,
     gain2_grad, bias2_grad, dbias_grad, vbias_grad, ubias_grad) = assemble(
        scalars, (order.tie(cur_a), far_a, side_a, last_a), chunk_rows,
        [(d, d)] * 3 + [(d, half), (d // 2, half)] + [(VEC_ROWS, d)] + [(1, d)] * 7 + [(1, half), (1, ff)],
        square_targets, "assemble_attn", vectors, [VMEM] * 10)

    spot_half = lambda t: jnp.where(on_first, t[:t.shape[0] // 2], t[t.shape[0] // 2:])
    block_ends = jnp.where(on_first, jnp.concatenate([dx0, dx_moved], axis=0),
                           jnp.concatenate([y_moved, y], axis=0))[None]
    return (
        block_ends,
        gain1_grad,
        bias1_grad,
        query_grad[None],
        qbias_grad,
        key_grad[None],
        value_grad[None],
        vbias_grad,
        first_full,
        spot_half(lines[VBIAS, :half]),
        out_grad[None],
        obias_grad,
        gain2_grad,
        bias2_grad,
        up_grad[None],
        ubias_grad,
        down_grad[None],
        dbias_grad,
    )


def solution(mesh):
    stacked = P("section", None, None)
    vector = P("section", None)
    return jax.shard_map(
        local,
        mesh=mesh,
        in_specs=(
            P("section", "dp", None), P("dp", None),
            vector, vector, stacked, vector, stacked, stacked, vector, P(), P(),
            stacked, vector, vector, vector, stacked, vector, stacked, vector,
        ),
        out_specs=(
            P("section", "dp", None),
            vector, vector, stacked, vector, stacked, stacked, vector, P("section"), P("section"),
            stacked, vector, vector, vector, stacked, vector, stacked, vector,
        ),
        check_vma=False,
    )
```

```python
import functools

import jax
import jax.numpy as jnp
from jax import lax
from jax.experimental import pallas as pl
from jax.experimental.pallas import tpu as pltpu
from jax.sharding import PartitionSpec as P

HEADS = 12
HEAD = 64
PAIR = 2 * HEAD
VMEM_BYTES = 64 * 1024 * 1024

eps_norm = 1e-05
neg_fill = -1e30

f32 = jnp.float32
bf16 = jnp.bfloat16

NN = (((1,), (0,)), ((), ()))
NT = (((1,), (1,)), ((), ()))
TN = (((0,), (0,)), ((), ()))

ANY = pl.BlockSpec(memory_space=pl.ANY)
SMEM = pl.BlockSpec(memory_space=pltpu.SMEM)
VMEM = pl.BlockSpec(memory_space=pltpu.VMEM)

GAIN1, BIAS1, QBIAS, VBIAS, OBIAS, GAIN2, BIAS2, DBIAS, UBIAS = range(9)
VEC_ROWS = 16

SMALL_STEP = 8


def mm(left, right, dims=NN):
    return lax.dot_general(left, right, dims, preferred_element_type=f32)


def sds(shape, dtype):
    return jax.ShapeDtypeStruct(shape, dtype)


def params():
    return pltpu.CompilerParams(vmem_limit_bytes=VMEM_BYTES)


def cost(micros):
    return pl.CostEstimate(flops=int(micros * 1.15e9), bytes_accessed=1, transcendentals=0)


def start_fetch(mine, own, recv, dst, sem):
    @pl.when(mine)
    def _():
        pltpu.make_async_copy(own, dst, sem).start()

    @pl.when(jnp.logical_not(mine))
    def _():
        pltpu.make_async_copy(recv, dst, sem).start()


def wait_fetch(own, dst, sem):
    pltpu.make_async_copy(own, dst, sem).wait()


def norm_parts(rows):
    centre = jnp.mean(rows, axis=-1, keepdims=True)
    centred = rows - centre
    spread = jnp.mean(centred * centred, axis=-1, keepdims=True)
    factor = lax.rsqrt(spread + eps_norm)
    return centred * factor, factor


def norm_back(grad_t, n, w):
    return w * (
        grad_t
        - jnp.mean(grad_t, axis=-1, keepdims=True)
        - n * jnp.mean(grad_t * n, axis=-1, keepdims=True)
    )


def first_keys(sec_ref, lengths_ref, shape, dim):
    at = lax.broadcasted_iota(jnp.int32, shape, dim)
    begin = jnp.zeros(shape, jnp.int32)
    cut = 0
    for i in range(lengths_ref.shape[1]):
        cut = cut + lengths_ref[sec_ref[0], i]
        begin = jnp.where(at >= cut, cut, begin)
    return begin


def row_sum(x):
    return jnp.sum(x, axis=0, keepdims=True)


def attend(rows, q_s, k_s, v_s, o_s, lse_s, bias_s):
    lane = lax.broadcasted_iota(jnp.int32, (1, PAIR), 1)
    step = rows // 2

    def pair(hp, carry):
        ls = pl.ds(pl.multiple_of(hp * PAIR, PAIR), PAIR)
        q2 = q_s[:, ls] * jnp.asarray(HEAD ** -0.5, bf16)
        k2 = k_s[:, ls]
        v2 = v_s[:, ls]
        zero = jnp.zeros((), bf16)
        for qb in range(2):
            qr = slice(qb * step, (qb + 1) * step)
            keys = (qb + 1) * step
            mixed = None
            for j in range(2):
                inside = (lane >= j * HEAD) & (lane < (j + 1) * HEAD)
                kh = jnp.where(inside, k2[:keys], zero)
                vh = jnp.where(inside, v2[:keys], zero)
                s = mm(q2[qr], kh, NT) + bias_s[qr, :keys]
                peak = jnp.max(s, axis=-1, keepdims=True)
                p = jnp.exp(s - peak)
                total = jnp.sum(p, axis=-1, keepdims=True)
                low = (p * (1.0 / total)).astype(bf16)
                part = mm(low, vh)
                mixed = part if mixed is None else mixed + part
                lse_s[qr, :] = jnp.where(lane == 2 * hp + j, peak + jnp.log(total), lse_s[qr, :])
            o_s[qr, ls] = mixed.astype(bf16)
        return carry

    lse_s[...] = jnp.zeros(lse_s.shape, f32)
    lax.fori_loop(0, HEADS // 2, pair, 0)


def attn_forward_steps(layer, sec_ref, x_ref, r_ref, start_ref, vec_ref, weights, outs, held, in_sem, out_sem):
    (qw_o, qw_r, kw_o, kw_r, vw_o, vw_r, fw, ow_o, ow_r), (wq, wk, wv, wo) = weights
    h_out, q_out, k_out, v_out, o_out, m_out, e_out, lse_out, sent_out = outs
    h_s, q_s, k_s, v_s, o_s, m_s, e_s, lse_s, lset_s, bias_s = held
    mine = sec_ref[0] == layer
    rows = x_ref.shape[0]
    half = fw.shape[1]
    copies = []

    def fetch():
        start_fetch(mine, qw_o, qw_r, wq, in_sem.at[0])
        start_fetch(mine, kw_o, kw_r, wk, in_sem.at[1])
        start_fetch(mine, vw_o, vw_r, wv.at[:, half:], in_sem.at[2])
        if layer == 0:
            pltpu.make_async_copy(fw, wv.at[:, :half], in_sem.at[3]).start()
        start_fetch(mine, ow_o, ow_r, wo, in_sem.at[4])

    def put(src, dst):
        copy = pltpu.make_async_copy(src, dst, out_sem.at[len(copies)])
        copy.start()
        copies.append(copy)

    def run():
        wide = x_ref[...].astype(f32)
        n, _ = norm_parts(wide)
        h_s[...] = (n * vec_ref[GAIN1:GAIN1 + 1, :] + vec_ref[BIAS1:BIAS1 + 1, :]).astype(bf16)
        put(h_s, h_out)
        theirs = pl.ds(pl.multiple_of((1 - sec_ref[0]) * half, half), half)
        put(h_s.at[:, theirs], sent_out.at[0, :, half:])
        at_row = lax.broadcasted_iota(jnp.int32, (rows, rows), 0)
        at_col = lax.broadcasted_iota(jnp.int32, (rows, rows), 1)
        bias_s[...] = jnp.where((at_col <= at_row) & (at_col >= first_keys(sec_ref, start_ref, (rows, 1), 0)), 0.0, neg_fill)
        wait_fetch(qw_o, wq, in_sem.at[0])
        q_s[...] = (mm(h_s[...], wq[...]) + vec_ref[QBIAS:QBIAS + 1, :]).astype(bf16)
        put(q_s, q_out)
        wait_fetch(kw_o, wk, in_sem.at[1])
        k_s[...] = mm(h_s[...], wk[...]).astype(bf16)
        put(k_s, k_out)
        wait_fetch(vw_o, wv.at[:, half:], in_sem.at[2])
        if layer == 0:
            wait_fetch(fw, wv.at[:, :half], in_sem.at[3])
            v_s[...] = (mm(h_s[...], wv[...]) + vec_ref[VBIAS:VBIAS + 1, :]).astype(bf16)
        else:
            v_s[:, :half] = r_ref[:, :half]
            v_s[:, half:] = (mm(h_s[...], wv[:, half:]) + vec_ref[VBIAS:VBIAS + 1, half:]).astype(bf16)
        put(v_s, v_out)
        attend(rows, q_s, k_s, v_s, o_s, lse_s, bias_s)
        put(o_s, o_out)
        put(o_s.at[:, theirs], sent_out.at[0, :, :half])
        lset_s[...] = jnp.transpose(lse_s[...])[:VEC_ROWS, :]
        put(lset_s, lse_out)
        wait_fetch(ow_o, wo, in_sem.at[4])
        m = x_ref[...].astype(f32) + (mm(o_s[...], wo[...]) + vec_ref[OBIAS:OBIAS + 1, :])
        m_s[...] = m
        put(m_s, m_out)
        n, _ = norm_parts(m)
        e_s[...] = (n * vec_ref[GAIN2:GAIN2 + 1, :] + vec_ref[BIAS2:BIAS2 + 1, :]).astype(bf16)
        put(e_s, e_out)
        put(e_s, sent_out.at[1])

    return fetch, run, copies


def attn_forward_kernel(layer, sec_ref, start_ref, vec_ref, own_ref, arrived_ref, *refs):
    x_out, x_s, x_sem = refs[18], refs[33], refs[34]
    rows = x_s.shape[0]
    slot = pl.ds(pl.multiple_of(sec_ref[0] * rows, rows), rows)
    start_fetch(sec_ref[0] == 0, own_ref.at[slot, :], arrived_ref.at[slot, :], x_s, x_sem.at[0])
    fetch, run, copies = attn_forward_steps(
        layer, sec_ref, x_s, None, start_ref, vec_ref, (refs[:9], refs[19:23]), refs[9:18], refs[23:33],
        refs[35], refs[36])
    fetch()
    wait_fetch(own_ref.at[slot, :], x_s, x_sem.at[0])
    keep = pltpu.make_async_copy(x_s, x_out, x_sem.at[1])
    keep.start()
    run()
    for copy in copies:
        copy.wait()
    keep.wait()


def attn_forward_shapes(rows, d):
    act = sds((rows, d), bf16)
    wbuf = pltpu.VMEM((d, d), bf16)
    abuf = pltpu.VMEM((rows, d), bf16)
    outs = [act, act, act, act, act, sds((rows, d), f32), act, sds((VEC_ROWS, rows), f32), sds((2, rows, d), bf16)]
    scratch = [wbuf, wbuf, wbuf, wbuf, abuf, abuf, abuf, abuf, abuf,
               pltpu.VMEM((rows, d), f32), abuf, pltpu.VMEM((rows, PAIR), f32),
               pltpu.VMEM((VEC_ROWS, rows), f32), pltpu.VMEM((rows, rows), f32),
               pltpu.SemaphoreType.DMA((5,)), pltpu.SemaphoreType.DMA((11,))]
    return outs, scratch


def attn_forward(layer, sec, start, vec, own, arrived, w):
    rows, d = own.shape[0] // 2, own.shape[1]
    outs, scratch = attn_forward_shapes(rows, d)
    return pl.pallas_call(
        functools.partial(attn_forward_kernel, layer),
        out_shape=outs + [sds((rows, d), bf16)],
        in_specs=[SMEM, SMEM, VMEM] + [ANY] * 11,
        out_specs=[ANY] * 10,
        scratch_shapes=scratch[:-2] + [pltpu.VMEM((rows, d), bf16), pltpu.SemaphoreType.DMA((2,))] + scratch[-2:],
        compiler_params=params(),
        cost_estimate=cost(80),
        name="attn_forward",
    )(sec, start, vec, own, arrived, w["qo"], w["qr"], w["ko"], w["kr"], w["vo"], w["vr"], w["f"], w["oo"], w["or"])


def gelu(u):
    half_u = 0.5 * u
    return half_u + half_u * jnp.tanh(u * (0.7978845608028654 + 0.035677408136300125 * (u * u)))


def middle_kernel(blk, sec_ref, e_ref, m_ref, r_ref, start_ref, vec0_ref, vec1_ref, *refs):
    up_o, up_r, dn_o, dn_r = refs[:4]
    attn_w, outs = refs[4:13], refs[13:28]
    wu0, wd0, wu1, u_s, a_s, f_s, x_s, acc, up_sem, put_sem = refs[28:38]
    wbufs, held, in_sem, out_sem = refs[38:42], refs[42:52], refs[52], refs[53]
    u0_out, a0_out, x_out, u1_out, a1_out, sent_out = outs[:6]
    steps = wu0.shape[0]
    section = sec_ref[0]
    cols = [pl.ds(b * blk, blk) for b in range(steps)]
    for b in range(steps):
        start_fetch(section == 0, up_o.at[:, cols[b]], up_r.at[:, cols[b]], wu0.at[b], up_sem.at[0, b])
    for b in range(steps):
        start_fetch(section == 0, dn_o.at[cols[b], :], dn_r.at[cols[b], :], wd0.at[b], up_sem.at[1, b])
    fetch, run, copies = attn_forward_steps(
        1, sec_ref, x_s, r_ref, start_ref, vec1_ref, (attn_w, wbufs), outs[6:], held, in_sem, out_sem)
    fetch()
    for b in range(steps):
        start_fetch(section == 1, up_o.at[:, cols[b]], up_r.at[:, cols[b]], wu1.at[b], up_sem.at[2, b])
    own = []

    def put(src, dst):
        copy = pltpu.make_async_copy(src, dst, put_sem.at[len(own)])
        copy.start()
        own.append(copy)

    def expand(layer, b, source, weights, vec_ref):
        wait_fetch(up_o.at[:, cols[0]], weights.at[b], up_sem.at[2 * layer, b])
        f_s[b % 2] = mm(source[...], weights[b]) + vec_ref[UBIAS + b:UBIAS + b + 1, :]

    def activate(layer, b, u_out, a_out):
        u = f_s[b % 2]
        u_s[layer, b] = u.astype(bf16)
        a_s[layer, b] = gelu(u).astype(bf16)
        put(u_s.at[layer, b], u_out.at[:, cols[b]])
        put(a_s.at[layer, b], a_out.at[:, cols[b]])

    expand(0, 0, e_ref, wu0, vec0_ref)
    for b in range(steps):
        if b + 1 < steps:
            expand(0, b + 1, e_ref, wu0, vec0_ref)
        activate(0, b, u0_out, a0_out)
        wait_fetch(dn_o.at[cols[0], :], wd0.at[b], up_sem.at[1, b])
        part = mm(a_s[0, b], wd0[b])
        acc[...] = part if b == 0 else acc[...] + part
    x_s[...] = (m_ref[...] + (acc[...] + vec0_ref[DBIAS:DBIAS + 1, :])).astype(bf16)
    put(x_s, x_out)
    run()
    expand(1, 0, held[6], wu1, vec1_ref)
    for b in range(steps):
        if b + 1 < steps:
            expand(1, b + 1, held[6], wu1, vec1_ref)
        activate(1, b, u1_out, a1_out)
    theirs = (1 - section) * (steps // 2)
    for b in range(steps // 2):
        for layer in range(2):
            put(a_s.at[layer, theirs + b], sent_out.at[layer, :, cols[b]])
    for copy in own + copies:
        copy.wait()


def middle(sec, e, m, r, start, vec, w):
    rows, d = e.shape
    ff = w["uo"].shape[1]
    blk = d
    n = ff // blk
    outs, scratch = attn_forward_shapes(rows, d)
    wide = sds((rows, ff), bf16)
    return pl.pallas_call(
        functools.partial(middle_kernel, blk),
        out_shape=[wide, wide, sds((rows, d), bf16), wide, wide, sds((2, rows, ff // 2), bf16)] + outs,
        in_specs=[SMEM] + [VMEM] * 3 + [SMEM] + [VMEM] * 2 + [ANY] * 13,
        out_specs=[ANY] * 15,
        scratch_shapes=[pltpu.VMEM((n, d, blk), bf16), pltpu.VMEM((n, blk, d), bf16), pltpu.VMEM((n, d, blk), bf16),
                        pltpu.VMEM((2, n, rows, blk), bf16), pltpu.VMEM((2, n, rows, blk), bf16),
                        pltpu.VMEM((2, rows, blk), f32), pltpu.VMEM((rows, d), bf16), pltpu.VMEM((rows, d), f32),
                        pltpu.SemaphoreType.DMA((3, n)), pltpu.SemaphoreType.DMA((4 * n + 1 + n,))] + scratch,
        compiler_params=params(),
        cost_estimate=cost(80),
        name="middle",
    )(sec, e, m, r, start, vec[0], vec[1], w["uo"], w["ur"], w["do"], w["dr"],
      w["qo"], w["qr"], w["ko"], w["kr"], w["vo"], w["vr"], w["f"], w["oo"], w["or"])


def theirs_at(steps):
    half = steps // 2

    def index(j, s):
        return (0, jnp.where(s[0] == 0, jnp.maximum(j - half, 0), jnp.minimum(j, half - 1)))
    return index


def feed_down_kernel(layer, blk, sec_ref, a_ref, m_ref, vec_ref, dn_o, dn_r, z_ref, wd, acc, sem):
    j = pl.program_id(0)
    steps = pl.num_programs(0)
    mine = sec_ref[0] == layer

    @pl.when(j == 0)
    def _():
        for b in range(dn_o.shape[0] // blk):
            cols = pl.ds(b * blk, blk)
            start_fetch(mine, dn_o.at[cols, :], dn_r.at[cols, :], wd.at[b], sem.at[b])

    wait_fetch(dn_o.at[pl.ds(0, blk), :], wd.at[j], sem.at[j])
    part = mm(a_ref[...], wd[j])

    @pl.when(j == 0)
    def _():
        acc[...] = part

    @pl.when((j > 0) & (j < steps - 1))
    def _():
        acc[...] += part

    @pl.when(j == steps - 1)
    def _():
        z_ref[...] = (m_ref[...] + (acc[...] + part + vec_ref[DBIAS:DBIAS + 1, :])).astype(bf16)


def feed_down(layer, sec, a, m, vec, w):
    rows, ff = a.shape
    d = m.shape[1]
    blk = d
    n = ff // blk
    return pl.pallas_call(
        functools.partial(feed_down_kernel, layer, blk),
        grid=(n,),
        out_shape=sds((rows, d), bf16),
        in_specs=[SMEM, pl.BlockSpec((rows, blk), lambda j: (0, j)), VMEM, VMEM, ANY, ANY],
        out_specs=pl.BlockSpec((rows, d), lambda j: (0, 0)),
        scratch_shapes=[pltpu.VMEM((n, blk, d), bf16), pltpu.VMEM((rows, d), f32), pltpu.SemaphoreType.DMA((n,))],
        compiler_params=params(),
        cost_estimate=cost(2),
        name="feed_down",
    )(sec, a, m, vec, w["do"], w["dr"])


def layer_backward_kernel(layer, blk, sec_ref, dz_ref, m_ref, lse_ref, start_ref, vec_ref, dr2_ref,
                          u_in, x_in, q_in, k_in, v_in, o_in,
                          up_o, up_r, dn_o, dn_r, qw_o, qw_r, kw_o, kw_r, vw_o, vw_r, fw, ow_o, ow_r,
                          du_out, sent_out, bundle_out, shared_ref, small_ref,
                          wu, wd, wq, wk, wv, wo, u_s, x_s, q_ref, k_ref, v_ref, o_ref, du_s, da_s, acc, dm_s,
                          bundle_ref, do_s, delta_s, bias_s, feed_sem, sem, in_sem, out_sem):
    mine = sec_ref[0] == layer
    rows, d = dz_ref.shape
    half = fw.shape[1]
    steps = wu.shape[0]
    cols = [pl.ds(b * blk, blk) for b in range(steps)]
    for b in range(steps):
        start_fetch(mine, dn_o.at[cols[b], :], dn_r.at[cols[b], :], wd.at[b], feed_sem.at[0, b])
        pltpu.make_async_copy(u_in.at[:, cols[b]], u_s.at[b], feed_sem.at[2, b]).start()
        start_fetch(mine, up_o.at[:, cols[b]], up_r.at[:, cols[b]], wu.at[b], feed_sem.at[1, b])
    start_fetch(mine, ow_o, ow_r, wo, sem.at[4])
    loads = [pltpu.make_async_copy(src, dst, in_sem.at[i]) for i, (src, dst) in enumerate(
        ((q_in, q_ref), (k_in, k_ref), (v_in, v_ref), (o_in, o_ref), (x_in, x_s)))]
    for load in loads:
        load.start()
    start_fetch(mine, qw_o, qw_r, wq, sem.at[0])
    start_fetch(mine, kw_o, kw_r, wk, sem.at[1])
    start_fetch(mine, vw_o, vw_r, wv.at[:, half:], sem.at[2])
    if layer == 0:
        pltpu.make_async_copy(fw, wv.at[:, :half], sem.at[3]).start()
    copies = []

    def put(src, dst):
        copy = pltpu.make_async_copy(src, dst, out_sem.at[len(copies)])
        copy.start()
        copies.append(copy)

    small_ref[...] = jnp.zeros(small_ref.shape, f32)

    def expand(b):
        wait_fetch(dn_o.at[cols[0], :], wd.at[b], feed_sem.at[0, b])
        da_s[b % 2] = mm(dz_ref[...], wd[b], NT)

    def activate(b):
        pltpu.make_async_copy(u_in.at[:, cols[b]], u_s.at[b], feed_sem.at[2, b]).wait()
        u = u_s[b].astype(f32)
        sq = u * u
        th = jnp.tanh(u * (0.7978845608028654 + 0.035677408136300125 * sq))
        slope = 0.5 + 0.5 * th + (0.5 * u) * (1.0 - th * th) * (0.7978845608028654 + 0.10703222440890037 * sq)
        du = (slope * da_s[b % 2]).astype(bf16)
        du_s[b] = du
        small_ref[UBIAS + b:UBIAS + b + 1, :] = row_sum(du.astype(f32))
        put(du_s.at[b], du_out.at[:, cols[b]])

    expand(0)
    for b in range(steps):
        if b + 1 < steps:
            expand(b + 1)
        activate(b)
        wait_fetch(up_o.at[:, cols[0]], wu.at[b], feed_sem.at[1, b])
        part = mm(du_s[b], wu[b], NT)
        acc[...] = part if b == 0 else acc[...] + part
    theirs = (1 - sec_ref[0]) * (steps // 2)
    for b in range(steps // 2):
        put(du_s.at[theirs + b], sent_out.at[b])
    de = acc[...]
    n, w = norm_parts(m_ref[...])
    dz = dz_ref[...].astype(f32)
    dm_s[...] = dz + norm_back(de * vec_ref[GAIN2:GAIN2 + 1, :], n, w)
    small_ref[GAIN2:GAIN2 + 1, :] = row_sum(de * n)
    small_ref[BIAS2:BIAS2 + 1, :] = row_sum(de)
    small_ref[DBIAS:DBIAS + 1, :] = row_sum(dz)

    low_ref, dq_ref, dk_ref, dv_ref, dx_ref = (bundle_ref.at[pl.ds(i * rows, rows), :] for i in range(5))
    low_ref[...] = dm_s[...].astype(bf16)
    at_key = lax.broadcasted_iota(jnp.int32, (rows, rows), 0)
    at_query = lax.broadcasted_iota(jnp.int32, (rows, rows), 1)
    bias_s[...] = jnp.where((at_key <= at_query) & (at_key >= first_keys(sec_ref, start_ref, (1, rows), 1)), 0.0, neg_fill)
    wait_fetch(ow_o, wo, sem.at[4])
    do = mm(low_ref[...], wo[...], NT).astype(bf16)
    do_s[...] = do
    for load in loads:
        load.wait()
    head_row = lax.broadcasted_iota(jnp.int32, (VEC_ROWS, d), 0)
    head_col = lax.broadcasted_iota(jnp.int32, (VEC_ROWS, d), 1) // HEAD
    pick = (head_row == head_col).astype(f32)
    delta_s[...] = lax.dot_general(pick, do.astype(f32) * o_ref[...].astype(f32), NT,
                                   precision=lax.Precision.HIGHEST, preferred_element_type=f32)
    lane = lax.broadcasted_iota(jnp.int32, (1, PAIR), 1)
    step = rows // 2
    scale = HEAD ** -0.5
    zero = jnp.zeros((), bf16)

    def pair(hp, carry):
        ls = pl.ds(pl.multiple_of(hp * PAIR, PAIR), PAIR)
        q2 = q_ref[:, ls] * jnp.asarray(scale, bf16)
        k2 = k_ref[:, ls]
        v2 = v_ref[:, ls]
        do2 = do_s[:, ls]
        dq_parts = []
        for kb in range(2):
            kr = slice(kb * step, (kb + 1) * step)
            first = kb * step
            dk = dv = dq = None
            for j in range(2):
                inside = (lane >= j * HEAD) & (lane < (j + 1) * HEAD)
                kh = jnp.where(inside, k2[kr], zero)
                vh = jnp.where(inside, v2[kr], zero)
                qh = jnp.where(inside, q2[first:], zero)
                doh = jnp.where(inside, do2[first:], zero)
                row = pl.ds(2 * hp + j, 1)
                st = mm(kh, qh, NT) + bias_s[kr, first:]
                pt = jnp.exp(st - lse_ref[row, first:])
                dpt = mm(vh, doh, NT)
                dst = (pt * (dpt - delta_s[row, first:])).astype(bf16)
                dv_j = mm(pt.astype(bf16), doh)
                dk_j = mm(dst, qh)
                dq_j = mm(dst, kh, TN)
                dk = dk_j if dk is None else dk + dk_j
                dv = dv_j if dv is None else dv + dv_j
                dq = dq_j if dq is None else dq + dq_j
            dk_ref[kr, ls] = dk.astype(bf16)
            if layer == 1:
                dv_ref[kr, ls] = dv.astype(bf16)

                @pl.when(hp < HEADS // 4)
                def _():
                    shared_ref[kr, ls] = dv
            else:
                extra = jnp.where(hp < HEADS // 4, dr2_ref[kr, pl.ds(pl.multiple_of((hp % (HEADS // 4)) * PAIR, PAIR), PAIR)], 0.0)
                dv_ref[kr, ls] = (dv + extra).astype(bf16)
            dq_parts.append(dq)
        dq_ref[:step, ls] = (dq_parts[0][:step] * scale).astype(bf16)
        dq_ref[step:, ls] = ((dq_parts[0][step:] + dq_parts[1]) * scale).astype(bf16)
        return carry

    if layer == 0:
        shared_ref[...] = jnp.zeros(shared_ref.shape, f32)
    lax.fori_loop(0, HEADS // 2, pair, 0)
    put(bundle_ref.at[pl.ds(0, 4 * rows), :], bundle_out.at[pl.ds(0, 4 * rows), :])

    wait_fetch(qw_o, wq, sem.at[0])
    dh = mm(dq_ref[...], wq[...], NT)
    wait_fetch(kw_o, wk, sem.at[1])
    dh = dh + mm(dk_ref[...], wk[...], NT)
    wait_fetch(vw_o, wv.at[:, half:], sem.at[2])
    if layer == 0:
        wait_fetch(fw, wv.at[:, :half], sem.at[3])
        dh = dh + mm(dv_ref[...], wv[...], NT)
    else:
        dh = dh + mm(dv_ref[:, half:], wv[:, half:], NT)
    n, w = norm_parts(x_s[...].astype(f32))
    dx_ref[...] = (dm_s[...] + norm_back(dh * vec_ref[GAIN1:GAIN1 + 1, :], n, w)).astype(bf16)
    small_ref[GAIN1:GAIN1 + 1, :] = row_sum(dh * n)
    small_ref[BIAS1:BIAS1 + 1, :] = row_sum(dh)
    small_ref[QBIAS:QBIAS + 1, :] = row_sum(dq_ref[...].astype(f32))
    small_ref[VBIAS:VBIAS + 1, :] = row_sum(dv_ref[...].astype(f32))
    small_ref[OBIAS:OBIAS + 1, :] = row_sum(low_ref[...].astype(f32))
    bundle_ref[5 * rows:, :] = small_ref[...].astype(bf16)
    put(bundle_ref.at[pl.ds(4 * rows, rows + VEC_ROWS), :], bundle_out.at[pl.ds(4 * rows, rows + VEC_ROWS), :])
    for copy in copies:
        copy.wait()


def layer_backward(layer, sec, dz, dz_at, t, start_row, vec, dr2, w):
    rows, ff = t["u"].shape
    d = t["m"].shape[1]
    half = w["f"].shape[1]
    blk = d
    n = ff // blk
    wbuf = pltpu.VMEM((d, d), bf16)
    act = pltpu.VMEM((rows, d), bf16)
    wide = pltpu.VMEM((rows, d), f32)
    blocks = pltpu.VMEM((n, rows, blk), bf16)
    dma = pltpu.SemaphoreType.DMA
    bundle = (5 * rows + VEC_ROWS, d)
    return pl.pallas_call(
        functools.partial(layer_backward_kernel, layer, blk),
        grid=(1,),
        out_shape=[sds((rows, ff), bf16), sds((n // 2, rows, blk), bf16), sds(bundle, bf16), sds((rows, half), f32),
                   sds((VEC_ROWS, d), f32)],
        in_specs=[SMEM, pl.BlockSpec((rows, d), lambda i: (dz_at, 0)), VMEM, VMEM, SMEM, VMEM, VMEM] + [ANY] * 19,
        out_specs=[ANY] * 3 + [VMEM] * 2,
        scratch_shapes=[pltpu.VMEM((n, d, blk), bf16), pltpu.VMEM((n, blk, d), bf16), wbuf, wbuf, wbuf, wbuf,
                        blocks, act, act, act, act, act, blocks, pltpu.VMEM((2, rows, blk), f32), wide, wide,
                        pltpu.VMEM(bundle, bf16), act, pltpu.VMEM((VEC_ROWS, rows), f32), pltpu.VMEM((rows, rows), f32),
                        dma((3, n)), dma((5,)), dma((5,)), dma((n + n // 2 + 2,))],
        compiler_params=params(),
        cost_estimate=cost(80),
        name="layer_backward",
    )(sec, dz, t["m"], t["lse"], start_row, vec, dr2, t["u"], t["x"], t["q"], t["k"], t["v"], t["o"],
      w["uo"], w["ur"], w["do"], w["dr"],
      w["qo"], w["qr"], w["ko"], w["kr"], w["vo"], w["vr"], w["f"], w["oo"], w["or"])


def store_chunks(ref, value):
    c, r, _ = ref.shape
    for i in range(c):
        ref[i] = value[i * r:(i + 1) * r].astype(bf16)


def quarter_of(g, s):
    return 2 * jnp.where(g < 2, 1 - s[1], s[1]) + g % 2


def quarters(kernel, scalars, in_specs, operands, shape, name):
    per = shape[0] // 2
    return pl.pallas_call(
        kernel,
        grid_spec=pltpu.PrefetchScalarGridSpec(
            num_scalar_prefetch=1, grid=(4,), in_specs=in_specs,
            out_specs=[pl.BlockSpec((per,) + shape[1:], lambda g, s: (jnp.minimum(g, 1), 0, 0)),
                       pl.BlockSpec((per,) + shape[1:], lambda g, s: (jnp.maximum(g - 2, 0), 0, 0))]),
        out_shape=[sds(shape, bf16)] * 2,
        compiler_params=params(),
        cost_estimate=cost(80),
        name=name,
    )(scalars, *operands)


def store_quarter(send_ref, keep_ref, value):
    g = pl.program_id(0)

    @pl.when(g < 2)
    def _():
        store_chunks(send_ref, value)

    @pl.when(g >= 2)
    def _():
        store_chunks(keep_ref, value)


def down_gradient(scalars, a, a_got, dz, dz_got, dz_at, chunk_rows):
    a_got, a_at = a_got
    rows, ff = a.shape
    d = dz.shape[1]
    q = d // 2

    def kernel(s_ref, a_ref, b_ref, x_ref, y_ref, send_ref, keep_ref):
        store_quarter(send_ref, keep_ref, mm(a_ref[...], x_ref[...], TN) + mm(b_ref[0], y_ref[...], TN))

    whole = pl.BlockSpec((rows, d), lambda g, s: (dz_at, 0))
    return quarters(
        kernel, scalars,
        [pl.BlockSpec((rows, q), lambda g, s: (0, 4 * s[0] + quarter_of(g, s))),
         pl.BlockSpec((1, rows, q), lambda g, s: (a_at, 0, quarter_of(g, s))), whole, whole],
        (a, a_got, dz, dz_got), (2 * q // chunk_rows, chunk_rows, d), "down_gradient")


def up_gradient(scalars, e, sent_got, du, du_got, chunk_rows):
    rows, ff = du.shape
    d = e.shape[1]
    q = d // 2

    def kernel(s_ref, e_ref, f_ref, du_ref, dg_ref, send_ref, keep_ref):
        store_quarter(send_ref, keep_ref, mm(e_ref[...], du_ref[...], TN) + mm(f_ref[0], dg_ref[0], TN))

    return quarters(
        kernel, scalars,
        [pl.BlockSpec((rows, q), lambda g, s: (0, g % 2)),
         pl.BlockSpec((1, rows, q), lambda g, s: (1, 0, g % 2)),
         pl.BlockSpec((rows, d), lambda g, s: (0, 2 * s[0] + quarter_of(g, s) // 2)),
         pl.BlockSpec((1, rows, d), lambda g, s: (quarter_of(g, s) // 2, 0, 0))],
        (e, sent_got, du, du_got), (2 * q // chunk_rows, chunk_rows, d), "up_gradient")


def vector_share(width, chunks):
    return max(PAIR, VEC_ROWS * width // chunks)


def attn_gradient(scalars, o, h, sent_got, bundle, bundle_got, small, chunk_rows, extra):
    rows, d = o.shape
    q = d // 2
    per = q // chunk_rows
    share = vector_share(d, 8 * per)

    def kernel(s_ref, o_ref, h_ref, l_ref, own_ref, got_ref, small_ref, small_got_ref, send_ref, keep_ref, sum_ref):
        sum_ref[...] = small_ref[...] + small_got_ref[...].astype(f32)
        g = pl.program_id(0)
        which = quarter_of(g, s_ref)
        for i in range(4):
            @pl.when(which == i)
            def _():
                left = o_ref if i == 0 else h_ref
                value = mm(left[...], own_ref[...], TN) + mm(l_ref[0], got_ref[...], TN)
                for side, ref in enumerate((send_ref, keep_ref)):
                    @pl.when(g // 2 == side)
                    def _():
                        ref[:, chunk_rows:, :] = jnp.zeros((per, extra, d), bf16)
                        for c in range(per):
                            ref[c, :chunk_rows, :] = value[c * chunk_rows:(c + 1) * chunk_rows].astype(bf16)
                        for part_index in range(2):
                            @pl.when(s_ref[0] == part_index)
                            def _():
                                for c in range(per):
                                    at = ((4 * part_index + i) * per + c) * share
                                    if at < VEC_ROWS * d:
                                        row = sum_ref[at // d:at // d + 1, at % d:at % d + share]
                                        ref[c, chunk_rows:chunk_rows + 1, :share] = row.astype(bf16)

    part = pl.BlockSpec((rows, q), lambda g, s: (0, s[0]))
    right = pl.BlockSpec((rows, d), lambda g, s: (quarter_of(g, s), 0))
    shape = (2 * per, chunk_rows + extra, d)
    return pl.pallas_call(
        kernel,
        grid_spec=pltpu.PrefetchScalarGridSpec(
            num_scalar_prefetch=1, grid=(4,),
            in_specs=[part, part,
                      pl.BlockSpec((1, rows, q), lambda g, s: (0, 0, jnp.minimum(quarter_of(g, s), 1))),
                      right, right, pl.BlockSpec((VEC_ROWS, d), lambda g, s: (0, 0)),
                      pl.BlockSpec((VEC_ROWS, d), lambda g, s: (5 * rows // VEC_ROWS, 0))],
            out_specs=[pl.BlockSpec((per,) + shape[1:], lambda g, s: (jnp.minimum(g, 1), 0, 0)),
                       pl.BlockSpec((per,) + shape[1:], lambda g, s: (jnp.maximum(g - 2, 0), 0, 0))],
            scratch_shapes=[pltpu.VMEM((VEC_ROWS, d), f32)]),
        out_shape=[sds(shape, bf16)] * 2,
        compiler_params=params(),
        cost_estimate=cost(80),
        name="attn_gradient",
    )(scalars, o, h, sent_got, bundle, bundle_got, small, bundle_got)


AXES = ("section", "dp")
SWAP = [(0, 1), (1, 0)]


def bit_orders(dp):
    bits = list(range(dp.bit_length() - 1))
    return bits, [1, 0] + bits[2:]


def exchange(array, dp, step):
    first, second = bit_orders(dp)
    pairs = [(i, i ^ (1 << first[step])) for i in range(dp)]
    pairs += [(dp + i, dp + (i ^ (1 << second[step]))) for i in range(dp)]
    return lax.ppermute(array, AXES, pairs)


def block_of(chunks, rows):
    best = 1
    for c in range(1, chunks + 1):
        if chunks % c == 0 and c * rows <= 768:
            best = c
    return best


def add_split(bit, parts):
    _, c, r, w = parts[0][0].shape
    counts = [p[0].shape[0] for p in parts]
    n = sum(counts)
    h = c // 2
    cb = block_of(h, r)
    nb = h // cb
    ends = [sum(counts[:i + 1]) for i in range(len(counts))]
    begins = [e - k for e, k in zip(ends, counts)]

    def kernel(s_ref, *refs):
        send_ref, keep_ref = refs[-2:]
        g, i = pl.program_id(0), pl.program_id(1)
        for t in range(len(parts)):
            @pl.when((i >= begins[t]) & (i < ends[t]))
            def _():
                total = (refs[2 * t][...].astype(f32) + refs[2 * t + 1][...].astype(f32)).astype(bf16)

                @pl.when(g == 0)
                def _():
                    send_ref[...] = total

                @pl.when(g == 1)
                def _():
                    keep_ref[...] = total

    def source(t):
        def index(g, i, j, s):
            inside = (i >= begins[t]) & (i < ends[t])
            side = jnp.where(g == 0, 1 - s[0], s[0])
            return (jnp.clip(i - begins[t], 0, counts[t] - 1), jnp.where(inside, side * nb + j, 0), 0, 0)
        return pl.BlockSpec((1, cb, r, w), index)

    def send_at(g, i, j, s):
        return (jnp.where(g == 0, i, n - 1), jnp.where(g == 0, j, nb - 1), 0, 0)

    def keep_at(g, i, j, s):
        return (jnp.where(g == 0, 0, i), jnp.where(g == 0, 0, j), 0, 0)

    flat = [x for p in parts for x in p]
    return pl.pallas_call(
        kernel,
        grid_spec=pltpu.PrefetchScalarGridSpec(
            num_scalar_prefetch=1, grid=(2, n, nb),
            in_specs=[source(t) for t in range(len(parts)) for _ in range(2)],
            out_specs=[pl.BlockSpec((1, cb, r, w), send_at), pl.BlockSpec((1, cb, r, w), keep_at)]),
        out_shape=[sds((n, h, r, w), bf16)] * 2,
        compiler_params=params(),
        cost_estimate=cost(SMALL_STEP),
        name="add_split",
    )(bit, *flat)


def merge(bit, cur, arrived):
    n, c, r, w = cur.shape
    cb = block_of(c, r)
    nb = c // cb

    def kernel(s_ref, a_ref, b_ref, out_ref):
        g = pl.program_id(1)

        @pl.when(g == s_ref[0])
        def _():
            out_ref[...] = a_ref[...]

        @pl.when(g != s_ref[0])
        def _():
            out_ref[...] = b_ref[...]

    def at(own):
        def index(i, g, j, s):
            mine = (g == s[0]) if own else (g != s[0])
            return (i, jnp.where(mine, j, 0), 0, 0)
        return pl.BlockSpec((1, cb, r, w), index)

    return pl.pallas_call(
        kernel,
        grid_spec=pltpu.PrefetchScalarGridSpec(
            num_scalar_prefetch=1, grid=(n, 2, nb), in_specs=[at(True), at(False)],
            out_specs=pl.BlockSpec((1, cb, r, w), lambda i, g, j, s: (i, g * nb + j, 0, 0))),
        out_shape=sds((n, 2 * c, r, w), bf16),
        compiler_params=params(),
        cost_estimate=cost(SMALL_STEP),
        name="merge",
    )(bit, cur, arrived)


def assemble(scalars, sources, chunk_rows, out_shapes, targets, name, finish=None, extra_specs=()):
    _, c, r, w = sources[0].shape
    cb = c // 2
    block = cb * chunk_rows

    def kernel(s_ref, *refs):
        ins, outs = refs[:4], refs[4:4 + len(out_shapes)]
        held, wide, in_sem, out_sem = refs[4 + len(out_shapes):]
        loads = [pltpu.make_async_copy(ins[i], held.at[i], in_sem.at[i]) for i in range(4)]
        for load in loads:
            load.start()
        for load in loads:
            load.wait()

        def chunks(part, t):
            own = s_ref[0] == part
            top, mid, low = t // 4, (t // 2) % 2, t % 2
            first = jnp.where(own, top, mid)
            second = jnp.where(own, mid, top)
            which = 2 * jnp.where(first == s_ref[1], 0, 1) + jnp.where(low == s_ref[2], 0, 1)
            return held.at[which, part, pl.ds(second * cb, cb)]

        copies = []
        for part in range(2):
            for t in range(8):
                at = part * 8 + t
                rows = chunks(part, t)
                for i in range(cb):
                    wide[at, i * chunk_rows:(i + 1) * chunk_rows, :] = rows[i, :chunk_rows, :].astype(f32)
                for source, target in targets(outs, part, t):
                    copy = pltpu.make_async_copy(wide.at[at, :, source], target, out_sem.at[len(copies)])
                    copy.start()
                    copies.append(copy)
        if finish is not None:
            finish(s_ref, chunks, wide, outs, [out_sem.at[len(copies) + i] for i in range(2)])
        for copy in copies:
            copy.wait()

    out_specs = [ANY] * (len(out_shapes) - len(extra_specs)) + list(extra_specs)
    return pl.pallas_call(
        kernel,
        out_shape=[sds(o, f32) for o in out_shapes],
        in_specs=[SMEM] + [ANY] * 4,
        out_specs=out_specs,
        scratch_shapes=[pltpu.VMEM((4, 2, c, r, w), bf16), pltpu.VMEM((16, block, w), f32),
                        pltpu.SemaphoreType.DMA((4,)), pltpu.SemaphoreType.DMA((20,))],
        compiler_params=params(),
        cost_estimate=cost(16),
        name=name,
    )(scalars, *sources)


def after(array, *earlier):
    return lax.optimization_barrier((array,) + earlier)[0]


class Order:
    def __init__(self):
        self.last = ()

    def mark(self, *arrays):
        self.last = arrays

    def also(self, *arrays):
        self.last = self.last + arrays

    def tie(self, array):
        return after(array, *self.last) if self.last else array


def pack_kernel(gain1, bias1, qbias, first_bias, vbias, obias, gain2, bias2, dbias, ubias, out_ref):
    d = out_ref.shape[1]
    half = first_bias.shape[1]
    out_ref[...] = jnp.zeros(out_ref.shape, f32)
    for row, ref in ((GAIN1, gain1), (BIAS1, bias1), (QBIAS, qbias), (OBIAS, obias), (GAIN2, gain2), (BIAS2, bias2),
                     (DBIAS, dbias)):
        out_ref[row:row + 1, :] = ref[...]
    out_ref[VBIAS:VBIAS + 1, :half] = first_bias[...]
    out_ref[VBIAS:VBIAS + 1, half:] = vbias[...]
    for i in range(ubias.shape[1] // d):
        out_ref[UBIAS + i:UBIAS + i + 1, :] = ubias[:, i * d:(i + 1) * d]


def pack_vectors(*vectors):
    return pl.pallas_call(
        pack_kernel,
        out_shape=sds((VEC_ROWS, vectors[0].shape[1]), f32),
        in_specs=[VMEM] * len(vectors),
        out_specs=VMEM,
        compiler_params=params(),
        cost_estimate=cost(2),
        name="pack_vectors",
    )(*vectors)


def local(
    boundary,
    lengths,
    norm_one_gain,
    norm_one_bias,
    query_weight,
    query_bias,
    key_weight,
    value_weight,
    value_bias,
    first_value_weight,
    first_value_bias,
    out_weight,
    out_bias,
    norm_two_gain,
    norm_two_bias,
    up_weight,
    up_bias,
    down_weight,
    down_bias,
):
    section = lax.axis_index("section")
    spot = lax.axis_index("dp")
    dp = lax.axis_size("dp")
    on_first = section == 0
    sec = jnp.reshape(section, (1,)).astype(jnp.int32)
    rows = boundary.shape[1] // 2
    d = boundary.shape[2]
    half = value_weight.shape[2]
    ff = up_weight.shape[2]

    def swap(array):
        return lax.ppermute(array, "section", SWAP)

    vec_own = pack_vectors(norm_one_gain, norm_one_bias, query_bias, first_value_bias[None], value_bias, out_bias,
                           norm_two_gain, norm_two_bias, down_bias, up_bias)
    own_rows = boundary[0]
    arrived_rows = swap(own_rows)
    vec_arrived = swap(vec_own)
    vec = (jnp.where(on_first, vec_own, vec_arrived), jnp.where(on_first, vec_arrived, vec_own))
    w = {"qo": query_weight[0], "ko": key_weight[0], "vo": value_weight[0], "oo": out_weight[0],
         "uo": up_weight[0], "do": down_weight[0], "f": first_value_weight}
    for name in "qkvo":
        w[name + "r"] = swap(w[name + "o"])
    w["ur"] = swap(after(w["uo"], w["qr"]))
    w["dr"] = swap(after(w["do"], w["kr"]))

    chunk_rows = ff // (2 * dp)
    extra = 16
    first_bits, second_bits = bit_orders(dp)
    levels = len(first_bits)
    bit = [((spot >> jnp.where(on_first, first_bits[s], second_bits[s])) & 1).astype(jnp.int32) for s in range(levels)]
    bits = [jnp.reshape(b, (1,)) for b in bit]
    scalars = jnp.stack([sec[0], bit[0], bit[2]])
    order = Order()

    h, q, k, v, o, m, e, lse, sent, x0 = attn_forward(0, sec, lengths, vec[0], own_rows, arrived_rows, w)
    kept = [dict(x=x0, h=h, q=q, k=k, v=v, o=o, m=m, e=e, lse=lse, sent_got=swap(sent))]
    u0, a0, x1, u1, a1, a_sent, h, q, k, v, o, m, e, lse, sent = middle(sec, e, m, v, lengths, vec, w)
    a_got = swap(a_sent)
    kept[0].update(u=u0, a=a0, a_got=(a_got, 0))
    kept.append(dict(x=x1, h=h, q=q, k=k, v=v, o=o, m=m, e=e, lse=lse, u=u1, a=a1, sent_got=swap(sent), a_got=(a_got, 1)))
    order.mark(x1)
    own_late = order.tie(own_rows)
    dz1 = jnp.where(on_first, arrived_rows[:rows], own_late[rows:])
    dz1_got = jnp.where(on_first, arrived_rows[rows:], own_late[:rows])
    order.mark(x1)

    def cut(level, parts):
        (first_keep, first_got), *rest = parts
        send, keep = add_split(bits[level], [(order.tie(first_keep), first_got)] + rest)
        order.mark(send)
        return keep, exchange(send, dp, level)

    def deep(part):
        for s in range(4, levels):
            part = cut(s, [part])
        return part

    def grow(level, cur, got):
        cur = merge(bits[level], order.tie(cur), got)
        order.mark(cur)
        return cur

    def first_sent(grads):
        send, keep = grads
        order.mark(send)
        return keep[None], exchange(send[None], dp, 0)

    def down_step(layer, dz, dz_got, dz_at):
        t = kept[layer]
        return first_sent(down_gradient(scalars, order.tie(t["a"]), t["a_got"], dz, dz_got, dz_at, chunk_rows))

    def back_step(layer, dz, dz_at, dr2):
        du, sent, bundle, dr2, small = layer_backward(
            layer, sec, dz, dz_at, dict(kept[layer], u=order.tie(kept[layer]["u"])), lengths, vec[layer], dr2, w)
        order.mark(bundle)
        return bundle, swap(bundle), dr2, small, du, swap(sent)

    def up_step(layer, back):
        t = kept[layer]
        return first_sent(up_gradient(scalars, order.tie(t["e"]), t["sent_got"], back[4], back[5], chunk_rows))

    def attn_grad_step(layer, attn):
        t = kept[layer]
        return first_sent(attn_gradient(scalars, order.tie(t["o"]), t["h"], t["sent_got"], attn[0], attn[1], attn[3],
                                        chunk_rows, extra))

    to_second = lambda t: lax.ppermute(t, "section", [(0, 1)])

    def summed(part, i):
        keep, got = part
        return (keep[i:i + 1].astype(f32) + got[i:i + 1].astype(f32)).astype(bf16)

    def hand_over(second, first):
        own = order.tie(jnp.where(on_first, first, second))
        sent = jnp.where(on_first, second, first)
        order.mark(sent)
        return own, swap(sent)

    def both_parts(pair):
        own, got = pair
        cur = merge(sec, order.tie(own), got)
        order.mark(cur)
        cur = jnp.swapaxes(cur, 0, 1)
        for s in range(levels - 1, 3, -1):
            cur = grow(s, cur, exchange(cur, dp, s))
        return cur, exchange(cur, dp, 3)

    back1 = back_step(1, dz1, 0, jnp.zeros((rows, half), f32))
    order.also(kept[0]["sent_got"], kept[1]["sent_got"])
    down1 = down_step(1, dz1, dz1_got, 0)
    up1 = up_step(1, back1)
    square1 = attn_grad_step(1, back1)
    down0 = down_step(0, back1[0], back1[1], 4)
    down1 = cut(1, [down1])
    back0 = back_step(0, back1[0], 4, back1[2])
    dx0, dx_moved = (t[4 * rows:5 * rows] for t in back0[:2])
    up1 = cut(1, [up1])
    square1 = cut(1, [square1])
    down0 = cut(1, [down0])
    up0 = up_step(0, back0)
    feed = cut(2, [down1, up1, down0])
    square0 = attn_grad_step(0, back0)
    square1 = cut(2, [square1])
    up0 = cut(1, [up0])
    feed = deep(cut(3, [feed]))
    square1 = deep(cut(3, [square1]))
    up0 = cut(2, [up0])
    square0 = cut(1, [square0])
    up0 = deep(cut(3, [up0]))
    square0 = cut(2, [square0])
    pair_d = hand_over(summed(feed, 0), summed(feed, 2))
    order.also(square1[1])
    square0 = deep(cut(3, [square0]))
    cur_d, got_d = both_parts(pair_d)
    pair_u = hand_over(summed(feed, 1), summed(up0, 0))
    b, e = summed(square1, 0), summed(square0, 0)

    chunk = sum(bit[s] << (levels - 1 - s) for s in range(levels))
    at_row = lax.broadcasted_iota(jnp.int32, e.shape, 2)
    at_col = lax.broadcasted_iota(jnp.int32, e.shape, 3)
    share = vector_share(d, 2 * dp)
    matrix_rows = (at_row < chunk_rows) & (at_col < half) & (chunk >= 3 * dp // 4)
    vector_row = (at_row >= chunk_rows) & (chunk * share >= VBIAS * d) & (chunk * share < VBIAS * d + half)
    b = jnp.where(matrix_rows | (vector_row & on_first), e, b)
    pair_a = hand_over(b, e)

    cur_d = grow(3, cur_d, got_d)
    got_d = exchange(cur_d, dp, 1)
    cur_u, got_u = both_parts(pair_u)
    cur_d = grow(1, cur_d, got_d)
    far_d = exchange(cur_d, dp, 2)
    side_d = exchange(cur_d, dp, 0)
    cur_a, got_a = both_parts(pair_a)
    cur_u = grow(3, cur_u, got_u)
    got_u = exchange(cur_u, dp, 1)
    cur_a = grow(3, cur_a, got_a)
    got_a = exchange(cur_a, dp, 1)
    order.also(far_d, side_d)
    last_d = exchange(order.tie(far_d), dp, 0)
    cur_u = grow(1, cur_u, got_u)
    far_u = exchange(cur_u, dp, 2)
    side_u = exchange(cur_u, dp, 0)
    cur_a = grow(1, cur_a, got_a)
    far_a = exchange(cur_a, dp, 2)
    side_a = exchange(cur_a, dp, 0)

    all_columns = slice(None)
    block = ff // 16
    order.also(far_u, side_u)
    last_u = exchange(order.tie(far_u), dp, 0)
    y = feed_down(1, sec, a1, order.tie(m), vec[1], w)
    order.mark(y)
    y_moved = to_second(y)
    down_grad, = assemble(
        scalars, (order.tie(cur_d), far_d, side_d, last_d), chunk_rows, [(ff, d)],
        lambda outs, part, t: [(all_columns, outs[0].at[pl.ds((8 * part + t) * block, block), :])], "assemble_down")
    order.mark(down_grad, far_a, side_a)
    last_a = exchange(order.tie(far_a), dp, 0)
    up_grad, = assemble(
        scalars, (order.tie(cur_u), far_u, side_u, last_u), chunk_rows, [(d, ff)],
        lambda outs, part, t: [(all_columns, outs[0].at[pl.ds(t % 4 * block, block), pl.ds((2 * part + t // 4) * d, d)])],
        "assemble_up")
    order.mark(up_grad, y_moved)

    def square_targets(outs, part, t):
        at = pl.ds((2 * part + t % 2) * block, block)
        if t // 2 < 3:
            return [(all_columns, outs[t // 2].at[at, :])]
        return [(pl.ds(half, half), outs[3].at[at, :])]

    def vectors(s_ref, chunks, wide, outs, sems):
        for part in range(2):
            @pl.when(s_ref[0] == part)
            def _():
                moves = [pltpu.make_async_copy(wide.at[8 * part + 6 + i, :, pl.ds(0, half)],
                                               outs[4].at[pl.ds(i * block, block), :], sems[i]) for i in range(2)]
                for move in moves:
                    move.start()
                for move in moves:
                    move.wait()
        lines = outs[5]
        for part in range(2):
            for t in range(8):
                rows_of = chunks(part, t)
                for i in range(dp // 8):
                    at = ((part * 8 + t) * (dp // 8) + i) * share
                    if at < VEC_ROWS * d:
                        lines[at // d:at // d + 1, at % d:at % d + share] = rows_of[i, chunk_rows:chunk_rows + 1, :share].astype(f32)
        for i, row in enumerate((GAIN1, BIAS1, QBIAS, OBIAS, GAIN2, BIAS2, DBIAS)):
            outs[6 + i][...] = lines[row:row + 1, :]
        outs[13][...] = lines[VBIAS:VBIAS + 1, half:]
        for i in range(ff // d):
            outs[14][:, i * d:(i + 1) * d] = lines[UBIAS + i:UBIAS + i + 1, :]

    (out_grad, query_grad, key_grad, value_grad, first_full, lines, gain1_grad, bias1_grad, qbias_grad, obias_grad,
     gain2_grad, bias2_grad, dbias_grad, vbias_grad, ubias_grad) = assemble(
        scalars, (order.tie(cur_a), far_a, side_a, last_a), chunk_rows,
        [(d, d)] * 3 + [(d, half), (d // 2, half)] + [(VEC_ROWS, d)] + [(1, d)] * 7 + [(1, half), (1, ff)],
        square_targets, "assemble_attn", vectors, [VMEM] * 10)

    spot_half = lambda t: jnp.where(on_first, t[:t.shape[0] // 2], t[t.shape[0] // 2:])
    block_ends = jnp.where(on_first, jnp.concatenate([dx0, dx_moved], axis=0),
                           jnp.concatenate([y_moved, y], axis=0))[None]
    return (
        block_ends,
        gain1_grad,
        bias1_grad,
        query_grad[None],
        qbias_grad,
        key_grad[None],
        value_grad[None],
        vbias_grad,
        first_full,
        spot_half(lines[VBIAS, :half]),
        out_grad[None],
        obias_grad,
        gain2_grad,
        bias2_grad,
        up_grad[None],
        ubias_grad,
        down_grad[None],
        dbias_grad,
    )


def solution(mesh):
    stacked = P("section", None, None)
    vector = P("section", None)
    return jax.shard_map(
        local,
        mesh=mesh,
        in_specs=(
            P("section", "dp", None), P("dp", None),
            vector, vector, stacked, vector, stacked, stacked, vector, P(), P(),
            stacked, vector, vector, vector, stacked, vector, stacked, vector,
        ),
        out_specs=(
            P("section", "dp", None),
            vector, vector, stacked, vector, stacked, stacked, vector, P("section"), P("section"),
            stacked, vector, vector, vector, stacked, vector, stacked, vector,
        ),
        check_vma=False,
    )
```
